256 devices in a mesh: px: 32 (over x, y, core), py: 8 (over z).
Axes of the slice: x: 4, y: 4, z: 8, core: 2. Of those that a mesh axis runs over, the one named last changes fastest.
Arguments:
- v_block: float32 [32, 32, 8, 2, 2048], P(None, 'px', 'py'), may hold values from -64 to 64
- edge_leaves: int32 [32, 8, 4, 2], replicated, may hold values from 0 to 15, as said below
- self_blocks: bfloat16 [32, 8, 2, 16, 128, 128], P('px', 'py'), may hold values from -0.375 to 0.375
- side_blocks: bfloat16 [32, 8, 4, 2, 256, 256], P('px', 'py'), may hold values from -0.25 to 0.25
- compress: bfloat16 [32, 8, 2, 2048, 256], P('px', 'py'), may hold values from -0.09375 to 0.09375
- expand: bfloat16 [32, 8, 2, 256, 2048], P('px', 'py'), may hold values from -0.25 to 0.25
- factors: bfloat16 [32, 8, 8, 2, 2, 256, 256], P('px', 'py'), may hold values from -0.1875 to 0.1875
Outputs:
- y_field: float32 [32, 32, 8, 2, 2048], P(None, 'px', 'py')
- new_basis: float32 [64, 32, 8, 2, 2048], P(None, 'px', 'py')
The draws below stay inside these ranges and needn't reach their ends.
Inputs may be any that keep to these rules, and one draw needn't show every extreme that they name: `edge_leaves`: for each patch the 8 listed leaves are distinct.
All inputs are finite; a program needn't handle non-finite values.
Results may differ from the reference program's by a relative error of at most 0.03.
Values may be sent and summed in bfloat16 or wider, within the bound.
No kernel may reach another device: no remote copies, remote signals or barrier semaphores. Data moves between devices by JAX's collectives and lax.ppermute only.
A program may use at most 64 MiB of HBM per device.

```python
import jax
import jax.numpy as jnp
from jax import lax

COLS = 32
UNK_DEV = 2048
LEAF = 128
EDGE = 2
RANK = 256
LEAVES = 16
GRID_X = 32
GRID_Y = 8
BITS_X = 5
LEVELS = 8
TOTAL_REAL = 1048576


def draw_edge_leaves(key, part):
    count = GRID_X * GRID_Y
    keys = jax.random.split(key, count)
    perms = jax.vmap(lambda k: jax.random.permutation(k, LEAVES))(keys).astype(jnp.int32)
    first = perms[:, :1]
    where = jnp.arange(count, dtype=jnp.int32)[:, None]
    target = jnp.where(where == 0, LEAVES - 1, jnp.where(where == 1, 0, first))
    moved = (perms - first + target) % LEAVES
    return moved[:, :4 * EDGE].reshape(GRID_X, GRID_Y, 4, EDGE).astype(jnp.int32)


def draw_v_block(key, part):
    shape = (COLS, GRID_X, GRID_Y, 2, UNK_DEV)
    rows = jnp.arange(GRID_X, dtype=jnp.float32)[:, None]
    cols = jnp.arange(GRID_Y, dtype=jnp.float32)[None, :]
    place = (rows * GRID_Y + cols) / (GRID_X * GRID_Y - 1.0)
    level = jnp.exp(jnp.log(8.0) * (place - 0.5))
    base = jnp.clip(jax.random.normal(key, shape, jnp.float32), -6.0, 6.0)
    return (base * level[None, :, :, None, None]).astype(jnp.float32)


def steps_of(rng, extent, shards, low, largest):
    level, own = 1.0, jax.random.fold_in(rng, 6)
    for axis_at, shards_of in shards:
        heights = jnp.exp(jax.random.uniform(jax.random.fold_in(own, axis_at), (shards_of,), jnp.float32, low / len(shards), largest / len(shards)))
        level = level * jnp.repeat(heights, extent[axis_at] // shards_of).reshape([-1 if axis == axis_at else 1 for axis in range(len(extent))])
    return level


def scatter_about(own_key, dims, scale, most, shards=(), kind=jnp.bfloat16):
    level = steps_of(own_key, dims, shards, -0.22, 0.18) if shards else 1.0
    drawn = jax.random.normal(own_key, dims, jnp.float32) * scale * level
    return jnp.minimum(jnp.maximum(drawn, -most), most).astype(kind)


def setup_inputs(seed: int = 0) -> dict:
    key_list = jax.random.split(jax.random.key(seed), 8)
    v_block = draw_v_block(jax.random.fold_in(key_list[7], 71), 0)
    edge_leaves = draw_edge_leaves(jax.random.fold_in(key_list[7], 71), 0)
    self_blocks = scatter_about(key_list[2], (GRID_X, GRID_Y, 2, LEAVES, LEAF, LEAF), (2 * LEAF) ** -0.5, 0.375, ((0, 32), (1, 8)))
    side_blocks = scatter_about(key_list[3], (GRID_X, GRID_Y, 4, 2, EDGE * LEAF, EDGE * LEAF), (2 * EDGE * LEAF) ** -0.5, 0.25, ((0, 32), (1, 8)))
    compress = scatter_about(key_list[4], (GRID_X, GRID_Y, 2, UNK_DEV, RANK), (2 * UNK_DEV) ** -0.5, 0.09375, ((0, 32), (1, 8)))
    expand = scatter_about(key_list[5], (GRID_X, GRID_Y, 2, RANK, UNK_DEV), (2 * RANK) ** -0.5, 0.25, ((0, 32), (1, 8)))
    factors = scatter_about(key_list[6], (GRID_X, GRID_Y, LEVELS, 2, 2, RANK, RANK), (4 * RANK) ** -0.5, 0.1875, ((0, 32), (1, 8)))
    return {"v_block": v_block, "edge_leaves": edge_leaves, "self_blocks": self_blocks, "side_blocks": side_blocks, "compress": compress, "expand": expand, "factors": factors}


def to_half(a):
    return lax.optimization_barrier(a.astype(jnp.bfloat16)).astype(jnp.float32)

def cprod(x, g):
    x = x.astype(jnp.float32)
    g = g.astype(jnp.float32)
    xr, xi = (x[..., 0, :], x[..., 1, :])
    gr, gi = (g[..., 0, :, :], g[..., 1, :, :])

    def mult(a, b):
        return jnp.einsum('...kn,...nm->...km', a, b)
    return jnp.stack([mult(xr, gr) - mult(xi, gi), mult(xr, gi) + mult(xi, gr)], axis=-2)

def cadj(x, g):
    x = x.astype(jnp.float32)
    g = g.astype(jnp.float32)
    xr, xi = (x[..., 0, :], x[..., 1, :])
    gr, gi = (g[..., 0, :, :], g[..., 1, :, :])

    def mult(a, b):
        return jnp.einsum('...km,...nm->...kn', a, b)
    return jnp.stack([mult(xr, gr) + mult(xi, gi), mult(xi, gr) - mult(xr, gi)], axis=-2)

def from_dir(arr, side):
    axis = side // 2
    zero = jnp.zeros_like(lax.slice_in_dim(arr, 0, 1, axis=axis))
    count = arr.shape[axis]
    if side % 2 == 0:
        return jnp.concatenate([zero, lax.slice_in_dim(arr, 0, count - 1, axis=axis)], axis=axis)
    return jnp.concatenate([lax.slice_in_dim(arr, 1, count, axis=axis), zero], axis=axis)

def partner(arr, level):
    if level < BITS_X:
        index = jnp.bitwise_xor(jnp.arange(GRID_X, dtype=jnp.int32), 1 << level)
        return jnp.take(arr, index, axis=0)
    index = jnp.bitwise_xor(jnp.arange(GRID_Y, dtype=jnp.int32), 1 << level - BITS_X)
    return jnp.take(arr, index, axis=1)

def take_edges(x4, onehot):
    picked = jnp.einsum('xysle,xykclb->xyskceb', onehot, x4, precision=lax.Precision.HIGHEST)
    return picked.reshape(GRID_X, GRID_Y, 4, COLS, 2, EDGE * LEAF)

def put_edges(terms, onehot):
    pieces = terms.reshape(GRID_X, GRID_Y, 4, COLS, 2, EDGE, LEAF)
    return jnp.einsum('xysle,xyskceb->xykclb', onehot, pieces, precision=lax.Precision.HIGHEST)

def leaf_apply(x4, blocks, adjoint):
    moved = jnp.transpose(x4, (0, 1, 4, 2, 3, 5))
    mats = jnp.transpose(blocks, (0, 1, 3, 2, 4, 5))
    out = cadj(moved, mats) if adjoint else cprod(moved, mats)
    return jnp.transpose(out, (0, 1, 3, 4, 2, 5))

def realify(a):
    rot = jnp.stack([-a[..., 1, :], a[..., 0, :]], axis=-2)
    full = jnp.concatenate([a, rot], axis=2)
    return jnp.transpose(full, (2, 0, 1, 3, 4)).reshape(2 * COLS, -1)

def reference(v_block, edge_leaves, self_blocks, side_blocks, compress, expand, factors):
    hp = lax.Precision.HIGHEST
    shape4 = (GRID_X, GRID_Y, COLS, 2, LEAVES, LEAF)
    shape3 = (GRID_X, GRID_Y, COLS, 2, UNK_DEV)
    vec = jnp.transpose(v_block, (1, 2, 0, 3, 4))
    vb = to_half(vec)
    onehot = (jnp.arange(LEAVES, dtype=jnp.int32)[None, None, None, :, None] == edge_leaves[:, :, :, None, :]).astype(jnp.float32)
    sides = side_blocks.astype(jnp.float32)
    x4 = vb.reshape(shape4)
    near = leaf_apply(x4, self_blocks, False)
    mine = take_edges(x4, onehot)
    recv = jnp.stack([from_dir(mine[:, :, s ^ 1], s) for s in range(4)], axis=2)
    near = near + put_edges(cprod(recv, sides), onehot)
    state = cprod(vb, compress)
    for level in range(LEVELS):
        sb = to_half(state)
        state = cprod(sb, factors[:, :, level, 0]) + cprod(partner(sb, level), factors[:, :, level, 1])
    y = near.reshape(shape3) + cprod(to_half(state), expand)
    yb = to_half(y)
    y4 = yb.reshape(shape4)
    znear = leaf_apply(y4, self_blocks, True)
    terms = to_half(cadj(take_edges(y4, onehot), sides))
    recv = jnp.stack([from_dir(terms[:, :, s ^ 1], s) for s in range(4)], axis=2)
    znear = znear + put_edges(recv, onehot)
    cot = cadj(yb, expand)
    for level in range(LEVELS - 1, -1, -1):
        gb = to_half(cot)
        message = to_half(cadj(gb, factors[:, :, level, 1]))
        cot = cadj(gb, factors[:, :, level, 0]) + partner(message, level)
    z = znear.reshape(shape3) + cadj(to_half(cot), compress)
    zr = realify(z)
    vr = realify(vec)
    coef = jnp.dot(zr, vr.T, precision=hp) / TOTAL_REAL
    proj = zr - jnp.dot(coef, vr, precision=hp)
    gram = jnp.dot(proj, proj.T, precision=hp) / TOTAL_REAL
    low = jnp.linalg.cholesky(gram)
    inverse = jax.scipy.linalg.solve_triangular(low, jnp.eye(2 * COLS, dtype=jnp.float32), lower=True)
    basis = jnp.dot(inverse, proj, precision=hp).reshape(2 * COLS, GRID_X, GRID_Y, 2, UNK_DEV)
    return (jnp.transpose(y, (2, 0, 1, 3, 4)), basis)
```

```python
import functools

import jax
import jax.numpy as jnp
from jax import lax
from jax.experimental import pallas as pl
from jax.experimental.pallas import tpu as pltpu
from jax.sharding import PartitionSpec as P

F32 = jnp.float32
BF16 = jnp.bfloat16
NT = (((1,), (1,)), ((), ()))
VM = pl.BlockSpec(memory_space=pltpu.VMEM)
SM = pl.BlockSpec(memory_space=pltpu.SMEM)


def call(kernel, outs, args, flops, smem=0, limit=24):
    size = sum(a.size * a.dtype.itemsize for a in args)
    return pl.pallas_call(
        kernel,
        out_shape=[jax.ShapeDtypeStruct(s, d) for s, d in outs],
        in_specs=[SM] * smem + [VM] * (len(args) - smem),
        out_specs=[VM] * len(outs),
        cost_estimate=pl.CostEstimate(flops=flops, bytes_accessed=size, transcendentals=0),
        compiler_params=pltpu.CompilerParams(vmem_limit_bytes=limit * 2**20),
    )(*args)


def mul(x, gr, gi):
    h = x.shape[0] // 2
    re, im = x[:h], x[h:]
    first = jnp.dot(x, gr, preferred_element_type=F32)
    second = jnp.dot(jnp.concatenate([-im, re], 0), gi, preferred_element_type=F32)
    return first + second


def adj(x, gr, gi):
    h = x.shape[0] // 2
    re, im = x[:h], x[h:]
    first = lax.dot_general(x, gr, NT, preferred_element_type=F32)
    second = lax.dot_general(jnp.concatenate([im, -re], 0), gi, NT, preferred_element_type=F32)
    return first + second


def leaf_at(at, leaf):
    return pl.ds(pl.multiple_of(at * leaf, leaf), leaf)


def split(x):
    high = x.astype(BF16)
    return high, (x - high.astype(F32)).astype(BF16)


def piece(ref, info, side, leaf):
    return jnp.concatenate(
        [ref[:, leaf_at(info[2 * side + e], leaf)] for e in range(2)], 1
    )


def head_kernel(leaf, info, v_ref, c_ref, vb_ref, m_ref, pb_ref, pc_ref, pd_ref):
    cols = vb_ref.shape[0] // 2
    leaves = vb_ref.shape[1] // leaf
    per = 2 * leaves
    for at in range(leaves):
        for part in range(2):
            rows = v_ref[pl.ds(2 * at + part, cols, stride=per), :]
            vb_ref[part * cols : (part + 1) * cols, at * leaf : (at + 1) * leaf] = rows.astype(BF16)
    vb = vb_ref[...]
    m_ref[: 2 * cols] = mul(vb, c_ref[0], c_ref[1]).astype(BF16)
    m_ref[2 * cols :] = piece(vb_ref, info, info[8], leaf)
    pb_ref[...] = piece(vb_ref, info, info[9], leaf)
    pc_ref[...] = piece(vb_ref, info, info[10], leaf)
    pd_ref[...] = piece(vb_ref, info, info[11], leaf)


def own_kernel(level, adjoint, s_ref, f_ref, o_ref):
    rows = o_ref.shape[0]
    product = adj if adjoint else mul
    o_ref[...] = product(s_ref[:rows], f_ref[level, 0, 0], f_ref[level, 0, 1])


def up_kernel(level, own_ref, r_ref, f_ref, *rest):
    rows = own_ref.shape[0]
    o_ref = rest[-1]
    state = own_ref[...] + mul(r_ref[:rows], f_ref[level, 1, 0], f_ref[level, 1, 1])
    o_ref[:rows] = state.astype(BF16)
    if len(rest) > 1:
        o_ref[rows:] = rest[0][...]


def leaves_kernel(leaf, adjoint, x_ref, b_ref, o_ref):
    product = adj if adjoint else mul
    for at in range(b_ref.shape[1]):
        cut = slice(at * leaf, (at + 1) * leaf)
        o_ref[:, cut] = product(x_ref[:, cut], b_ref[0, at], b_ref[1, at])


def sides_kernel(leaf, info, near_ref, ra_ref, rb_ref, rc_ref, rd_ref, b_ref, o_ref):
    rows = near_ref.shape[0]
    o_ref[...] = near_ref[...]
    for at, ref in enumerate((ra_ref, rb_ref, rc_ref, rd_ref)):
        side = info[8 + at]
        x = ref[ref.shape[0] - rows :]
        term = mul(x, b_ref[side, 0], b_ref[side, 1])
        for e in range(2):
            o_ref[:, leaf_at(info[2 * side + e], leaf)] += term[:, e * leaf : (e + 1) * leaf]


def field_kernel(leaf, level, own_ref, r_ref, f_ref, near_ref, e_ref, y_ref, yb_ref, g_ref, m_ref):
    rows = own_ref.shape[0]
    cols = rows // 2
    leaves = yb_ref.shape[1] // leaf
    state = own_ref[...] + mul(r_ref[:rows], f_ref[level, 1, 0], f_ref[level, 1, 1])
    y = near_ref[...] + mul(state.astype(BF16), e_ref[0], e_ref[1])
    yb = y.astype(BF16)
    yb_ref[...] = yb
    g = adj(yb, e_ref[0], e_ref[1]).astype(BF16)
    g_ref[...] = g
    m_ref[...] = adj(g, f_ref[level, 1, 0], f_ref[level, 1, 1]).astype(BF16)
    for at in range(leaves):
        for part in range(2):
            y_ref[pl.ds(2 * at + part, cols, stride=2 * leaves), :] = y[
                part * cols : (part + 1) * cols, at * leaf : (at + 1) * leaf
            ]


def terms_kernel(leaf, info, yb_ref, b_ref, *outs):
    for at, o_ref in enumerate(outs):
        side = info[8 + at]
        x = piece(yb_ref, info, side, leaf)
        o_ref[...] = adj(x, b_ref[side, 0], b_ref[side, 1]).astype(BF16)


def down_kernel(level, own_ref, r_ref, f_ref, *rest):
    rows = own_ref.shape[0]
    g_ref, m_ref = rest[-2:]
    g = (own_ref[...] + r_ref[:rows].astype(F32)).astype(BF16)
    g_ref[...] = g
    m_ref[:rows] = adj(g, f_ref[level, 1, 0], f_ref[level, 1, 1]).astype(BF16)
    if len(rest) > 2:
        m_ref[rows:] = rest[0][...]


def close_kernel(
    leaf, info, near_ref, own_ref, ra_ref, rb_ref, rc_ref, rd_ref, c_ref, v_ref, x_ref, p_ref
):
    rows = own_ref.shape[0]
    cols = rows // 2
    unknowns = near_ref.shape[1]
    leaves = unknowns // leaf
    g = (own_ref[...] + ra_ref[:rows].astype(F32)).astype(BF16)
    x_ref[:rows] = near_ref[...] + adj(g, c_ref[0], c_ref[1])
    for at, ref in enumerate((ra_ref, rb_ref, rc_ref, rd_ref)):
        side = info[8 + at]
        low = ref.shape[0] - rows
        for e in range(2):
            x_ref[:rows, leaf_at(info[2 * side + e], leaf)] += ref[
                low:, e * leaf : (e + 1) * leaf
            ].astype(F32)
    for at in range(leaves):
        for part in range(2):
            x_ref[rows + part * cols : rows + (part + 1) * cols, at * leaf : (at + 1) * leaf] = (
                v_ref[pl.ds(2 * at + part, cols, stride=2 * leaves), :]
            )
    high, low = split(x_ref[...])
    cross = lax.dot_general(high, low, NT, preferred_element_type=F32)
    s = lax.dot_general(high, high, NT, preferred_element_type=F32) + cross + cross.T

    def block(i, j):
        return s[i * cols : (i + 1) * cols, j * cols : (j + 1) * cols]

    below = lax.broadcasted_iota(jnp.int32, (cols, cols), 0) >= lax.broadcasted_iota(
        jnp.int32, (cols, cols), 1
    )
    zz = jnp.where(below, block(0, 0) + block(1, 1), block(1, 0) - block(0, 1))
    vv = jnp.where(below, block(2, 2) + block(3, 3), block(3, 2) - block(2, 3))
    p_ref[...] = jnp.concatenate(
        [zz, vv, block(0, 2) + block(1, 3), block(1, 2) - block(0, 3)], 1
    )


def exact_dot(a, b, dims=(((1,), (0,)), ((), ()))):
    return lax.dot_general(a, b, dims, preferred_element_type=F32, precision=lax.Precision.HIGHEST)


def real_form(re, im):
    return jnp.concatenate(
        [jnp.concatenate([re, im], 1), jnp.concatenate([-im, re], 1)], 0
    )


def inverse_factor(gram):
    size = gram.shape[0]
    eye = (
        lax.broadcasted_iota(jnp.int32, (size, size), 0)
        == lax.broadcasted_iota(jnp.int32, (size, size), 1)
    ).astype(F32)
    wide = jnp.concatenate([gram, eye], 1)
    blocks = [wide[8 * j : 8 * j + 8] for j in range(size // 8)]
    width = wide.shape[1]
    sub = lax.broadcasted_iota(jnp.int32, (8, width), 0)
    done = [jnp.zeros((8, width), F32) for _ in blocks]

    def lanes(b, k):
        return jnp.broadcast_to(b[:, k : k + 1], (8, width))

    def row(b, r):
        return jnp.broadcast_to(b[r : r + 1, :], (8, width))

    for k in range(0, size, 2):
        j0, r = divmod(k, 8)
        cols_a = [lanes(b, k) for b in blocks[j0:]]
        cols_b = [lanes(b, k + 1) for b in blocks[j0:]]
        a, b, c = row(cols_a[0], r), row(cols_b[0], r), row(cols_b[0], r + 1)
        row_a, row_b = row(blocks[j0], r), row(blocks[j0], r + 1)
        a_inv = 1.0 / a
        l = b * a_inv
        d = c - b * l
        d_inv = 1.0 / d
        row_b = row_b - l * row_a
        done[j0] = jnp.where(sub == r, row_a * lax.rsqrt(a), done[j0])
        done[j0] = jnp.where(sub == r + 1, row_b * lax.rsqrt(d), done[j0])
        scaled_a, scaled_b = row_a * a_inv, row_b * d_inv
        for i, j in enumerate(range(j0, len(blocks))):
            ca, cb = cols_a[i], cols_b[i] - l * cols_a[i]
            step = ca * scaled_a + cb * scaled_b
            if j == j0:
                step = jnp.where(sub > r + 1, step, 0.0)
            blocks[j] = blocks[j] - step
    return jnp.concatenate(done, 0)[:, size:]


def finish_kernel(leaf, total, pa_ref, pb_ref, x_ref, o_ref):
    p = (pa_ref[...] + pb_ref[...]) * (1.0 / total)
    cols = p.shape[0]
    lower = lax.broadcasted_iota(jnp.int32, (cols, cols), 0)
    upper = lax.broadcasted_iota(jnp.int32, (cols, cols), 1)
    eye = (lower == upper).astype(F32)

    def turned(a):
        return exact_dot(a, eye, (((0,), (0,)), ((), ())))

    def hermitian(t):
        strict = jnp.where(lower > upper, t, 0.0)
        above = jnp.where(lower < upper, t, 0.0)
        re = jnp.where(lower >= upper, t, 0.0) + turned(strict)
        return real_form(re, above - turned(above))

    zz = hermitian(p[:, :cols])
    vv = hermitian(p[:, cols : 2 * cols])
    h = real_form(p[:, 2 * cols : 3 * cols], p[:, 3 * cols :])
    nt = (((1,), (1,)), ((), ()))
    middle = exact_dot(h, vv) - 2.0 * h
    gram = zz + exact_dot(middle, h, nt)
    inverse = inverse_factor(gram)
    w = exact_dot(inverse, h)
    l1, l2 = inverse[:, :cols], inverse[:, cols:]
    w1, w2 = w[:, :cols], w[:, cols:]
    mix = jnp.concatenate(
        [
            jnp.concatenate([l1, -l2, -w1, w2], 1),
            jnp.concatenate([l2, l1, -w2, -w1], 1),
        ],
        0,
    )
    mix_high, mix_low = split(mix)
    high, low = split(x_ref[...])
    out = (
        jnp.dot(mix_high, high, preferred_element_type=F32)
        + jnp.dot(mix_high, low, preferred_element_type=F32)
        + jnp.dot(mix_low, high, preferred_element_type=F32)
    )
    rows = 2 * cols
    leaves = x_ref.shape[1] // leaf
    for at in range(leaves):
        for part in range(2):
            o_ref[pl.ds(2 * at + part, rows, stride=2 * leaves), :] = out[
                part * rows : (part + 1) * rows, at * leaf : (at + 1) * leaf
            ]


def per_device(v_block, edge_leaves, self_blocks, side_blocks, compress, expand, factors):
    cols = v_block.shape[0]
    unknowns = v_block.shape[4]
    leaves = self_blocks.shape[3]
    leaf = self_blocks.shape[4]
    levels = factors.shape[2]
    rank = compress.shape[4]
    rows = 2 * cols
    row_count = lax.axis_size("px")
    col_count = lax.axis_size("py")
    row_bits = row_count.bit_length() - 1
    total = 2 * unknowns * row_count * col_count
    row_at = lax.axis_index("px")
    col_at = lax.axis_index("py")
    selfs = self_blocks.reshape(self_blocks.shape[2:])
    sides = side_blocks.reshape(side_blocks.shape[2:])
    squeeze = compress.reshape(compress.shape[2:])
    spread = expand.reshape(expand.shape[2:])
    sections = factors.reshape(factors.shape[2:])
    own_leaves = lax.dynamic_slice(edge_leaves, (row_at, col_at, 0, 0), (1, 1, 4, 2)).reshape(8)
    odd_row, odd_col = row_at % 2, col_at % 2
    order = jnp.stack([1 - odd_row, odd_row, 3 - odd_col, 2 + odd_col]).astype(jnp.int32)
    info = jnp.concatenate([own_leaves, order])
    tall = v_block.reshape(cols, 2, leaves, leaf).transpose(0, 2, 1, 3).reshape(-1, leaf)

    def partner(x, level):
        if level < row_bits:
            return lax.ppermute(x, "px", [(i, i ^ 1 << level) for i in range(row_count)])
        bit = level - row_bits
        return lax.ppermute(x, "py", [(i, i ^ 1 << bit) for i in range(col_count)])

    def beyond(x, axis, count):
        pairs = [(i, i + 1) for i in range(1, count - 1, 2)]
        return lax.ppermute(x, axis, pairs + [(j, i) for i, j in pairs])

    small = ((rows, rank), BF16)
    double = ((2 * rows, rank), BF16)
    wide = ((rows, rank), F32)
    step_flops = 8 * cols * rank * rank
    patch_flops = 8 * cols * rank * unknowns
    leaf_flops = 8 * cols * leaf * unknowns

    half, sent, piece_b, piece_c, piece_d = call(
        functools.partial(head_kernel, leaf),
        [((rows, unknowns), BF16), double, small, small, small],
        [info, tall, squeeze],
        patch_flops,
        smem=1,
    )
    (near,) = call(
        functools.partial(leaves_kernel, leaf, False),
        [((rows, unknowns), F32)],
        [half, selfs],
        leaf_flops,
    )
    got = {}
    for level in range(levels):
        arrived = partner(sent, level)
        (own,) = call(
            functools.partial(own_kernel, level, False), [wide], [sent, sections], step_flops
        )
        if level == 0:
            got["a"] = arrived
        if level == 1:
            got["b"] = beyond(piece_b, "px", row_count)
        if level == 2:
            got["d"] = beyond(piece_d, "py", col_count)
        if level == row_bits:
            got["c"] = arrived
            (near,) = call(
                functools.partial(sides_kernel, leaf),
                [((rows, unknowns), F32)],
                [info, near, got["a"], got["b"], got["c"], got["d"], sides],
                4 * step_flops,
                smem=1,
            )
        if level < levels - 1:
            extra = [piece_c] if level == row_bits - 1 else []
            (sent,) = call(
                functools.partial(up_kernel, level),
                [double if extra else small],
                [own, arrived, sections] + extra,
                step_flops,
            )
    y, yb, g, message = call(
        functools.partial(field_kernel, leaf, levels - 1),
        [((rows * leaves, leaf), F32), ((rows, unknowns), BF16), small, small],
        [own, arrived, sections, near, spread],
        2 * patch_flops,
    )
    terms = call(
        functools.partial(terms_kernel, leaf), [small] * 4, [info, yb, sides], 4 * step_flops, smem=1
    )
    (z_near,) = call(
        functools.partial(leaves_kernel, leaf, True),
        [((rows, unknowns), F32)],
        [yb, selfs],
        leaf_flops,
    )
    for level in range(levels - 1, -1, -1):
        arrived = partner(message, level)
        (own,) = call(functools.partial(own_kernel, level, True), [wide], [g, sections], step_flops)
        if level == levels - 1:
            got["b"] = beyond(terms[1], "px", row_count)
        if level == levels - 2:
            got["d"] = beyond(terms[3], "py", col_count)
        if level == row_bits:
            got["c"] = arrived
        if level > 0:
            extra = [terms[0]] if level == 1 else [terms[2]] if level == row_bits + 1 else []
            g, message = call(
                functools.partial(down_kernel, level - 1),
                [small, double if extra else small],
                [own, arrived, sections] + extra,
                step_flops,
            )
    stacked, part = call(
        functools.partial(close_kernel, leaf),
        [((2 * rows, unknowns), F32), ((cols, 4 * cols), F32)],
        [info, z_near, own, arrived, got["b"], got["c"], got["d"], squeeze, tall],
        patch_flops,
        smem=1,
    )
    for level in range(levels):
        other = partner(part, level)
        if level < levels - 1:
            part = part + other
    (basis,) = call(
        functools.partial(finish_kernel, leaf, total),
        [((2 * rows * leaves, leaf), F32)],
        [part, other, stacked],
        8 * rows * rows * unknowns,
    )

    def patch_form(a, count):
        a = a.reshape(count, leaves, 2, leaf).transpose(0, 2, 1, 3)
        return a.reshape(count, 1, 1, 2, unknowns)

    return patch_form(y, cols), patch_form(basis, rows)


def solution(mesh):
    in_specs = (
        P(None, "px", "py", None, None),
        P(),
        P("px", "py", None, None, None, None),
        P("px", "py", None, None, None, None),
        P("px", "py", None, None, None),
        P("px", "py", None, None, None),
        P("px", "py", None, None, None, None, None),
    )
    out_specs = (P(None, "px", "py", None, None), P(None, "px", "py", None, None))
    return jax.shard_map(
        per_device, mesh=mesh, in_specs=in_specs, out_specs=out_specs, check_vma=False
    )
```

```python
import functools

import jax
import jax.numpy as jnp
from jax import lax
from jax.experimental import pallas as pl
from jax.experimental.pallas import tpu as pltpu
from jax.sharding import PartitionSpec as P

F32 = jnp.float32
BF16 = jnp.bfloat16
NT = (((1,), (1,)), ((), ()))
VM = pl.BlockSpec(memory_space=pltpu.VMEM)
SM = pl.BlockSpec(memory_space=pltpu.SMEM)

HEAD, LOAD = 214, 196


def call(kernel, outs, args, flops, smem=0, limit=24, after=(), out_spec=VM, scratch=()):
    size = sum(a.size * a.dtype.itemsize for a in args)
    args = list(args) + list(after)
    count, extra = len(args), len(after)

    def body(*refs):
        kernel(*refs[: count - extra], *refs[count:])

    return pl.pallas_call(
        body,
        out_shape=[jax.ShapeDtypeStruct(s, d) for s, d in outs],
        in_specs=[SM] * smem + [VM] * (count - smem),
        out_specs=[out_spec] * len(outs),
        scratch_shapes=list(scratch),
        cost_estimate=pl.CostEstimate(flops=flops, bytes_accessed=size, transcendentals=0),
        compiler_params=pltpu.CompilerParams(vmem_limit_bytes=limit * 2**20),
    )(*args)


def mul(x, gr, gi):
    h = x.shape[0] // 2
    re, im = x[:h], x[h:]
    first = jnp.dot(x, gr, preferred_element_type=F32)
    second = jnp.dot(jnp.concatenate([-im, re], 0), gi, preferred_element_type=F32)
    return first + second


def adj(x, gr, gi):
    h = x.shape[0] // 2
    re, im = x[:h], x[h:]
    first = lax.dot_general(x, gr, NT, preferred_element_type=F32)
    second = lax.dot_general(jnp.concatenate([im, -re], 0), gi, NT, preferred_element_type=F32)
    return first + second


def leaf_at(at, leaf):
    return pl.ds(pl.multiple_of(at * leaf, leaf), leaf)


def split(x):
    high = x.astype(BF16)
    return high, (x - high.astype(F32)).astype(BF16)


def piece(ref, info, side, leaf):
    return jnp.concatenate(
        [ref[:, leaf_at(info[2 * side + e], leaf)] for e in range(2)], 1
    )


def head_kernel(leaf, v_in, c_in, vb_ref, m_ref, v_ref, c_ref, v_sems, c_sems):
    cols, lines, _ = v_ref.shape
    count = v_sems.shape[0]
    step = lines // count
    width = step // 2 * leaf
    copies = []
    for at in range(count):
        some = slice(at * step, (at + 1) * step)
        cut = slice(at * width, (at + 1) * width)
        pair = [
            pltpu.make_async_copy(v_in.at[:, some], v_ref.at[:, some], v_sems.at[at]),
            pltpu.make_async_copy(c_in.at[:, cut], c_ref.at[:, cut], c_sems.at[at]),
        ]
        for copy in pair:
            copy.start()
        copies.append(pair)
    total = None
    for at in range(count):
        copies[at][0].wait()
        for row in range(at * step, (at + 1) * step):
            of, part = divmod(row, 2)
            vb_ref[part * cols : (part + 1) * cols, of * leaf : (of + 1) * leaf] = v_ref[
                :, row
            ].astype(BF16)
        copies[at][1].wait()
        cut = slice(at * width, (at + 1) * width)
        product = mul(vb_ref[:, cut], c_ref[0, cut], c_ref[1, cut])
        total = product if total is None else total + product
    m_ref[...] = total.astype(BF16)


def head(leaf, tall, squeeze):
    cols = tall.shape[0]
    unknowns, rank = squeeze.shape[1:]
    count = 4
    return pl.pallas_call(
        functools.partial(head_kernel, leaf),
        in_specs=[pl.BlockSpec(memory_space=pltpu.HBM)] * 2,
        out_specs=[VM] * 2,
        out_shape=[
            jax.ShapeDtypeStruct((2 * cols, unknowns), BF16),
            jax.ShapeDtypeStruct((2 * cols, rank), BF16),
        ],
        scratch_shapes=[
            pltpu.VMEM(tall.shape, F32),
            pltpu.VMEM(squeeze.shape, BF16),
            pltpu.SemaphoreType.DMA((count,)),
            pltpu.SemaphoreType.DMA((count,)),
        ],
        cost_estimate=pl.CostEstimate(
            flops=8 * cols * rank * unknowns,
            bytes_accessed=tall.size * 4 + squeeze.size * 2,
            transcendentals=0,
        ),
        compiler_params=pltpu.CompilerParams(vmem_limit_bytes=HEAD * 2**18),
    )(tall, squeeze)


def load_kernel(f_in, o_ref, sem):
    copy = pltpu.make_async_copy(f_in, o_ref, sem)
    copy.start()
    copy.wait()


def load(sections):
    return pl.pallas_call(
        load_kernel,
        in_specs=[pl.BlockSpec(memory_space=pltpu.HBM)],
        out_specs=VM,
        out_shape=jax.ShapeDtypeStruct(sections.shape, BF16),
        scratch_shapes=[pltpu.SemaphoreType.DMA],
        cost_estimate=pl.CostEstimate(
            flops=0, bytes_accessed=2 * sections.size, transcendentals=0
        ),
        compiler_params=pltpu.CompilerParams(vmem_limit_bytes=LOAD * 2**18),
    )(sections)


def pick_kernel(leaf, info, vb_ref, *outs):
    for at, o_ref in enumerate(outs):
        o_ref[...] = piece(vb_ref, info, info[8 + at], leaf)


def basis_kernel(leaf, v_ref, high_ref, low_ref, p_ref):
    cols = v_ref.shape[0]
    for row in range(v_ref.shape[1]):
        of, part = divmod(row, 2)
        place = (slice(part * cols, (part + 1) * cols), slice(of * leaf, (of + 1) * leaf))
        high, low = split(v_ref[:, row])
        high_ref[place] = high
        low_ref[place] = low
    high = high_ref[...]
    cross = lax.dot_general(high, low_ref[...], NT, preferred_element_type=F32)
    s = lax.dot_general(high, high, NT, preferred_element_type=F32) + cross + cross.T
    p_ref[...] = packed(s, cols)


def packed(s, cols):
    below = lax.broadcasted_iota(jnp.int32, (cols, cols), 0) >= lax.broadcasted_iota(
        jnp.int32, (cols, cols), 1
    )
    re = s[:cols, :cols] + s[cols:, cols:]
    return jnp.where(below, re, s[cols:, :cols] - s[:cols, cols:])


def own_kernel(level, adjoint, s_ref, f_ref, o_ref):
    rows = o_ref.shape[0]
    product = adj if adjoint else mul
    o_ref[...] = product(s_ref[:rows], f_ref[level, 0, 0], f_ref[level, 0, 1])


def up_kernel(level, own_ref, r_ref, f_ref, *rest):
    rows = own_ref.shape[0]
    o_ref = rest[-1]
    state = own_ref[...] + mul(r_ref[:rows], f_ref[level, 1, 0], f_ref[level, 1, 1])
    o_ref[:rows] = state.astype(BF16)
    if len(rest) > 1:
        o_ref[rows:] = rest[0][...]


def leaves_kernel(leaf, adjoint, x_ref, b_ref, o_ref):
    product = adj if adjoint else mul
    for at in range(b_ref.shape[1]):
        cut = slice(at * leaf, (at + 1) * leaf)
        o_ref[:, cut] = product(x_ref[:, cut], b_ref[0, at], b_ref[1, at])


def sides_kernel(leaf, info, near_ref, ra_ref, rb_ref, rc_ref, rd_ref, b_ref, o_ref):
    rows = near_ref.shape[0]
    o_ref[...] = near_ref[...]
    for at, ref in enumerate((ra_ref, rb_ref, rc_ref, rd_ref)):
        side = info[8 + at]
        x = ref[ref.shape[0] - rows :]
        term = mul(x, b_ref[side, 0], b_ref[side, 1])
        for e in range(2):
            o_ref[:, leaf_at(info[2 * side + e], leaf)] += term[:, e * leaf : (e + 1) * leaf]


def field_kernel(level, own_ref, r_ref, f_ref, near_ref, e_ref, y_ref, yb_ref, g_ref, m_ref):
    rows = own_ref.shape[0]
    state = own_ref[...] + mul(r_ref[:rows], f_ref[level, 1, 0], f_ref[level, 1, 1])
    y = near_ref[...] + mul(state.astype(BF16), e_ref[0], e_ref[1])
    y_ref[...] = y
    yb = y.astype(BF16)
    yb_ref[...] = yb
    g = adj(yb, e_ref[0], e_ref[1]).astype(BF16)
    g_ref[...] = g
    m_ref[...] = adj(g, f_ref[level, 1, 0], f_ref[level, 1, 1]).astype(BF16)


def shape_kernel(leaf, y_ref, o_ref):
    cols = o_ref.shape[0]
    for row in range(o_ref.shape[1]):
        of, part = divmod(row, 2)
        o_ref[:, row] = y_ref[part * cols : (part + 1) * cols, of * leaf : (of + 1) * leaf]


def terms_kernel(leaf, info, yb_ref, b_ref, *outs):
    for at, o_ref in enumerate(outs):
        side = info[8 + at]
        x = piece(yb_ref, info, side, leaf)
        o_ref[...] = adj(x, b_ref[side, 0], b_ref[side, 1]).astype(BF16)


def down_kernel(level, own_ref, r_ref, f_ref, *rest):
    rows = own_ref.shape[0]
    g_ref, m_ref = rest[-2:]
    g = (own_ref[...] + r_ref[:rows].astype(F32)).astype(BF16)
    g_ref[...] = g
    m_ref[:rows] = adj(g, f_ref[level, 1, 0], f_ref[level, 1, 1]).astype(BF16)
    if len(rest) > 2:
        m_ref[rows:] = rest[0][...]


def close_kernel(
    leaf, info, near_ref, own_ref, ra_ref, rb_ref, rc_ref, rd_ref, c_ref, vh_ref, vl_ref, vv_ref,
    zh_ref, zl_ref, p_ref, z_ref
):
    rows = own_ref.shape[0]
    cols = rows // 2
    g = (own_ref[...] + ra_ref[:rows].astype(F32)).astype(BF16)
    z_ref[...] = near_ref[...] + adj(g, c_ref[0], c_ref[1])
    for at, ref in enumerate((ra_ref, rb_ref, rc_ref, rd_ref)):
        side = info[8 + at]
        low = ref.shape[0] - rows
        for e in range(2):
            z_ref[:, leaf_at(info[2 * side + e], leaf)] += ref[
                low:, e * leaf : (e + 1) * leaf
            ].astype(F32)
    high, low = split(z_ref[...])
    zh_ref[...] = high
    zl_ref[...] = low
    many = jnp.concatenate([high, low, vh_ref[...], vl_ref[...]], 0)
    s = lax.dot_general(high, many, NT, preferred_element_type=F32)
    cross = s[:, rows : 2 * rows]
    zz = s[:, :rows] + cross + cross.T
    zv = s[:, 2 * rows : 3 * rows] + s[:, 3 * rows :]
    zv += lax.dot_general(low, vh_ref[...], NT, preferred_element_type=F32)
    p_ref[...] = jnp.concatenate(
        [
            packed(zz, cols),
            vv_ref[...],
            zv[:cols, :cols] + zv[cols:, cols:],
            zv[cols:, :cols] - zv[:cols, cols:],
        ],
        1,
    )


def spread_kernel(*refs):
    o_ref = refs[-1]
    total = sum(parts_of(refs[:-1]))
    for at in range(o_ref.shape[0]):
        o_ref[at] = total


def parts_of(refs):
    return [ref[at] for ref in refs for at in range(ref.shape[0])]


def exact_dot(a, b, dims=(((1,), (0,)), ((), ()))):
    return lax.dot_general(a, b, dims, preferred_element_type=F32, precision=lax.Precision.HIGHEST)


def real_form(re, im):
    return jnp.concatenate(
        [jnp.concatenate([re, im], 1), jnp.concatenate([-im, re], 1)], 0
    )


def inverse_factor(gram):
    size, step = gram.shape[0], 8
    eye = (
        lax.broadcasted_iota(jnp.int32, (size, size), 0)
        == lax.broadcasted_iota(jnp.int32, (size, size), 1)
    ).astype(F32)
    wide = jnp.concatenate([gram, eye], 1)
    width = wide.shape[1]
    blocks = [wide[step * j : step * (j + 1)] for j in range(size // step)]
    sub = lax.broadcasted_iota(jnp.int32, (step, width), 0)
    done = []
    for at in range(size // step):
        left = [
            [jnp.broadcast_to(b[:, at * step + p : at * step + p + 1], (step, width)) for b in blocks[at:]]
            for p in range(step)
        ]
        pivot = [
            [jnp.broadcast_to(left[q][0][p : p + 1], (step, width)) for q in range(p + 1)]
            for p in range(step)
        ]
        lines = [jnp.broadcast_to(blocks[at][p : p + 1], (step, width)) for p in range(step)]
        result = jnp.zeros((step, width), F32)
        updates = [None] * len(left[0])
        for p in range(step):
            inverse = 1.0 / pivot[p][p]
            result = jnp.where(sub == p, lines[p] * lax.rsqrt(pivot[p][p]), result)
            scaled = lines[p] * inverse
            for q in range(p + 1, step):
                ratio = pivot[q][p] * inverse
                lines[q] = lines[q] - ratio * lines[p]
                for r in range(p + 1, q + 1):
                    pivot[q][r] = pivot[q][r] - ratio * pivot[r][p]
                for i in range(1, len(left[q])):
                    left[q][i] = left[q][i] - ratio * left[p][i]
            for i in range(1, len(updates)):
                term = left[p][i] * scaled
                updates[i] = term if p == 0 else updates[i] + term
        done.append(result)
        for i in range(1, len(updates)):
            blocks[at + i] = blocks[at + i] - updates[i]
    return jnp.concatenate(done, 0)[:, size:]


def finish_kernel(leaf, total, p_ref, zh_ref, zl_ref, vh_ref, vl_ref, o_ref, buffer, sems):
    p = sum(parts_of([p_ref])) * (1.0 / total)
    cols = p.shape[0]
    lower = lax.broadcasted_iota(jnp.int32, (cols, cols), 0)
    upper = lax.broadcasted_iota(jnp.int32, (cols, cols), 1)
    eye = (lower == upper).astype(F32)

    def turned(a):
        return exact_dot(a, eye, (((0,), (0,)), ((), ())))

    def hermitian(t):
        strict = jnp.where(lower > upper, t, 0.0)
        above = jnp.where(lower < upper, t, 0.0)
        re = jnp.where(lower >= upper, t, 0.0) + turned(strict)
        return real_form(re, above - turned(above))

    zz = hermitian(p[:, :cols])
    vv = hermitian(p[:, cols : 2 * cols])
    h = real_form(p[:, 2 * cols : 3 * cols], p[:, 3 * cols :])
    nt = (((1,), (1,)), ((), ()))
    middle = exact_dot(h, vv) - 2.0 * h
    gram = zz + exact_dot(middle, h, nt)
    inverse = inverse_factor(gram)
    w = exact_dot(inverse, h)
    l1, l2 = inverse[:, :cols], inverse[:, cols:]
    w1, w2 = w[:, :cols], w[:, cols:]
    mix = jnp.concatenate(
        [
            jnp.concatenate([l1, -l2, -w1, w2], 1),
            jnp.concatenate([l2, l1, -w2, -w1], 1),
        ],
        0,
    )
    mix_high, mix_low = split(mix)
    mix = jnp.concatenate([mix_high, mix_high, mix_low], 1)
    rows = 2 * cols
    count, _, lines, _ = buffer.shape
    width = lines // 2 * leaf
    copies = []
    for at in range(count):
        cut = slice(at * width, (at + 1) * width)
        high = [zh_ref[:, cut], vh_ref[:, cut]]
        x = jnp.concatenate(high + [zl_ref[:, cut], vl_ref[:, cut]] + high, 0)
        out = jnp.dot(mix, x, preferred_element_type=F32)
        for line in range(lines):
            of, part = divmod(line, 2)
            buffer[at, :, line] = out[part * rows : (part + 1) * rows, of * leaf : (of + 1) * leaf]
        copy = pltpu.make_async_copy(
            buffer.at[at], o_ref.at[:, at * lines : (at + 1) * lines], sems.at[at]
        )
        copy.start()
        copies.append(copy)
    for copy in copies:
        copy.wait()


def per_device(v_block, edge_leaves, self_blocks, side_blocks, compress, expand, factors):
    cols = v_block.shape[0]
    unknowns = v_block.shape[4]
    leaves = self_blocks.shape[3]
    leaf = self_blocks.shape[4]
    levels = factors.shape[2]
    rank = compress.shape[4]
    rows = 2 * cols
    row_count = lax.axis_size("px")
    col_count = lax.axis_size("py")
    row_bits = row_count.bit_length() - 1
    total = 2 * unknowns * row_count * col_count
    row_at = lax.axis_index("px")
    col_at = lax.axis_index("py")
    selfs = self_blocks.reshape(self_blocks.shape[2:])
    sides = side_blocks.reshape(side_blocks.shape[2:])
    squeeze = compress.reshape(compress.shape[2:])
    spread = expand.reshape(expand.shape[2:])
    sections = factors.reshape(factors.shape[2:])
    own_leaves = lax.dynamic_slice(edge_leaves, (row_at, col_at, 0, 0), (1, 1, 4, 2)).reshape(8)
    odd_row, odd_col = row_at % 2, col_at % 2
    order = jnp.stack([1 - odd_row, odd_row, 3 - odd_col, 2 + odd_col]).astype(jnp.int32)
    info = jnp.concatenate([own_leaves, order])
    tall = v_block.reshape(cols, 2, leaves, leaf).transpose(0, 2, 1, 3).reshape(cols, -1, leaf)

    def partner(x, level):
        if level < row_bits:
            return lax.ppermute(x, "px", [(i, i ^ 1 << level) for i in range(row_count)])
        bit = level - row_bits
        return lax.ppermute(x, "py", [(i, i ^ 1 << bit) for i in range(col_count)])

    def beyond(x, axis, count):
        pairs = [(i, i + 1) for i in range(1, count - 1, 2)]
        return lax.ppermute(x, axis, pairs + [(j, i) for i, j in pairs])

    small = ((rows, rank), BF16)
    double = ((2 * rows, rank), BF16)
    wide = ((rows, rank), F32)
    step_flops = 8 * cols * rank * rank
    patch_flops = 8 * cols * rank * unknowns
    leaf_flops = 8 * cols * leaf * unknowns

    half, sent = head(leaf, tall, squeeze)
    pieces = call(functools.partial(pick_kernel, leaf), [small] * 4, [info, half], 0, smem=1)
    got = {}
    for level in range(levels):
        arrived = partner(sent, level)
        after = []
        if level == 0:
            sections = load(sections)
        if level == 2:
            got["a"] = partner(pieces[0], 0)
            got["b"] = beyond(pieces[1], "px", row_count)
        if level == 3:
            got["d"] = beyond(pieces[3], "py", col_count)
            after = [got["a"], got["b"]]
        if level == 4:
            (near,) = call(
                functools.partial(leaves_kernel, leaf, False),
                [((rows, unknowns), F32)],
                [half, selfs],
                leaf_flops,
            )
            after = [got["d"], near]
        if level == row_bits:
            got["c"] = arrived
        if level == row_bits + 1:
            (near,) = call(
                functools.partial(sides_kernel, leaf),
                [((rows, unknowns), F32)],
                [info, near, got["a"], got["b"], got["c"], got["d"], sides],
                4 * step_flops,
                smem=1,
            )
            after = [near, spread]
        (own,) = call(
            functools.partial(own_kernel, level, False),
            [wide],
            [sent, sections],
            step_flops,
            after=after,
        )
        if level < levels - 1:
            extra = [pieces[2]] if level == row_bits - 1 else []
            (sent,) = call(
                functools.partial(up_kernel, level),
                [double if extra else small],
                [own, arrived, sections] + extra,
                step_flops,
            )
    y, yb, g, message = call(
        functools.partial(field_kernel, levels - 1),
        [((rows, unknowns), F32), ((rows, unknowns), BF16), small, small],
        [own, arrived, sections, near, spread],
        2 * patch_flops,
    )
    terms = call(
        functools.partial(terms_kernel, leaf), [small] * 4, [info, yb, sides], 4 * step_flops, smem=1
    )
    for level in range(levels - 1, -1, -1):
        arrived = partner(message, level)
        after = []
        if level == levels - 1:
            (shaped,) = call(
                functools.partial(shape_kernel, leaf), [((cols, 2 * leaves, leaf), F32)], [y], 0
            )
            after = list(terms)
        if level == levels - 2:
            (z_near,) = call(
                functools.partial(leaves_kernel, leaf, True),
                [((rows, unknowns), F32)],
                [yb, selfs],
                leaf_flops,
            )
            got["b"] = beyond(terms[1], "px", row_count)
            after = [z_near]
        if level == row_bits:
            got["c"] = arrived
            got["d"] = beyond(terms[3], "py", col_count)
            after = [got["b"]]
        if level == row_bits - 1:
            after = [got["d"]]
        if level == 3:
            v_high, v_low, vv = call(
                functools.partial(basis_kernel, leaf),
                [((rows, unknowns), BF16), ((rows, unknowns), BF16), ((cols, cols), F32)],
                [tall],
                leaf_flops,
            )
            after = [v_high, v_low, vv]
        if level == 1:
            after = [squeeze]
        (own,) = call(
            functools.partial(own_kernel, level, True),
            [wide],
            [g, sections],
            step_flops,
            after=after,
        )
        if level > 0:
            extra = [terms[0]] if level == 1 else [terms[2]] if level == row_bits + 1 else []
            g, message = call(
                functools.partial(down_kernel, level - 1),
                [small, double if extra else small],
                [own, arrived, sections] + extra,
                step_flops,
            )
    z_high, z_low, part = call(
        functools.partial(close_kernel, leaf),
        [((rows, unknowns), BF16), ((rows, unknowns), BF16), ((cols, 4 * cols), F32)],
        [info, z_near, own, arrived, got["b"], got["c"], got["d"], squeeze, v_high, v_low, vv],
        patch_flops,
        smem=1,
        scratch=[pltpu.VMEM((rows, unknowns), F32)],
    )
    part = part.reshape(1, cols, 4 * cols)
    chips = row_count // 2
    (part,) = call(
        spread_kernel, [((chips, cols, 4 * cols), F32)], [part, partner(part, 0)], 0
    )
    groups = [[2 * i + core for i in range(chips)] for core in range(2)]
    part = lax.all_to_all(part, "px", 0, 0, axis_index_groups=groups, tiled=True)
    (part,) = call(spread_kernel, [((col_count, cols, 4 * cols), F32)], [part], 0)
    part = lax.all_to_all(part, "py", 0, 0, tiled=True)
    lines = 8
    (basis,) = call(
        functools.partial(finish_kernel, leaf, total),
        [((rows, 2 * leaves, leaf), F32)],
        [part, z_high, z_low, v_high, v_low],
        8 * rows * rows * unknowns,
        out_spec=pl.BlockSpec(memory_space=pl.ANY),
        scratch=[
            pltpu.VMEM((2 * leaves // lines, rows, lines, leaf), F32),
            pltpu.SemaphoreType.DMA((2 * leaves // lines,)),
        ],
    )

    def patch_form(a):
        count = a.shape[0]
        a = a.reshape(count, leaves, 2, leaf).transpose(0, 2, 1, 3)
        return a.reshape(count, 1, 1, 2, unknowns)

    return patch_form(shaped), patch_form(basis)


def solution(mesh):
    in_specs = (
        P(None, "px", "py", None, None),
        P(),
        P("px", "py", None, None, None, None),
        P("px", "py", None, None, None, None),
        P("px", "py", None, None, None),
        P("px", "py", None, None, None),
        P("px", "py", None, None, None, None, None),
    )
    out_specs = (P(None, "px", "py", None, None), P(None, "px", "py", None, None))
    return jax.shard_map(
        per_device, mesh=mesh, in_specs=in_specs, out_specs=out_specs, check_vma=False
    )
```

```python
import functools

import jax
import jax.numpy as jnp
from jax import lax
from jax.experimental import pallas as pl
from jax.experimental.pallas import tpu as pltpu
from jax.sharding import PartitionSpec as P

F32 = jnp.float32
BF16 = jnp.bfloat16
NT = (((1,), (1,)), ((), ()))
VM = pl.BlockSpec(memory_space=pltpu.VMEM)
SM = pl.BlockSpec(memory_space=pltpu.SMEM)

HEAD, EARLY, LATE = 214, 203, 200


def call(kernel, outs, args, flops, smem=0, limit=24, after=(), out_spec=VM, scratch=()):
    size = sum(a.size * a.dtype.itemsize for a in args)
    args = list(args) + list(after)
    count, extra = len(args), len(after)

    def body(*refs):
        kernel(*refs[: count - extra], *refs[count:])

    return pl.pallas_call(
        body,
        out_shape=[jax.ShapeDtypeStruct(s, d) for s, d in outs],
        in_specs=[SM] * smem + [VM] * (count - smem),
        out_specs=[out_spec] * len(outs),
        scratch_shapes=list(scratch),
        cost_estimate=pl.CostEstimate(flops=flops, bytes_accessed=size, transcendentals=0),
        compiler_params=pltpu.CompilerParams(vmem_limit_bytes=limit * 2**20),
    )(*args)


def mul(x, gr, gi):
    h = x.shape[0] // 2
    re, im = x[:h], x[h:]
    first = jnp.dot(x, gr, preferred_element_type=F32)
    second = jnp.dot(jnp.concatenate([-im, re], 0), gi, preferred_element_type=F32)
    return first + second


def adj(x, gr, gi):
    h = x.shape[0] // 2
    re, im = x[:h], x[h:]
    first = lax.dot_general(x, gr, NT, preferred_element_type=F32)
    second = lax.dot_general(jnp.concatenate([im, -re], 0), gi, NT, preferred_element_type=F32)
    return first + second


def leaf_at(at, leaf):
    return pl.ds(pl.multiple_of(at * leaf, leaf), leaf)


def split(x):
    high = x.astype(BF16)
    return high, (x - high.astype(F32)).astype(BF16)


def piece(ref, info, side, leaf):
    return jnp.concatenate(
        [ref[:, leaf_at(info[2 * side + e], leaf)] for e in range(2)], 1
    )


def head_kernel(leaf, v_in, c_in, vb_ref, m_ref, v_ref, c_ref, v_sems, c_sems):
    cols, lines, _ = v_ref.shape
    count = v_sems.shape[0]
    step = lines // count
    width = step // 2 * leaf
    copies = []
    for at in range(count):
        some = slice(at * step, (at + 1) * step)
        cut = slice(at * width, (at + 1) * width)
        pair = [
            pltpu.make_async_copy(v_in.at[:, some], v_ref.at[:, some], v_sems.at[at]),
            pltpu.make_async_copy(c_in.at[:, cut], c_ref.at[:, cut], c_sems.at[at]),
        ]
        for copy in pair:
            copy.start()
        copies.append(pair)
    total = None
    for at in range(count):
        copies[at][0].wait()
        for row in range(at * step, (at + 1) * step):
            of, part = divmod(row, 2)
            vb_ref[part * cols : (part + 1) * cols, of * leaf : (of + 1) * leaf] = v_ref[
                :, row
            ].astype(BF16)
        copies[at][1].wait()
        cut = slice(at * width, (at + 1) * width)
        product = mul(vb_ref[:, cut], c_ref[0, cut], c_ref[1, cut])
        total = product if total is None else total + product
    m_ref[...] = total.astype(BF16)


def head(leaf, tall, squeeze):
    cols = tall.shape[0]
    unknowns, rank = squeeze.shape[1:]
    count = 4
    return pl.pallas_call(
        functools.partial(head_kernel, leaf),
        in_specs=[pl.BlockSpec(memory_space=pltpu.HBM)] * 2,
        out_specs=[VM] * 2,
        out_shape=[
            jax.ShapeDtypeStruct((2 * cols, unknowns), BF16),
            jax.ShapeDtypeStruct((2 * cols, rank), BF16),
        ],
        scratch_shapes=[
            pltpu.VMEM(tall.shape, F32),
            pltpu.VMEM(squeeze.shape, BF16),
            pltpu.SemaphoreType.DMA((count,)),
            pltpu.SemaphoreType.DMA((count,)),
        ],
        cost_estimate=pl.CostEstimate(
            flops=8 * cols * rank * unknowns,
            bytes_accessed=tall.size * 4 + squeeze.size * 2,
            transcendentals=0,
        ),
        compiler_params=pltpu.CompilerParams(vmem_limit_bytes=HEAD * 2**18),
    )(tall, squeeze)


def load_kernel(begin, f_in, o_ref, sem):
    copy = pltpu.make_async_copy(f_in.at[begin : begin + o_ref.shape[0]], o_ref, sem)
    copy.start()
    copy.wait()


def load(sections, begin, end, limit):
    shape = (end - begin,) + sections.shape[1:]
    return pl.pallas_call(
        functools.partial(load_kernel, begin),
        in_specs=[pl.BlockSpec(memory_space=pltpu.HBM)],
        out_specs=VM,
        out_shape=jax.ShapeDtypeStruct(shape, BF16),
        scratch_shapes=[pltpu.SemaphoreType.DMA],
        cost_estimate=pl.CostEstimate(
            flops=0, bytes_accessed=2 * sections.size, transcendentals=0
        ),
        compiler_params=pltpu.CompilerParams(vmem_limit_bytes=limit * 2**18),
    )(sections)


def pick_kernel(leaf, info, vb_ref, *outs):
    for at, o_ref in enumerate(outs):
        o_ref[...] = piece(vb_ref, info, info[8 + at], leaf)


def basis_kernel(leaf, v_ref, high_ref, low_ref, p_ref):
    cols = v_ref.shape[0]
    for row in range(v_ref.shape[1]):
        of, part = divmod(row, 2)
        place = (slice(part * cols, (part + 1) * cols), slice(of * leaf, (of + 1) * leaf))
        high, low = split(v_ref[:, row])
        high_ref[place] = high
        low_ref[place] = low
    high = high_ref[...]
    cross = lax.dot_general(high, low_ref[...], NT, preferred_element_type=F32)
    s = lax.dot_general(high, high, NT, preferred_element_type=F32) + cross + cross.T
    p_ref[...] = packed(s, cols)


def packed(s, cols):
    below = lax.broadcasted_iota(jnp.int32, (cols, cols), 0) >= lax.broadcasted_iota(
        jnp.int32, (cols, cols), 1
    )
    re = s[:cols, :cols] + s[cols:, cols:]
    return jnp.where(below, re, s[cols:, :cols] - s[:cols, cols:])


def own_kernel(level, adjoint, s_ref, f_ref, o_ref):
    rows = o_ref.shape[0]
    product = adj if adjoint else mul
    o_ref[...] = product(s_ref[:rows], f_ref[level, 0, 0], f_ref[level, 0, 1])


def up_kernel(level, own_ref, r_ref, f_ref, *rest):
    rows = own_ref.shape[0]
    o_ref = rest[-1]
    state = own_ref[...] + mul(r_ref[:rows], f_ref[level, 1, 0], f_ref[level, 1, 1])
    o_ref[:rows] = state.astype(BF16)
    if len(rest) > 1:
        o_ref[rows:] = rest[0][...]


def leaves_kernel(leaf, adjoint, x_ref, b_ref, o_ref):
    product = adj if adjoint else mul
    for at in range(b_ref.shape[1]):
        cut = slice(at * leaf, (at + 1) * leaf)
        o_ref[:, cut] = product(x_ref[:, cut], b_ref[0, at], b_ref[1, at])


def sides_kernel(leaf, info, near_ref, ra_ref, rb_ref, rc_ref, rd_ref, b_ref, o_ref):
    rows = near_ref.shape[0]
    o_ref[...] = near_ref[...]
    for at, ref in enumerate((ra_ref, rb_ref, rc_ref, rd_ref)):
        side = info[8 + at]
        x = ref[ref.shape[0] - rows :]
        term = mul(x, b_ref[side, 0], b_ref[side, 1])
        for e in range(2):
            o_ref[:, leaf_at(info[2 * side + e], leaf)] += term[:, e * leaf : (e + 1) * leaf]


def field_kernel(level, own_ref, r_ref, f_ref, near_ref, e_ref, y_ref, yb_ref, g_ref, m_ref):
    rows = own_ref.shape[0]
    state = own_ref[...] + mul(r_ref[:rows], f_ref[level, 1, 0], f_ref[level, 1, 1])
    y = near_ref[...] + mul(state.astype(BF16), e_ref[0], e_ref[1])
    y_ref[...] = y
    yb = y.astype(BF16)
    yb_ref[...] = yb
    g = adj(yb, e_ref[0], e_ref[1]).astype(BF16)
    g_ref[...] = g
    m_ref[...] = adj(g, f_ref[level, 1, 0], f_ref[level, 1, 1]).astype(BF16)


def shape_kernel(leaf, y_ref, o_ref):
    cols = o_ref.shape[0]
    for row in range(o_ref.shape[1]):
        of, part = divmod(row, 2)
        o_ref[:, row] = y_ref[part * cols : (part + 1) * cols, of * leaf : (of + 1) * leaf]


def terms_kernel(leaf, info, yb_ref, b_ref, *outs):
    for at, o_ref in enumerate(outs):
        side = info[8 + at]
        x = piece(yb_ref, info, side, leaf)
        o_ref[...] = adj(x, b_ref[side, 0], b_ref[side, 1]).astype(BF16)


def down_kernel(level, own_ref, r_ref, f_ref, *rest):
    rows = own_ref.shape[0]
    g_ref, m_ref = rest[-2:]
    g = (own_ref[...] + r_ref[:rows].astype(F32)).astype(BF16)
    g_ref[...] = g
    m_ref[:rows] = adj(g, f_ref[level, 1, 0], f_ref[level, 1, 1]).astype(BF16)
    if len(rest) > 2:
        m_ref[rows:] = rest[0][...]


def gather_kernel(leaf, info, near_ref, ra_ref, rb_ref, rc_ref, rd_ref, o_ref):
    rows = near_ref.shape[0]
    o_ref[...] = near_ref[...]
    for at, ref in enumerate((ra_ref, rb_ref, rc_ref, rd_ref)):
        side = info[8 + at]
        low = ref.shape[0] - rows
        for e in range(2):
            o_ref[:, leaf_at(info[2 * side + e], leaf)] += ref[
                low:, e * leaf : (e + 1) * leaf
            ].astype(F32)


def close_kernel(near_ref, own_ref, r_ref, c_ref, vh_ref, vl_ref, vv_ref, zh_ref, zl_ref, p_ref):
    rows = own_ref.shape[0]
    cols = rows // 2
    g = (own_ref[...] + r_ref[...].astype(F32)).astype(BF16)
    high, low = split(near_ref[...] + adj(g, c_ref[0], c_ref[1]))
    zh_ref[...] = high
    zl_ref[...] = low
    many = jnp.concatenate([high, low, vh_ref[...], vl_ref[...]], 0)
    s = lax.dot_general(high, many, NT, preferred_element_type=F32)
    cross = s[:, rows : 2 * rows]
    zz = s[:, :rows] + cross + cross.T
    zv = s[:, 2 * rows : 3 * rows] + s[:, 3 * rows :]
    zv += lax.dot_general(low, vh_ref[...], NT, preferred_element_type=F32)
    p_ref[...] = jnp.concatenate(
        [
            packed(zz, cols),
            vv_ref[...],
            zv[:cols, :cols] + zv[cols:, cols:],
            zv[cols:, :cols] - zv[:cols, cols:],
        ],
        1,
    )


def spread_kernel(*refs):
    o_ref = refs[-1]
    total = sum(parts_of(refs[:-1]))
    for at in range(o_ref.shape[0]):
        o_ref[at] = total


def parts_of(refs):
    return [ref[at] for ref in refs for at in range(ref.shape[0])]


def exact_dot(a, b, dims=(((1,), (0,)), ((), ()))):
    return lax.dot_general(a, b, dims, preferred_element_type=F32, precision=lax.Precision.HIGHEST)


def real_form(re, im):
    return jnp.concatenate(
        [jnp.concatenate([re, im], 1), jnp.concatenate([-im, re], 1)], 0
    )


def inverse_factor(gram):
    size, step = gram.shape[0], 8
    eye = (
        lax.broadcasted_iota(jnp.int32, (size, size), 0)
        == lax.broadcasted_iota(jnp.int32, (size, size), 1)
    ).astype(F32)
    wide = jnp.concatenate([gram, eye], 1)
    width = wide.shape[1]
    blocks = [wide[step * j : step * (j + 1)] for j in range(size // step)]
    sub = lax.broadcasted_iota(jnp.int32, (step, width), 0)
    done = []
    for at in range(size // step):
        left = [
            [jnp.broadcast_to(b[:, at * step + p : at * step + p + 1], (step, width)) for b in blocks[at:]]
            for p in range(step)
        ]
        pivot = [
            [jnp.broadcast_to(left[q][0][p : p + 1], (step, width)) for q in range(p + 1)]
            for p in range(step)
        ]
        lines = [jnp.broadcast_to(blocks[at][p : p + 1], (step, width)) for p in range(step)]
        result = jnp.zeros((step, width), F32)
        updates = [None] * len(left[0])
        for p in range(step):
            inverse = 1.0 / pivot[p][p]
            result = jnp.where(sub == p, lines[p] * lax.rsqrt(pivot[p][p]), result)
            scaled = lines[p] * inverse
            for q in range(p + 1, step):
                ratio = pivot[q][p] * inverse
                lines[q] = lines[q] - ratio * lines[p]
                for r in range(p + 1, q + 1):
                    pivot[q][r] = pivot[q][r] - ratio * pivot[r][p]
                for i in range(1, len(left[q])):
                    left[q][i] = left[q][i] - ratio * left[p][i]
            for i in range(1, len(updates)):
                term = left[p][i] * scaled
                updates[i] = term if p == 0 else updates[i] + term
        done.append(result)
        for i in range(1, len(updates)):
            blocks[at + i] = blocks[at + i] - updates[i]
    return jnp.concatenate(done, 0)[:, size:]


def finish_kernel(leaf, total, p_ref, zh_ref, zl_ref, vh_ref, vl_ref, o_ref, buffer, sems):
    p = sum(parts_of([p_ref])) * (1.0 / total)
    cols = p.shape[0]
    lower = lax.broadcasted_iota(jnp.int32, (cols, cols), 0)
    upper = lax.broadcasted_iota(jnp.int32, (cols, cols), 1)

    def hermitian(t):
        turned = t.T
        re = jnp.where(lower >= upper, t, turned)
        im = jnp.where(lower < upper, t, jnp.where(lower > upper, -turned, 0.0))
        return real_form(re, im)

    zz = hermitian(p[:, :cols])
    vv = hermitian(p[:, cols : 2 * cols])
    h = real_form(p[:, 2 * cols : 3 * cols], p[:, 3 * cols :])
    nt = (((1,), (1,)), ((), ()))
    middle = exact_dot(h, vv) - 2.0 * h
    gram = zz + exact_dot(middle, h, nt)
    inverse = inverse_factor(gram)
    w = exact_dot(inverse, h)
    l1, l2 = inverse[:, :cols], inverse[:, cols:]
    w1, w2 = w[:, :cols], w[:, cols:]
    mix = jnp.concatenate(
        [
            jnp.concatenate([l1, -l2, -w1, w2], 1),
            jnp.concatenate([l2, l1, -w2, -w1], 1),
        ],
        0,
    )
    mix_high, mix_low = split(mix)
    mix = jnp.concatenate([mix_high, mix_high, mix_low], 1)
    rows = 2 * cols
    count, _, lines, _ = buffer.shape
    width = lines // 2 * leaf
    copies = []
    for at in range(count):
        cut = slice(at * width, (at + 1) * width)
        high = [zh_ref[:, cut], vh_ref[:, cut]]
        x = jnp.concatenate(high + [zl_ref[:, cut], vl_ref[:, cut]] + high, 0)
        out = jnp.dot(mix, x, preferred_element_type=F32)
        for line in range(lines):
            of, part = divmod(line, 2)
            buffer[at, :, line] = out[part * rows : (part + 1) * rows, of * leaf : (of + 1) * leaf]
        copy = pltpu.make_async_copy(
            buffer.at[at], o_ref.at[:, at * lines : (at + 1) * lines], sems.at[at]
        )
        copy.start()
        copies.append(copy)
    for copy in copies:
        copy.wait()


def per_device(v_block, edge_leaves, self_blocks, side_blocks, compress, expand, factors):
    cols = v_block.shape[0]
    unknowns = v_block.shape[4]
    leaves = self_blocks.shape[3]
    leaf = self_blocks.shape[4]
    levels = factors.shape[2]
    rank = compress.shape[4]
    rows = 2 * cols
    row_count = lax.axis_size("px")
    col_count = lax.axis_size("py")
    row_bits = row_count.bit_length() - 1
    total = 2 * unknowns * row_count * col_count
    row_at = lax.axis_index("px")
    col_at = lax.axis_index("py")
    selfs = self_blocks.reshape(self_blocks.shape[2:])
    sides = side_blocks.reshape(side_blocks.shape[2:])
    squeeze = compress.reshape(compress.shape[2:])
    spread = expand.reshape(expand.shape[2:])
    sections = factors.reshape(factors.shape[2:])
    own_leaves = lax.dynamic_slice(edge_leaves, (row_at, col_at, 0, 0), (1, 1, 4, 2)).reshape(8)
    odd_row, odd_col = row_at % 2, col_at % 2
    order = jnp.stack([1 - odd_row, odd_row, 3 - odd_col, 2 + odd_col]).astype(jnp.int32)
    info = jnp.concatenate([own_leaves, order])
    tall = v_block.reshape(cols, 2, leaves, leaf).transpose(0, 2, 1, 3).reshape(cols, -1, leaf)

    def partner(x, level):
        if level < row_bits:
            return lax.ppermute(x, "px", [(i, i ^ 1 << level) for i in range(row_count)])
        bit = level - row_bits
        return lax.ppermute(x, "py", [(i, i ^ 1 << bit) for i in range(col_count)])

    def beyond(x, axis, count):
        pairs = [(i, i + 1) for i in range(1, count - 1, 2)]
        return lax.ppermute(x, axis, pairs + [(j, i) for i, j in pairs])

    small = ((rows, rank), BF16)
    double = ((2 * rows, rank), BF16)
    wide = ((rows, rank), F32)
    step_flops = 8 * cols * rank * rank
    patch_flops = 8 * cols * rank * unknowns
    leaf_flops = 8 * cols * leaf * unknowns

    half, sent = head(leaf, tall, squeeze)
    early = 3
    first = load(sections, 0, early, EARLY)
    rest = load(sections, early, levels, LATE)

    def weights(level):
        return (first, level) if level < early else (rest, level - early)

    got = {}
    for level in range(levels):
        arrived = partner(sent, level)
        after = []
        if level == 1:
            pieces = call(
                functools.partial(pick_kernel, leaf), [small] * 4, [info, half], 0, smem=1, after=[sent]
            )
            after = list(pieces) + [rest]
        if level == 2:
            (near,) = call(
                functools.partial(leaves_kernel, leaf, False),
                [((rows, unknowns), F32)],
                [half, selfs],
                leaf_flops,
                after=[sent],
            )
            after = [near]
            got["a"] = partner(pieces[0], 0)
        if level == 3:
            after = [got["a"]]
        if level == row_bits:
            got["c"] = arrived
            got["b"] = beyond(pieces[1], "px", row_count)
            got["d"] = beyond(pieces[3], "py", col_count)
        if level == levels - 1:
            (near,) = call(
                functools.partial(sides_kernel, leaf),
                [((rows, unknowns), F32)],
                [info, near, got["a"], got["b"], got["c"], got["d"], sides],
                4 * step_flops,
                smem=1,
                after=[sent],
            )
            after = [near, spread]
        f, at = weights(level)
        (own,) = call(
            functools.partial(own_kernel, at, False),
            [wide],
            [sent, f],
            step_flops,
            after=after,
        )
        if level < levels - 1:
            extra = [pieces[2]] if level == row_bits - 1 else []
            (sent,) = call(
                functools.partial(up_kernel, at),
                [double if extra else small],
                [own, arrived, f] + extra,
                step_flops,
            )
    y, yb, g, message = call(
        functools.partial(field_kernel, at),
        [((rows, unknowns), F32), ((rows, unknowns), BF16), small, small],
        [own, arrived, f, near, spread],
        2 * patch_flops,
    )
    terms = call(
        functools.partial(terms_kernel, leaf), [small] * 4, [info, yb, sides], 4 * step_flops, smem=1
    )
    (shaped,) = call(
        functools.partial(shape_kernel, leaf), [((cols, 2 * leaves, leaf), F32)], [y], 0
    )
    for level in range(levels - 1, -1, -1):
        arrived = partner(message, level)
        after = []
        if level == levels - 1:
            after = list(terms)
        if level == levels - 2:
            (z_near,) = call(
                functools.partial(leaves_kernel, leaf, True),
                [((rows, unknowns), F32)],
                [yb, selfs],
                leaf_flops,
                after=[message],
            )
            after = [z_near]
        if level == row_bits:
            got["c"] = arrived
        if level == 4:
            v_high, v_low, vv = call(
                functools.partial(basis_kernel, leaf),
                [((rows, unknowns), BF16), ((rows, unknowns), BF16), ((cols, cols), F32)],
                [tall],
                leaf_flops,
                after=[message],
            )
            after = [v_high, v_low, vv]
        if level == 3:
            got["d"] = beyond(terms[3], "py", col_count)
        if level == 2:
            after = [got["d"]]
            got["a"] = partner(terms[0], 0)
        if level == 1:
            after = [got["a"], squeeze]
            got["b"] = beyond(terms[1], "px", row_count)
        if level == 0:
            (z_near,) = call(
                functools.partial(gather_kernel, leaf),
                [((rows, unknowns), F32)],
                [info, z_near, got["a"], got["b"], got["c"], got["d"]],
                0,
                smem=1,
            )
            after = [z_near]
        f, at = weights(level)
        (own,) = call(
            functools.partial(own_kernel, at, True),
            [wide],
            [g, f],
            step_flops,
            after=after,
        )
        if level > 0:
            extra = [terms[2]] if level == row_bits + 1 else []
            f, at = weights(level - 1)
            g, message = call(
                functools.partial(down_kernel, at),
                [small, double if extra else small],
                [own, arrived, f] + extra,
                step_flops,
            )
    z_high, z_low, part = call(
        close_kernel,
        [((rows, unknowns), BF16), ((rows, unknowns), BF16), ((cols, 4 * cols), F32)],
        [z_near, own, arrived, squeeze, v_high, v_low, vv],
        patch_flops,
    )
    part = part.reshape(1, cols, 4 * cols)
    chips = row_count // 2
    (part,) = call(
        spread_kernel, [((chips, cols, 4 * cols), F32)], [part, partner(part, 0)], 0
    )
    groups = [[2 * i + core for i in range(chips)] for core in range(2)]
    part = lax.all_to_all(part, "px", 0, 0, axis_index_groups=groups, tiled=True)
    (part,) = call(spread_kernel, [((col_count, cols, 4 * cols), F32)], [part], 0)
    part = lax.all_to_all(part, "py", 0, 0, tiled=True)
    lines = 8
    (basis,) = call(
        functools.partial(finish_kernel, leaf, total),
        [((rows, 2 * leaves, leaf), F32)],
        [part, z_high, z_low, v_high, v_low],
        8 * rows * rows * unknowns,
        out_spec=pl.BlockSpec(memory_space=pl.ANY),
        scratch=[
            pltpu.VMEM((2 * leaves // lines, rows, lines, leaf), F32),
            pltpu.SemaphoreType.DMA((2 * leaves // lines,)),
        ],
    )

    def patch_form(a):
        count = a.shape[0]
        a = a.reshape(count, leaves, 2, leaf).transpose(0, 2, 1, 3)
        return a.reshape(count, 1, 1, 2, unknowns)

    return patch_form(shaped), patch_form(basis)


def solution(mesh):
    in_specs = (
        P(None, "px", "py", None, None),
        P(),
        P("px", "py", None, None, None, None),
        P("px", "py", None, None, None, None),
        P("px", "py", None, None, None),
        P("px", "py", None, None, None),
        P("px", "py", None, None, None, None, None),
    )
    out_specs = (P(None, "px", "py", None, None), P(None, "px", "py", None, None))
    return jax.shard_map(
        per_device, mesh=mesh, in_specs=in_specs, out_specs=out_specs, check_vma=False
    )
```

```python
import functools
import math

import jax
import jax.numpy as jnp
from jax import lax
from jax.experimental import pallas as pl
from jax.experimental.pallas import tpu as pltpu
from jax.sharding import PartitionSpec as P

F32 = jnp.float32
BF16 = jnp.bfloat16
NT = (((1,), (1,)), ((), ()))
VM = pl.BlockSpec(memory_space=pltpu.VMEM)
SM = pl.BlockSpec(memory_space=pltpu.SMEM)

HEAD, EARLY, LATE, OTHER = 214, 200, 188, 180


def call(kernel, outs, args, flops, smem=0, limit=24, after=(), out_spec=VM, scratch=()):
    size = sum(a.size * a.dtype.itemsize for a in args)
    args = list(args) + list(after)
    count, extra = len(args), len(after)

    def body(*refs):
        kernel(*refs[: count - extra], *refs[count:])

    return pl.pallas_call(
        body,
        out_shape=[jax.ShapeDtypeStruct(s, d) for s, d in outs],
        in_specs=[SM] * smem + [VM] * (count - smem),
        out_specs=[out_spec] * len(outs),
        scratch_shapes=list(scratch),
        cost_estimate=pl.CostEstimate(flops=flops, bytes_accessed=size, transcendentals=0),
        compiler_params=pltpu.CompilerParams(vmem_limit_bytes=limit * 2**20),
    )(*args)


def mul(x, gr, gi):
    h = x.shape[0] // 2
    re, im = x[:h], x[h:]
    first = jnp.dot(x, gr, preferred_element_type=F32)
    second = jnp.dot(jnp.concatenate([-im, re], 0), gi, preferred_element_type=F32)
    return first + second


def adj(x, gr, gi):
    h = x.shape[0] // 2
    re, im = x[:h], x[h:]
    first = lax.dot_general(x, gr, NT, preferred_element_type=F32)
    second = lax.dot_general(jnp.concatenate([im, -re], 0), gi, NT, preferred_element_type=F32)
    return first + second


def leaf_at(at, leaf):
    return pl.ds(pl.multiple_of(at * leaf, leaf), leaf)


def split(x):
    high = x.astype(BF16)
    return high, (x - high.astype(F32)).astype(BF16)


def piece(ref, info, side, leaf):
    return jnp.concatenate(
        [ref[:, leaf_at(info[2 * side + e], leaf)] for e in range(2)], 1
    )


def head_kernel(leaf, v_in, c_in, vb_ref, m_ref, v_ref, c_ref, v_sems, c_sems):
    cols, lines, _ = v_ref.shape
    count = v_sems.shape[0]
    step = lines // count
    width = step // 2 * leaf
    copies = []
    for at in range(count):
        some = slice(at * step, (at + 1) * step)
        cut = slice(at * width, (at + 1) * width)
        pair = [
            pltpu.make_async_copy(v_in.at[:, some], v_ref.at[:, some], v_sems.at[at]),
            pltpu.make_async_copy(c_in.at[:, cut], c_ref.at[:, cut], c_sems.at[at]),
        ]
        for copy in pair:
            copy.start()
        copies.append(pair)
    total = None
    for at in range(count):
        copies[at][0].wait()
        for row in range(at * step, (at + 1) * step):
            of, part = divmod(row, 2)
            vb_ref[part * cols : (part + 1) * cols, of * leaf : (of + 1) * leaf] = v_ref[
                :, row
            ].astype(BF16)
        copies[at][1].wait()
        cut = slice(at * width, (at + 1) * width)
        product = mul(vb_ref[:, cut], c_ref[0, cut], c_ref[1, cut])
        total = product if total is None else total + product
    m_ref[...] = total.astype(BF16)


def head(leaf, tall, squeeze):
    cols = tall.shape[0]
    unknowns, rank = squeeze.shape[1:]
    count = 4
    return pl.pallas_call(
        functools.partial(head_kernel, leaf),
        in_specs=[pl.BlockSpec(memory_space=pltpu.HBM)] * 2,
        out_specs=[VM] * 2,
        out_shape=[
            jax.ShapeDtypeStruct((2 * cols, unknowns), BF16),
            jax.ShapeDtypeStruct((2 * cols, rank), BF16),
        ],
        scratch_shapes=[
            pltpu.VMEM(tall.shape, F32),
            pltpu.VMEM(squeeze.shape, BF16),
            pltpu.SemaphoreType.DMA((count,)),
            pltpu.SemaphoreType.DMA((count,)),
        ],
        cost_estimate=pl.CostEstimate(
            flops=8 * cols * rank * unknowns,
            bytes_accessed=tall.size * 4 + squeeze.size * 2,
            transcendentals=0,
        ),
        compiler_params=pltpu.CompilerParams(vmem_limit_bytes=HEAD * 2**18),
    )(tall, squeeze)


def load_kernel(begin, f_in, *rest):
    o_ref, sem = rest[-2:]
    copy = pltpu.make_async_copy(f_in.at[begin : begin + o_ref.shape[0]], o_ref, sem)
    copy.start()
    copy.wait()


def load(sections, begin, end, limit, after=()):
    shape = (end - begin,) + sections.shape[1:]
    return pl.pallas_call(
        functools.partial(load_kernel, begin),
        in_specs=[pl.BlockSpec(memory_space=pltpu.HBM)] + [VM] * len(after),
        out_specs=VM,
        out_shape=jax.ShapeDtypeStruct(shape, BF16),
        scratch_shapes=[pltpu.SemaphoreType.DMA],
        cost_estimate=pl.CostEstimate(
            flops=0, bytes_accessed=2 * math.prod(shape), transcendentals=0
        ),
        compiler_params=pltpu.CompilerParams(vmem_limit_bytes=limit * 2**18),
    )(sections, *after)


def pick_kernel(leaf, info, vb_ref, *outs):
    for at, o_ref in enumerate(outs):
        o_ref[...] = piece(vb_ref, info, info[8 + at], leaf)


def basis_kernel(leaf, v_ref, high_ref, low_ref, p_ref):
    cols = v_ref.shape[0]
    for row in range(v_ref.shape[1]):
        of, part = divmod(row, 2)
        place = (slice(part * cols, (part + 1) * cols), slice(of * leaf, (of + 1) * leaf))
        high, low = split(v_ref[:, row])
        high_ref[place] = high
        low_ref[place] = low
    high = high_ref[...]
    cross = lax.dot_general(high, low_ref[...], NT, preferred_element_type=F32)
    s = lax.dot_general(high, high, NT, preferred_element_type=F32) + cross + cross.T
    p_ref[...] = packed(s, cols)


def packed(s, cols):
    below = lax.broadcasted_iota(jnp.int32, (cols, cols), 0) >= lax.broadcasted_iota(
        jnp.int32, (cols, cols), 1
    )
    re = s[:cols, :cols] + s[cols:, cols:]
    return jnp.where(below, re, s[cols:, :cols] - s[:cols, cols:])


def own_kernel(at, adjoint, s_ref, f_ref, *rest):
    o_ref = rest[-1]
    rows = o_ref.shape[0] // len(rest)
    product = adj if adjoint else mul
    for part, f in enumerate((f_ref,) + rest[:-1]):
        cut = slice(part * rows, (part + 1) * rows)
        o_ref[cut] = product(s_ref[cut], f[at, 0, 0], f[at, 0, 1])


def up_kernel(at, count, own_ref, r_ref, *rest):
    rows = own_ref.shape[0] // count
    outs = rest[count:]
    for part, f in enumerate(rest[:count]):
        cut = slice(part * rows, (part + 1) * rows)
        state = own_ref[cut] + mul(r_ref[cut], f[at, 1, 0], f[at, 1, 1])
        if len(outs) == count:
            outs[part][...] = state.astype(BF16)
        else:
            outs[0][cut] = state.astype(BF16)


def join_kernel(a_ref, b_ref, o_ref):
    rows = a_ref.shape[0]
    o_ref[:rows] = a_ref[...]
    o_ref[rows:] = b_ref[...]


def leaves_kernel(leaf, adjoint, x_ref, b_ref, o_ref):
    product = adj if adjoint else mul
    for at in range(b_ref.shape[1]):
        cut = slice(at * leaf, (at + 1) * leaf)
        o_ref[:, cut] = product(x_ref[:, cut], b_ref[0, at], b_ref[1, at])


def sides_kernel(leaf, info, near_ref, ra_ref, rb_ref, rc_ref, rd_ref, b_ref, o_ref):
    o_ref[...] = near_ref[...]
    for at, ref in enumerate((ra_ref, rb_ref, rc_ref, rd_ref)):
        side = info[8 + at]
        term = mul(ref[...], b_ref[side, 0], b_ref[side, 1])
        for e in range(2):
            o_ref[:, leaf_at(info[2 * side + e], leaf)] += term[:, e * leaf : (e + 1) * leaf]


def field_kernel(info, mine_ref, sent_ref, near_ref, e_ref, y_ref, yb_ref, g_ref, state_ref):
    chosen(info, mine_ref, sent_ref, state_ref)
    y = near_ref[...] + mul(state_ref[...], e_ref[0], e_ref[1])
    y_ref[...] = y
    yb = y.astype(BF16)
    yb_ref[...] = yb
    g_ref[...] = adj(yb, e_ref[0], e_ref[1]).astype(BF16)


def chosen(info, mine_ref, sent_ref, o_ref):
    @pl.when(info[12] == 1)
    def _():
        o_ref[...] = mine_ref[...]

    @pl.when(info[12] == 0)
    def _():
        o_ref[...] = sent_ref[...]


def shape_kernel(leaf, y_ref, o_ref):
    cols = o_ref.shape[0]
    for row in range(o_ref.shape[1]):
        of, part = divmod(row, 2)
        o_ref[:, row] = y_ref[part * cols : (part + 1) * cols, of * leaf : (of + 1) * leaf]


def terms_kernel(leaf, info, yb_ref, b_ref, *outs):
    for at, o_ref in enumerate(outs):
        side = info[8 + at]
        x = piece(yb_ref, info, side, leaf)
        o_ref[...] = adj(x, b_ref[side, 0], b_ref[side, 1]).astype(BF16)


def turn_kernel(at, a_ref, b_ref, f_ref, fo_ref, g_ref, m_ref):
    rows = a_ref.shape[0]
    for part, (x, f) in enumerate(((a_ref, f_ref), (b_ref, fo_ref))):
        cut = slice(part * rows, (part + 1) * rows)
        g_ref[cut] = x[...]
        m_ref[cut] = adj(x[...], f[at, 1, 0], f[at, 1, 1]).astype(BF16)


def down_kernel(at, own_ref, r_ref, f_ref, fo_ref, g_ref, m_ref):
    rows = own_ref.shape[0] // 2
    for part, f in enumerate((f_ref, fo_ref)):
        cut = slice(part * rows, (part + 1) * rows)
        g = (own_ref[cut] + r_ref[cut].astype(F32)).astype(BF16)
        g_ref[cut] = g
        m_ref[cut] = adj(g, f[at, 1, 0], f[at, 1, 1]).astype(BF16)


def last_kernel(own_ref, r_ref, f_ref, fo_ref, mine_ref, other_ref):
    rows = mine_ref.shape[0]
    a, b = [
        (own_ref[cut] + r_ref[cut].astype(F32)).astype(BF16)
        for cut in (slice(0, rows), slice(rows, 2 * rows))
    ]
    for x, f, y, h, o_ref in ((a, f_ref, b, fo_ref, mine_ref), (b, fo_ref, a, f_ref, other_ref)):
        message = adj(y, h[0, 1, 0], h[0, 1, 1]).astype(BF16).astype(F32)
        o_ref[...] = (adj(x, f[0, 0, 0], f[0, 0, 1]) + message).astype(BF16)


def gather_kernel(leaf, info, near_ref, ra_ref, rb_ref, rc_ref, rd_ref, o_ref):
    o_ref[...] = near_ref[...]
    for at, ref in enumerate((ra_ref, rb_ref, rc_ref, rd_ref)):
        side = info[8 + at]
        for e in range(2):
            o_ref[:, leaf_at(info[2 * side + e], leaf)] += ref[:, e * leaf : (e + 1) * leaf].astype(F32)


def close_kernel(
    info, near_ref, mine_ref, sent_ref, c_ref, vh_ref, vl_ref, vv_ref, zh_ref, zl_ref, p_ref, g_ref
):
    rows = mine_ref.shape[0]
    cols = rows // 2
    chosen(info, mine_ref, sent_ref, g_ref)
    high, low = split(near_ref[...] + adj(g_ref[...], c_ref[0], c_ref[1]))
    zh_ref[...] = high
    zl_ref[...] = low
    many = jnp.concatenate([high, low, vh_ref[...], vl_ref[...]], 0)
    s = lax.dot_general(high, many, NT, preferred_element_type=F32)
    cross = s[:, rows : 2 * rows]
    zz = s[:, :rows] + cross + cross.T
    zv = s[:, 2 * rows : 3 * rows] + s[:, 3 * rows :]
    zv += lax.dot_general(low, vh_ref[...], NT, preferred_element_type=F32)
    p_ref[...] = jnp.concatenate(
        [
            packed(zz, cols),
            vv_ref[...],
            zv[:cols, :cols] + zv[cols:, cols:],
            zv[cols:, :cols] - zv[:cols, cols:],
        ],
        1,
    )


def spread_kernel(*refs):
    o_ref = refs[-1]
    total = sum(parts_of(refs[:-1]))
    for at in range(o_ref.shape[0]):
        o_ref[at] = total


def parts_of(refs):
    return [ref[at] for ref in refs for at in range(ref.shape[0])]


def exact_dot(a, b, dims=(((1,), (0,)), ((), ()))):
    return lax.dot_general(a, b, dims, preferred_element_type=F32, precision=lax.Precision.HIGHEST)


def real_form(re, im):
    return jnp.concatenate(
        [jnp.concatenate([re, im], 1), jnp.concatenate([-im, re], 1)], 0
    )


def inverse_factor(gram):
    size, step = gram.shape[0], 8
    eye = (
        lax.broadcasted_iota(jnp.int32, (size, size), 0)
        == lax.broadcasted_iota(jnp.int32, (size, size), 1)
    ).astype(F32)
    wide = jnp.concatenate([gram, eye], 1)
    width = wide.shape[1]
    blocks = [wide[step * j : step * (j + 1)] for j in range(size // step)]
    sub = lax.broadcasted_iota(jnp.int32, (step, width), 0)
    done = []
    for at in range(size // step):
        left = [
            [jnp.broadcast_to(b[:, at * step + p : at * step + p + 1], (step, width)) for b in blocks[at:]]
            for p in range(step)
        ]
        pivot = [
            [jnp.broadcast_to(left[q][0][p : p + 1], (step, width)) for q in range(p + 1)]
            for p in range(step)
        ]
        lines = [jnp.broadcast_to(blocks[at][p : p + 1], (step, width)) for p in range(step)]
        result = jnp.zeros((step, width), F32)
        updates = [None] * len(left[0])
        for p in range(step):
            inverse = 1.0 / pivot[p][p]
            result = jnp.where(sub == p, lines[p] * lax.rsqrt(pivot[p][p]), result)
            scaled = lines[p] * inverse
            for q in range(p + 1, step):
                ratio = pivot[q][p] * inverse
                lines[q] = lines[q] - ratio * lines[p]
                for r in range(p + 1, q + 1):
                    pivot[q][r] = pivot[q][r] - ratio * pivot[r][p]
                for i in range(1, len(left[q])):
                    left[q][i] = left[q][i] - ratio * left[p][i]
            for i in range(1, len(updates)):
                term = left[p][i] * scaled
                updates[i] = term if p == 0 else updates[i] + term
        done.append(result)
        for i in range(1, len(updates)):
            blocks[at + i] = blocks[at + i] - updates[i]
    return jnp.concatenate(done, 0)[:, size:]


def finish_kernel(leaf, total, p_ref, zh_ref, zl_ref, vh_ref, vl_ref, o_ref, buffer, sems):
    p = sum(parts_of([p_ref])) * (1.0 / total)
    cols = p.shape[0]
    lower = lax.broadcasted_iota(jnp.int32, (cols, cols), 0)
    upper = lax.broadcasted_iota(jnp.int32, (cols, cols), 1)

    def hermitian(t):
        turned = t.T
        re = jnp.where(lower >= upper, t, turned)
        im = jnp.where(lower < upper, t, jnp.where(lower > upper, -turned, 0.0))
        return real_form(re, im)

    zz = hermitian(p[:, :cols])
    vv = hermitian(p[:, cols : 2 * cols])
    h = real_form(p[:, 2 * cols : 3 * cols], p[:, 3 * cols :])
    nt = (((1,), (1,)), ((), ()))
    middle = exact_dot(h, vv) - 2.0 * h
    gram = zz + exact_dot(middle, h, nt)
    inverse = inverse_factor(gram)
    w = exact_dot(inverse, h)
    l1, l2 = inverse[:, :cols], inverse[:, cols:]
    w1, w2 = w[:, :cols], w[:, cols:]
    mix = jnp.concatenate(
        [
            jnp.concatenate([l1, -l2, -w1, w2], 1),
            jnp.concatenate([l2, l1, -w2, -w1], 1),
        ],
        0,
    )
    mix_high, mix_low = split(mix)
    mix = jnp.concatenate([mix_high, mix_high, mix_low], 1)
    rows = 2 * cols
    count, _, lines, _ = buffer.shape
    width = lines // 2 * leaf
    copies = []
    for at in range(count):
        cut = slice(at * width, (at + 1) * width)
        high = [zh_ref[:, cut], vh_ref[:, cut]]
        x = jnp.concatenate(high + [zl_ref[:, cut], vl_ref[:, cut]] + high, 0)
        out = jnp.dot(mix, x, preferred_element_type=F32)
        for line in range(lines):
            of, part = divmod(line, 2)
            buffer[at, :, line] = out[part * rows : (part + 1) * rows, of * leaf : (of + 1) * leaf]
        copy = pltpu.make_async_copy(
            buffer.at[at], o_ref.at[:, at * lines : (at + 1) * lines], sems.at[at]
        )
        copy.start()
        copies.append(copy)
    for copy in copies:
        copy.wait()


def per_device(v_block, edge_leaves, self_blocks, side_blocks, compress, expand, factors):
    cols = v_block.shape[0]
    unknowns = v_block.shape[4]
    leaves = self_blocks.shape[3]
    leaf = self_blocks.shape[4]
    levels = factors.shape[2]
    rank = compress.shape[4]
    rows = 2 * cols
    row_count = lax.axis_size("px")
    col_count = lax.axis_size("py")
    row_bits = row_count.bit_length() - 1
    total = 2 * unknowns * row_count * col_count
    row_at = lax.axis_index("px")
    col_at = lax.axis_index("py")
    selfs = self_blocks.reshape(self_blocks.shape[2:])
    sides = side_blocks.reshape(side_blocks.shape[2:])
    squeeze = compress.reshape(compress.shape[2:])
    spread = expand.reshape(expand.shape[2:])
    sections = factors.reshape(factors.shape[2:])
    own_leaves = lax.dynamic_slice(edge_leaves, (row_at, col_at, 0, 0), (1, 1, 4, 2)).reshape(8)
    odd_row, odd_col = row_at % 2, col_at % 2
    order = jnp.stack([1 - odd_row, odd_row, 3 - odd_col, 2 + odd_col]).astype(jnp.int32)
    info = jnp.concatenate([own_leaves, order, odd_row[None].astype(jnp.int32)])
    tall = v_block.reshape(cols, 2, leaves, leaf).transpose(0, 2, 1, 3).reshape(cols, -1, leaf)

    def partner(x, level):
        near_bit, far_bit = (1 << level, 0) if level < row_bits else (0, 1 << level - row_bits)
        pairs = [
            (i * col_count + j, (i ^ near_bit) * col_count + (j ^ far_bit))
            for i in range(1, row_count, 2)
            for j in range(col_count)
        ]
        return lax.ppermute(x, ("px", "py"), pairs)

    def swapped(x, axis, count):
        return lax.ppermute(x, axis, [(i, i ^ 1) for i in range(count)])

    def over(x):
        return lax.ppermute(x, "px", [(i, i + 1) for i in range(0, row_count, 2)])

    def back(x):
        return lax.ppermute(x, "px", [(i + 1, i) for i in range(0, row_count, 2)])

    def beyond(x, axis, count):
        pairs = [(i, i + 1) for i in range(1, count - 1, 2)]
        return lax.ppermute(x, axis, pairs + [(j, i) for i, j in pairs])

    small = ((rows, rank), BF16)
    double = ((2 * rows, rank), BF16)
    wide = ((rows, rank), F32)
    wide_double = ((2 * rows, rank), F32)
    step_flops = 8 * cols * rank * rank
    patch_flops = 8 * cols * rank * unknowns
    leaf_flops = 8 * cols * leaf * unknowns

    half, sent = head(leaf, tall, squeeze)
    bounds = [0, 1, 3, levels]
    sections_sent = over(sections)
    zero = load(sections, 0, 1, EARLY, [sent])
    arrived = swapped(sent, "px", row_count)
    (own,) = call(functools.partial(own_kernel, 0, False), [wide], [sent, zero], step_flops)
    (sent,) = call(functools.partial(up_kernel, 0, 1), [small], [own, arrived, zero], step_flops)
    first = load(sections, 1, 3, EARLY, [sent])
    other = over(sent)
    (sent,) = call(join_kernel, [double], [sent, other], 0, after=[first])
    held = {0: zero, 1: first}
    held_other = {}

    def weights(level):
        at = sum(level >= low for low in bounds[1:-1])
        for now, array, limit in ((held, sections, LATE), (held_other, sections_sent, OTHER)):
            if at not in now:
                now[at] = load(array, bounds[at], bounds[at + 1], limit, [sent])
        return [held[at], held_other[at]], level - bounds[at]

    got = {}
    for level in range(1, levels):
        arrived = partner(sent, level)
        after, ended = [], []
        if level == 1:
            pieces = call(
                functools.partial(pick_kernel, leaf), [small] * 4, [info, half], 0, smem=1, after=[sent]
            )
            after = list(pieces)
        if level == 2:
            f, _ = weights(level + 1)
            ended = f
            (near,) = call(
                functools.partial(leaves_kernel, leaf, False),
                [((rows, unknowns), F32)],
                [half, selfs],
                leaf_flops,
                after=[sent],
            )
            after = [near]
        if level == 3:
            got["a"] = swapped(pieces[0], "px", row_count)
            ended = [got["a"]]
        if level == row_bits + 1:
            got["b"] = beyond(pieces[1], "px", row_count)
            ended = [got["b"]]
            got["c"] = swapped(pieces[2], "py", col_count)
            got["d"] = beyond(pieces[3], "py", col_count)
        f, at = weights(level)
        (own,) = call(
            functools.partial(own_kernel, at, False),
            [wide_double],
            [sent] + f,
            2 * step_flops,
            after=after,
        )
        last = level == levels - 1
        outs = call(
            functools.partial(up_kernel, at, 2),
            [small, small] if last else [double],
            [own, arrived] + f,
            2 * step_flops,
            after=ended,
        )
        sent = outs[0]
    mine, other = outs
    other = back(other)
    (near,) = call(
        functools.partial(sides_kernel, leaf),
        [((rows, unknowns), F32)],
        [info, near, got["a"], got["b"], got["c"], got["d"], sides],
        4 * step_flops,
        smem=1,
        after=[mine],
    )
    y, yb, g = call(
        field_kernel,
        [((rows, unknowns), F32), ((rows, unknowns), BF16), small],
        [info, mine, other, near, spread],
        2 * patch_flops,
        smem=1,
        scratch=[pltpu.VMEM((rows, rank), BF16)],
    )
    other = over(g)
    terms = call(
        functools.partial(terms_kernel, leaf), [small] * 4, [info, yb, sides], 4 * step_flops, smem=1
    )
    (shaped,) = call(
        functools.partial(shape_kernel, leaf), [((cols, 2 * leaves, leaf), F32)], [y], 0
    )
    f, at = weights(levels - 1)
    g, message = call(
        functools.partial(turn_kernel, at), [double, double], [g, other] + f, 2 * step_flops
    )
    for level in range(levels - 1, 0, -1):
        arrived = partner(message, level)
        after, ended = [], []
        if level == levels - 1:
            after = list(terms)
        if level == levels - 2:
            (z_near,) = call(
                functools.partial(leaves_kernel, leaf, True),
                [((rows, unknowns), F32)],
                [yb, selfs],
                leaf_flops,
                after=[message],
            )
            after = [z_near]
        if level == 4:
            v_high, v_low, vv = call(
                functools.partial(basis_kernel, leaf),
                [((rows, unknowns), BF16), ((rows, unknowns), BF16), ((cols, cols), F32)],
                [tall],
                leaf_flops,
                after=[message],
            )
            after = [v_high, v_low, vv]
            got["c"] = swapped(terms[2], "py", col_count)
            ended = [got["c"]]
        if level == 3:
            got["d"] = beyond(terms[3], "py", col_count)
            ended = [got["d"]]
        if level == 2:
            got["a"] = swapped(terms[0], "px", row_count)
            ended = [got["a"]]
        if level == 1:
            after = [squeeze]
            got["b"] = beyond(terms[1], "px", row_count)
        f, at = weights(level)
        (own,) = call(
            functools.partial(own_kernel, at, True),
            [wide_double],
            [g] + f,
            2 * step_flops,
            after=after,
        )
        if level > 1:
            f, at = weights(level - 1)
            g, message = call(
                functools.partial(down_kernel, at),
                [double, double],
                [own, arrived] + f,
                2 * step_flops,
                after=ended,
            )
    f, at = weights(0)
    mine, other = call(
        last_kernel, [small, small], [own, arrived] + f, 4 * step_flops
    )
    other = back(other)
    (z_near,) = call(
        functools.partial(gather_kernel, leaf),
        [((rows, unknowns), F32)],
        [info, z_near, got["a"], got["b"], got["c"], got["d"]],
        0,
        smem=1,
    )
    z_high, z_low, part = call(
        close_kernel,
        [((rows, unknowns), BF16), ((rows, unknowns), BF16), ((cols, 4 * cols), F32)],
        [info, z_near, mine, other, squeeze, v_high, v_low, vv],
        patch_flops,
        smem=1,
        scratch=[pltpu.VMEM((rows, rank), BF16)],
    )
    part = part.reshape(1, cols, 4 * cols)
    chips = row_count // 2
    (part,) = call(
        spread_kernel, [((chips, cols, 4 * cols), F32)], [part, swapped(part, "px", row_count)], 0
    )
    groups = [[2 * i + core for i in range(chips)] for core in range(2)]
    part = lax.all_to_all(part, "px", 0, 0, axis_index_groups=groups, tiled=True)
    (part,) = call(spread_kernel, [((col_count, cols, 4 * cols), F32)], [part], 0)
    part = lax.all_to_all(part, "py", 0, 0, tiled=True)
    lines = 8
    (basis,) = call(
        functools.partial(finish_kernel, leaf, total),
        [((rows, 2 * leaves, leaf), F32)],
        [part, z_high, z_low, v_high, v_low],
        8 * rows * rows * unknowns,
        out_spec=pl.BlockSpec(memory_space=pl.ANY),
        scratch=[
            pltpu.VMEM((2 * leaves // lines, rows, lines, leaf), F32),
            pltpu.SemaphoreType.DMA((2 * leaves // lines,)),
        ],
    )

    def patch_form(a):
        count = a.shape[0]
        a = a.reshape(count, leaves, 2, leaf).transpose(0, 2, 1, 3)
        return a.reshape(count, 1, 1, 2, unknowns)

    return patch_form(shaped), patch_form(basis)


def solution(mesh):
    in_specs = (
        P(None, "px", "py", None, None),
        P(),
        P("px", "py", None, None, None, None),
        P("px", "py", None, None, None, None),
        P("px", "py", None, None, None),
        P("px", "py", None, None, None),
        P("px", "py", None, None, None, None, None),
    )
    out_specs = (P(None, "px", "py", None, None), P(None, "px", "py", None, None))
    return jax.shard_map(
        per_device, mesh=mesh, in_specs=in_specs, out_specs=out_specs, check_vma=False
    )
```

```python
import functools

import jax
import jax.numpy as jnp
from jax import lax
from jax.experimental import pallas as pl
from jax.experimental.pallas import tpu as pltpu
from jax.sharding import PartitionSpec as P

F32 = jnp.float32
BF16 = jnp.bfloat16
NT = (((1,), (1,)), ((), ()))
VM = pl.BlockSpec(memory_space=pltpu.VMEM)
SM = pl.BlockSpec(memory_space=pltpu.SMEM)

HEAD, EARLY, LATE = 214, 203, 200


def call(kernel, outs, args, flops, smem=0, limit=24, after=(), out_spec=VM, scratch=()):
    size = sum(a.size * a.dtype.itemsize for a in args)
    args = list(args) + list(after)
    count, extra = len(args), len(after)

    def body(*refs):
        kernel(*refs[: count - extra], *refs[count:])

    return pl.pallas_call(
        body,
        out_shape=[jax.ShapeDtypeStruct(s, d) for s, d in outs],
        in_specs=[SM] * smem + [VM] * (count - smem),
        out_specs=[out_spec] * len(outs),
        scratch_shapes=list(scratch),
        cost_estimate=pl.CostEstimate(flops=flops, bytes_accessed=size, transcendentals=0),
        compiler_params=pltpu.CompilerParams(vmem_limit_bytes=limit * 2**20),
    )(*args)


def mul(x, gr, gi):
    h = x.shape[0] // 2
    re, im = x[:h], x[h:]
    first = jnp.dot(x, gr, preferred_element_type=F32)
    second = jnp.dot(jnp.concatenate([-im, re], 0), gi, preferred_element_type=F32)
    return first + second


def adj(x, gr, gi):
    h = x.shape[0] // 2
    re, im = x[:h], x[h:]
    first = lax.dot_general(x, gr, NT, preferred_element_type=F32)
    second = lax.dot_general(jnp.concatenate([im, -re], 0), gi, NT, preferred_element_type=F32)
    return first + second


def leaf_at(at, leaf):
    return pl.ds(pl.multiple_of(at * leaf, leaf), leaf)


def split(x):
    high = x.astype(BF16)
    return high, (x - high.astype(F32)).astype(BF16)


def piece(ref, info, side, leaf):
    return jnp.concatenate(
        [ref[:, leaf_at(info[2 * side + e], leaf)] for e in range(2)], 1
    )


def head_kernel(leaf, v_in, c_in, vb_ref, m_ref, v_ref, c_ref, v_sems, c_sems):
    cols, lines, _ = v_ref.shape
    count = v_sems.shape[0]
    step = lines // count
    width = step // 2 * leaf
    copies = []
    for at in range(count):
        some = slice(at * step, (at + 1) * step)
        cut = slice(at * width, (at + 1) * width)
        pair = [
            pltpu.make_async_copy(v_in.at[:, some], v_ref.at[:, some], v_sems.at[at]),
            pltpu.make_async_copy(c_in.at[:, cut], c_ref.at[:, cut], c_sems.at[at]),
        ]
        for copy in pair:
            copy.start()
        copies.append(pair)
    total = None
    for at in range(count):
        copies[at][0].wait()
        for row in range(at * step, (at + 1) * step):
            of, part = divmod(row, 2)
            vb_ref[part * cols : (part + 1) * cols, of * leaf : (of + 1) * leaf] = v_ref[
                :, row
            ].astype(BF16)
        copies[at][1].wait()
        cut = slice(at * width, (at + 1) * width)
        product = mul(vb_ref[:, cut], c_ref[0, cut], c_ref[1, cut])
        total = product if total is None else total + product
    m_ref[...] = total.astype(BF16)


def head(leaf, tall, squeeze):
    cols = tall.shape[0]
    unknowns, rank = squeeze.shape[1:]
    count = 4
    return pl.pallas_call(
        functools.partial(head_kernel, leaf),
        in_specs=[pl.BlockSpec(memory_space=pltpu.HBM)] * 2,
        out_specs=[VM] * 2,
        out_shape=[
            jax.ShapeDtypeStruct((2 * cols, unknowns), BF16),
            jax.ShapeDtypeStruct((2 * cols, rank), BF16),
        ],
        scratch_shapes=[
            pltpu.VMEM(tall.shape, F32),
            pltpu.VMEM(squeeze.shape, BF16),
            pltpu.SemaphoreType.DMA((count,)),
            pltpu.SemaphoreType.DMA((count,)),
        ],
        cost_estimate=pl.CostEstimate(
            flops=8 * cols * rank * unknowns,
            bytes_accessed=tall.size * 4 + squeeze.size * 2,
            transcendentals=0,
        ),
        compiler_params=pltpu.CompilerParams(vmem_limit_bytes=HEAD * 2**18),
    )(tall, squeeze)


def load_kernel(begin, f_in, o_ref, sem):
    copy = pltpu.make_async_copy(f_in.at[begin : begin + o_ref.shape[0]], o_ref, sem)
    copy.start()
    copy.wait()


def load(sections, begin, end, limit):
    shape = (end - begin,) + sections.shape[1:]
    return pl.pallas_call(
        functools.partial(load_kernel, begin),
        in_specs=[pl.BlockSpec(memory_space=pltpu.HBM)],
        out_specs=VM,
        out_shape=jax.ShapeDtypeStruct(shape, BF16),
        scratch_shapes=[pltpu.SemaphoreType.DMA],
        cost_estimate=pl.CostEstimate(
            flops=0, bytes_accessed=2 * sections.size, transcendentals=0
        ),
        compiler_params=pltpu.CompilerParams(vmem_limit_bytes=limit * 2**18),
    )(sections)


def pick_kernel(leaf, info, vb_ref, *outs):
    for at, o_ref in enumerate(outs):
        o_ref[...] = piece(vb_ref, info, info[8 + at], leaf)


def basis_kernel(leaf, v_ref, high_ref, low_ref, p_ref):
    cols = v_ref.shape[0]
    for row in range(v_ref.shape[1]):
        of, part = divmod(row, 2)
        place = (slice(part * cols, (part + 1) * cols), slice(of * leaf, (of + 1) * leaf))
        high, low = split(v_ref[:, row])
        high_ref[place] = high
        low_ref[place] = low
    high = high_ref[...]
    cross = lax.dot_general(high, low_ref[...], NT, preferred_element_type=F32)
    s = lax.dot_general(high, high, NT, preferred_element_type=F32) + cross + cross.T
    p_ref[...] = packed(s, cols)


def packed(s, cols):
    below = lax.broadcasted_iota(jnp.int32, (cols, cols), 0) >= lax.broadcasted_iota(
        jnp.int32, (cols, cols), 1
    )
    re = s[:cols, :cols] + s[cols:, cols:]
    return jnp.where(below, re, s[cols:, :cols] - s[:cols, cols:])


def own_kernel(level, adjoint, s_ref, f_ref, o_ref):
    rows = o_ref.shape[0]
    product = adj if adjoint else mul
    o_ref[...] = product(s_ref[:rows], f_ref[level, 0, 0], f_ref[level, 0, 1])


def up_kernel(level, own_ref, r_ref, f_ref, *rest):
    rows = own_ref.shape[0]
    o_ref = rest[-1]
    state = own_ref[...] + mul(r_ref[:rows], f_ref[level, 1, 0], f_ref[level, 1, 1])
    o_ref[:rows] = state.astype(BF16)
    if len(rest) > 1:
        o_ref[rows:] = rest[0][...]


def leaves_kernel(leaf, adjoint, x_ref, b_ref, o_ref):
    product = adj if adjoint else mul
    for at in range(b_ref.shape[1]):
        cut = slice(at * leaf, (at + 1) * leaf)
        o_ref[:, cut] = product(x_ref[:, cut], b_ref[0, at], b_ref[1, at])


def sides_kernel(leaf, info, near_ref, ra_ref, rb_ref, rc_ref, rd_ref, b_ref, o_ref):
    rows = near_ref.shape[0]
    o_ref[...] = near_ref[...]
    for at, ref in enumerate((ra_ref, rb_ref, rc_ref, rd_ref)):
        side = info[8 + at]
        x = ref[ref.shape[0] - rows :]
        term = mul(x, b_ref[side, 0], b_ref[side, 1])

        @pl.when(info[12 + at] == 1)
        def _():
            for e in range(2):
                o_ref[:, leaf_at(info[2 * side + e], leaf)] += term[:, e * leaf : (e + 1) * leaf]


def field_kernel(level, own_ref, r_ref, f_ref, near_ref, e_ref, y_ref, yb_ref, g_ref, m_ref):
    rows = own_ref.shape[0]
    state = own_ref[...] + mul(r_ref[:rows], f_ref[level, 1, 0], f_ref[level, 1, 1])
    y = near_ref[...] + mul(state.astype(BF16), e_ref[0], e_ref[1])
    y_ref[...] = y
    yb = y.astype(BF16)
    yb_ref[...] = yb
    g = adj(yb, e_ref[0], e_ref[1]).astype(BF16)
    g_ref[...] = g
    m_ref[...] = adj(g, f_ref[level, 1, 0], f_ref[level, 1, 1]).astype(BF16)


def shape_kernel(leaf, y_ref, o_ref):
    cols = o_ref.shape[0]
    for row in range(o_ref.shape[1]):
        of, part = divmod(row, 2)
        o_ref[:, row] = y_ref[part * cols : (part + 1) * cols, of * leaf : (of + 1) * leaf]


def terms_kernel(leaf, info, yb_ref, b_ref, *outs):
    for at, o_ref in enumerate(outs):
        side = info[8 + at]
        x = piece(yb_ref, info, side, leaf)
        o_ref[...] = adj(x, b_ref[side, 0], b_ref[side, 1]).astype(BF16)


def down_kernel(level, own_ref, r_ref, f_ref, *rest):
    rows = own_ref.shape[0]
    g_ref, m_ref = rest[-2:]
    g = (own_ref[...] + r_ref[:rows].astype(F32)).astype(BF16)
    g_ref[...] = g
    m_ref[:rows] = adj(g, f_ref[level, 1, 0], f_ref[level, 1, 1]).astype(BF16)
    if len(rest) > 2:
        m_ref[rows:] = rest[0][...]


def gather_kernel(leaf, info, near_ref, ra_ref, rb_ref, rc_ref, rd_ref, o_ref):
    rows = near_ref.shape[0]
    o_ref[...] = near_ref[...]
    for at, ref in enumerate((ra_ref, rb_ref, rc_ref, rd_ref)):
        side = info[8 + at]
        low = ref.shape[0] - rows

        @pl.when(info[12 + at] == 1)
        def _():
            for e in range(2):
                o_ref[:, leaf_at(info[2 * side + e], leaf)] += ref[
                    low:, e * leaf : (e + 1) * leaf
                ].astype(F32)


def close_kernel(near_ref, own_ref, r_ref, c_ref, vh_ref, vl_ref, vv_ref, zh_ref, zl_ref, p_ref):
    rows = own_ref.shape[0]
    cols = rows // 2
    g = (own_ref[...] + r_ref[...].astype(F32)).astype(BF16)
    high, low = split(near_ref[...] + adj(g, c_ref[0], c_ref[1]))
    zh_ref[...] = high
    zl_ref[...] = low
    many = jnp.concatenate([high, low, vh_ref[...], vl_ref[...]], 0)
    s = lax.dot_general(high, many, NT, preferred_element_type=F32)
    cross = s[:, rows : 2 * rows]
    zz = s[:, :rows] + cross + cross.T
    zv = s[:, 2 * rows : 3 * rows] + s[:, 3 * rows :]
    zv += lax.dot_general(low, vh_ref[...], NT, preferred_element_type=F32)
    p_ref[...] = jnp.concatenate(
        [
            packed(zz, cols),
            vv_ref[...],
            zv[:cols, :cols] + zv[cols:, cols:],
            zv[cols:, :cols] - zv[:cols, cols:],
        ],
        1,
    )


def spread_kernel(*refs):
    o_ref = refs[-1]
    total = sum(parts_of(refs[:-1]))
    for at in range(o_ref.shape[0]):
        o_ref[at] = total


def parts_of(refs):
    return [ref[at] for ref in refs for at in range(ref.shape[0])]


def exact_dot(a, b, dims=(((1,), (0,)), ((), ()))):
    return lax.dot_general(a, b, dims, preferred_element_type=F32, precision=lax.Precision.HIGHEST)


def real_form(re, im):
    return jnp.concatenate(
        [jnp.concatenate([re, im], 1), jnp.concatenate([-im, re], 1)], 0
    )


def inverse_factor(gram):
    size, step = gram.shape[0], 8
    eye = (
        lax.broadcasted_iota(jnp.int32, (size, size), 0)
        == lax.broadcasted_iota(jnp.int32, (size, size), 1)
    ).astype(F32)
    wide = jnp.concatenate([gram, eye], 1)
    width = wide.shape[1]
    blocks = [wide[step * j : step * (j + 1)] for j in range(size // step)]
    sub = lax.broadcasted_iota(jnp.int32, (step, width), 0)
    done = []
    for at in range(size // step):
        left = [
            [jnp.broadcast_to(b[:, at * step + p : at * step + p + 1], (step, width)) for b in blocks[at:]]
            for p in range(step)
        ]
        pivot = [
            [jnp.broadcast_to(left[q][0][p : p + 1], (step, width)) for q in range(p + 1)]
            for p in range(step)
        ]
        lines = [jnp.broadcast_to(blocks[at][p : p + 1], (step, width)) for p in range(step)]
        result = jnp.zeros((step, width), F32)
        updates = [None] * len(left[0])
        for p in range(step):
            inverse = 1.0 / pivot[p][p]
            result = jnp.where(sub == p, lines[p] * lax.rsqrt(pivot[p][p]), result)
            scaled = lines[p] * inverse
            for q in range(p + 1, step):
                ratio = pivot[q][p] * inverse
                lines[q] = lines[q] - ratio * lines[p]
                for r in range(p + 1, q + 1):
                    pivot[q][r] = pivot[q][r] - ratio * pivot[r][p]
                for i in range(1, len(left[q])):
                    left[q][i] = left[q][i] - ratio * left[p][i]
            for i in range(1, len(updates)):
                term = left[p][i] * scaled
                updates[i] = term if p == 0 else updates[i] + term
        done.append(result)
        for i in range(1, len(updates)):
            blocks[at + i] = blocks[at + i] - updates[i]
    return jnp.concatenate(done, 0)[:, size:]


def finish_kernel(leaf, total, p_ref, zh_ref, zl_ref, vh_ref, vl_ref, o_ref, buffer, sems):
    p = sum(parts_of([p_ref])) * (1.0 / total)
    cols = p.shape[0]
    lower = lax.broadcasted_iota(jnp.int32, (cols, cols), 0)
    upper = lax.broadcasted_iota(jnp.int32, (cols, cols), 1)

    def hermitian(t):
        turned = t.T
        re = jnp.where(lower >= upper, t, turned)
        im = jnp.where(lower < upper, t, jnp.where(lower > upper, -turned, 0.0))
        return real_form(re, im)

    zz = hermitian(p[:, :cols])
    vv = hermitian(p[:, cols : 2 * cols])
    h = real_form(p[:, 2 * cols : 3 * cols], p[:, 3 * cols :])
    nt = (((1,), (1,)), ((), ()))
    middle = exact_dot(h, vv) - 2.0 * h
    gram = zz + exact_dot(middle, h, nt)
    inverse = inverse_factor(gram)
    w = exact_dot(inverse, h)
    l1, l2 = inverse[:, :cols], inverse[:, cols:]
    w1, w2 = w[:, :cols], w[:, cols:]
    mix = jnp.concatenate(
        [
            jnp.concatenate([l1, -l2, -w1, w2], 1),
            jnp.concatenate([l2, l1, -w2, -w1], 1),
        ],
        0,
    )
    mix_high, mix_low = split(mix)
    mix = jnp.concatenate([mix_high, mix_high, mix_low], 1)
    rows = 2 * cols
    count, _, lines, _ = buffer.shape
    width = lines // 2 * leaf
    copies = []
    for at in range(count):
        cut = slice(at * width, (at + 1) * width)
        high = [zh_ref[:, cut], vh_ref[:, cut]]
        x = jnp.concatenate(high + [zl_ref[:, cut], vl_ref[:, cut]] + high, 0)
        out = jnp.dot(mix, x, preferred_element_type=F32)
        for line in range(lines):
            of, part = divmod(line, 2)
            buffer[at, :, line] = out[part * rows : (part + 1) * rows, of * leaf : (of + 1) * leaf]
        copy = pltpu.make_async_copy(
            buffer.at[at], o_ref.at[:, at * lines : (at + 1) * lines], sems.at[at]
        )
        copy.start()
        copies.append(copy)
    for copy in copies:
        copy.wait()


def per_device(v_block, edge_leaves, self_blocks, side_blocks, compress, expand, factors):
    cols = v_block.shape[0]
    unknowns = v_block.shape[4]
    leaves = self_blocks.shape[3]
    leaf = self_blocks.shape[4]
    levels = factors.shape[2]
    rank = compress.shape[4]
    rows = 2 * cols
    row_count = lax.axis_size("px")
    col_count = lax.axis_size("py")
    row_bits = row_count.bit_length() - 1
    total = 2 * unknowns * row_count * col_count
    row_at = lax.axis_index("px")
    col_at = lax.axis_index("py")
    selfs = self_blocks.reshape(self_blocks.shape[2:])
    sides = side_blocks.reshape(side_blocks.shape[2:])
    squeeze = compress.reshape(compress.shape[2:])
    spread = expand.reshape(expand.shape[2:])
    sections = factors.reshape(factors.shape[2:])
    own_leaves = lax.dynamic_slice(edge_leaves, (row_at, col_at, 0, 0), (1, 1, 4, 2)).reshape(8)
    odd_row, odd_col = row_at % 2, col_at % 2
    order = jnp.stack([1 - odd_row, odd_row, 3 - odd_col, 2 + odd_col]).astype(jnp.int32)
    inner_row = (row_at > 0) & (row_at < row_count - 1)
    inner_col = (col_at > 0) & (col_at < col_count - 1)
    inner = jnp.stack([inner_row, inner_row, inner_col, inner_col]).astype(jnp.int32)
    ones = jnp.array([1, 0, 1, 0], jnp.int32)
    info = jnp.concatenate([own_leaves, order, jnp.maximum(inner, ones)])
    tall = v_block.reshape(cols, 2, leaves, leaf).transpose(0, 2, 1, 3).reshape(cols, -1, leaf)

    def partner(x, level):
        if level < row_bits:
            return lax.ppermute(x, "px", [(i, i ^ 1 << level) for i in range(row_count)])
        bit = level - row_bits
        return lax.ppermute(x, "py", [(i, i ^ 1 << bit) for i in range(col_count)])

    def beyond(x, axis, count):
        pairs = [(i, (i + 1) % count) for i in range(1, count, 2)]
        return lax.ppermute(x, axis, pairs + [(j, i) for i, j in pairs])

    small = ((rows, rank), BF16)
    double = ((2 * rows, rank), BF16)
    wide = ((rows, rank), F32)
    step_flops = 8 * cols * rank * rank
    patch_flops = 8 * cols * rank * unknowns
    leaf_flops = 8 * cols * leaf * unknowns

    half, sent = head(leaf, tall, squeeze)
    early = 3
    first = load(sections, 0, early, EARLY)
    rest = load(sections, early, levels, LATE)

    def weights(level):
        return (first, level) if level < early else (rest, level - early)

    got = {}
    for level in range(levels):
        arrived = partner(sent, level)
        after = []
        if level == 1:
            pieces = call(
                functools.partial(pick_kernel, leaf), [small] * 4, [info, half], 0, smem=1, after=[sent]
            )
            after = list(pieces) + [rest]
        if level == 2:
            (near,) = call(
                functools.partial(leaves_kernel, leaf, False),
                [((rows, unknowns), F32)],
                [half, selfs],
                leaf_flops,
                after=[sent],
            )
            after = [near]
            got["a"] = partner(pieces[0], 0)
        if level == 3:
            after = [got["a"]]
        if level == row_bits:
            got["c"] = arrived
            got["b"] = beyond(pieces[1], "px", row_count)
            got["d"] = beyond(pieces[3], "py", col_count)
        if level == levels - 1:
            (near,) = call(
                functools.partial(sides_kernel, leaf),
                [((rows, unknowns), F32)],
                [info, near, got["a"], got["b"], got["c"], got["d"], sides],
                4 * step_flops,
                smem=1,
                after=[sent],
            )
            after = [near, spread]
        f, at = weights(level)
        (own,) = call(
            functools.partial(own_kernel, at, False),
            [wide],
            [sent, f],
            step_flops,
            after=after,
        )
        if level < levels - 1:
            extra = [pieces[2]] if level == row_bits - 1 else []
            (sent,) = call(
                functools.partial(up_kernel, at),
                [double if extra else small],
                [own, arrived, f] + extra,
                step_flops,
            )
    y, yb, g, message = call(
        functools.partial(field_kernel, at),
        [((rows, unknowns), F32), ((rows, unknowns), BF16), small, small],
        [own, arrived, f, near, spread],
        2 * patch_flops,
    )
    terms = call(
        functools.partial(terms_kernel, leaf), [small] * 4, [info, yb, sides], 4 * step_flops, smem=1
    )
    (shaped,) = call(
        functools.partial(shape_kernel, leaf), [((cols, 2 * leaves, leaf), F32)], [y], 0
    )
    for level in range(levels - 1, -1, -1):
        arrived = partner(message, level)
        after = []
        if level == levels - 1:
            after = list(terms)
        if level == levels - 2:
            (z_near,) = call(
                functools.partial(leaves_kernel, leaf, True),
                [((rows, unknowns), F32)],
                [yb, selfs],
                leaf_flops,
                after=[message],
            )
            after = [z_near]
        if level == row_bits:
            got["c"] = arrived
        if level == 4:
            v_high, v_low, vv = call(
                functools.partial(basis_kernel, leaf),
                [((rows, unknowns), BF16), ((rows, unknowns), BF16), ((cols, cols), F32)],
                [tall],
                leaf_flops,
                after=[message],
            )
            after = [v_high, v_low, vv]
        if level == 3:
            got["d"] = beyond(terms[3], "py", col_count)
        if level == 2:
            after = [got["d"]]
            got["a"] = partner(terms[0], 0)
        if level == 1:
            after = [got["a"], squeeze]
            got["b"] = beyond(terms[1], "px", row_count)
        if level == 0:
            (z_near,) = call(
                functools.partial(gather_kernel, leaf),
                [((rows, unknowns), F32)],
                [info, z_near, got["a"], got["b"], got["c"], got["d"]],
                0,
                smem=1,
            )
            after = [z_near]
        f, at = weights(level)
        (own,) = call(
            functools.partial(own_kernel, at, True),
            [wide],
            [g, f],
            step_flops,
            after=after,
        )
        if level > 0:
            extra = [terms[2]] if level == row_bits + 1 else []
            f, at = weights(level - 1)
            g, message = call(
                functools.partial(down_kernel, at),
                [small, double if extra else small],
                [own, arrived, f] + extra,
                step_flops,
            )
    z_high, z_low, part = call(
        close_kernel,
        [((rows, unknowns), BF16), ((rows, unknowns), BF16), ((cols, 4 * cols), F32)],
        [z_near, own, arrived, squeeze, v_high, v_low, vv],
        patch_flops,
    )
    part = part.reshape(1, cols, 4 * cols)
    chips = row_count // 2
    (part,) = call(
        spread_kernel, [((chips, cols, 4 * cols), F32)], [part, partner(part, 0)], 0
    )
    groups = [[2 * i + core for i in range(chips)] for core in range(2)]
    part = lax.all_to_all(part, "px", 0, 0, axis_index_groups=groups, tiled=True)
    (part,) = call(spread_kernel, [((col_count, cols, 4 * cols), F32)], [part], 0)
    part = lax.all_to_all(part, "py", 0, 0, tiled=True)
    lines = 8
    (basis,) = call(
        functools.partial(finish_kernel, leaf, total),
        [((rows, 2 * leaves, leaf), F32)],
        [part, z_high, z_low, v_high, v_low],
        8 * rows * rows * unknowns,
        out_spec=pl.BlockSpec(memory_space=pl.ANY),
        scratch=[
            pltpu.VMEM((2 * leaves // lines, rows, lines, leaf), F32),
            pltpu.SemaphoreType.DMA((2 * leaves // lines,)),
        ],
    )

    def patch_form(a):
        count = a.shape[0]
        a = a.reshape(count, leaves, 2, leaf).transpose(0, 2, 1, 3)
        return a.reshape(count, 1, 1, 2, unknowns)

    return patch_form(shaped), patch_form(basis)


def solution(mesh):
    in_specs = (
        P(None, "px", "py", None, None),
        P(),
        P("px", "py", None, None, None, None),
        P("px", "py", None, None, None, None),
        P("px", "py", None, None, None),
        P("px", "py", None, None, None),
        P("px", "py", None, None, None, None, None),
    )
    out_specs = (P(None, "px", "py", None, None), P(None, "px", "py", None, None))
    return jax.shard_map(
        per_device, mesh=mesh, in_specs=in_specs, out_specs=out_specs, check_vma=False
    )
```

```python
import functools
import math

import jax
import jax.numpy as jnp
from jax import lax
from jax.experimental import pallas as pl
from jax.experimental.pallas import tpu as pltpu
from jax.sharding import PartitionSpec as P

F32 = jnp.float32
BF16 = jnp.bfloat16
NT = (((1,), (1,)), ((), ()))
VM = pl.BlockSpec(memory_space=pltpu.VMEM)
SM = pl.BlockSpec(memory_space=pltpu.SMEM)

HEAD, EARLY, LATE, OTHER = 214, 200, 188, 180


def call(kernel, outs, args, flops, smem=0, limit=24, after=(), out_spec=VM, scratch=()):
    size = sum(a.size * a.dtype.itemsize for a in args)
    args = list(args) + list(after)
    count, extra = len(args), len(after)

    def body(*refs):
        kernel(*refs[: count - extra], *refs[count:])

    return pl.pallas_call(
        body,
        out_shape=[jax.ShapeDtypeStruct(s, d) for s, d in outs],
        in_specs=[SM] * smem + [VM] * (count - smem),
        out_specs=[out_spec] * len(outs),
        scratch_shapes=list(scratch),
        cost_estimate=pl.CostEstimate(flops=flops, bytes_accessed=size, transcendentals=0),
        compiler_params=pltpu.CompilerParams(vmem_limit_bytes=limit * 2**20),
    )(*args)


def mul(x, gr, gi):
    h = x.shape[0] // 2
    re, im = x[:h], x[h:]
    first = jnp.dot(x, gr, preferred_element_type=F32)
    second = jnp.dot(jnp.concatenate([-im, re], 0), gi, preferred_element_type=F32)
    return first + second


def adj(x, gr, gi):
    h = x.shape[0] // 2
    re, im = x[:h], x[h:]
    first = lax.dot_general(x, gr, NT, preferred_element_type=F32)
    second = lax.dot_general(jnp.concatenate([im, -re], 0), gi, NT, preferred_element_type=F32)
    return first + second


def leaf_at(at, leaf):
    return pl.ds(pl.multiple_of(at * leaf, leaf), leaf)


def split(x):
    high = x.astype(BF16)
    return high, (x - high.astype(F32)).astype(BF16)


def piece(ref, info, side, leaf):
    return jnp.concatenate(
        [ref[:, leaf_at(info[2 * side + e], leaf)] for e in range(2)], 1
    )


def head_kernel(leaf, v_in, c_in, vb_ref, m_ref, v_ref, c_ref, v_sems, c_sems):
    cols, lines, _ = v_ref.shape
    count = v_sems.shape[0]
    step = lines // count
    width = step // 2 * leaf
    copies = []
    for at in range(count):
        some = slice(at * step, (at + 1) * step)
        cut = slice(at * width, (at + 1) * width)
        pair = [
            pltpu.make_async_copy(v_in.at[:, some], v_ref.at[:, some], v_sems.at[at]),
            pltpu.make_async_copy(c_in.at[:, cut], c_ref.at[:, cut], c_sems.at[at]),
        ]
        for copy in pair:
            copy.start()
        copies.append(pair)
    total = None
    for at in range(count):
        copies[at][0].wait()
        for row in range(at * step, (at + 1) * step):
            of, part = divmod(row, 2)
            vb_ref[part * cols : (part + 1) * cols, of * leaf : (of + 1) * leaf] = v_ref[
                :, row
            ].astype(BF16)
        copies[at][1].wait()
        cut = slice(at * width, (at + 1) * width)
        product = mul(vb_ref[:, cut], c_ref[0, cut], c_ref[1, cut])
        total = product if total is None else total + product
    m_ref[...] = total.astype(BF16)


def head(leaf, tall, squeeze):
    cols = tall.shape[0]
    unknowns, rank = squeeze.shape[1:]
    count = 4
    return pl.pallas_call(
        functools.partial(head_kernel, leaf),
        in_specs=[pl.BlockSpec(memory_space=pltpu.HBM)] * 2,
        out_specs=[VM] * 2,
        out_shape=[
            jax.ShapeDtypeStruct((2 * cols, unknowns), BF16),
            jax.ShapeDtypeStruct((2 * cols, rank), BF16),
        ],
        scratch_shapes=[
            pltpu.VMEM(tall.shape, F32),
            pltpu.VMEM(squeeze.shape, BF16),
            pltpu.SemaphoreType.DMA((count,)),
            pltpu.SemaphoreType.DMA((count,)),
        ],
        cost_estimate=pl.CostEstimate(
            flops=8 * cols * rank * unknowns,
            bytes_accessed=tall.size * 4 + squeeze.size * 2,
            transcendentals=0,
        ),
        compiler_params=pltpu.CompilerParams(vmem_limit_bytes=HEAD * 2**18),
    )(tall, squeeze)


def load_kernel(begin, f_in, *rest):
    o_ref, sem = rest[-2:]
    copy = pltpu.make_async_copy(f_in.at[begin : begin + o_ref.shape[0]], o_ref, sem)
    copy.start()
    copy.wait()


def load(sections, begin, end, limit, after=()):
    shape = (end - begin,) + sections.shape[1:]
    return pl.pallas_call(
        functools.partial(load_kernel, begin),
        in_specs=[pl.BlockSpec(memory_space=pltpu.HBM)] + [VM] * len(after),
        out_specs=VM,
        out_shape=jax.ShapeDtypeStruct(shape, BF16),
        scratch_shapes=[pltpu.SemaphoreType.DMA],
        cost_estimate=pl.CostEstimate(
            flops=0, bytes_accessed=2 * math.prod(shape), transcendentals=0
        ),
        compiler_params=pltpu.CompilerParams(vmem_limit_bytes=limit * 2**18),
    )(sections, *after)


def pick_kernel(leaf, info, vb_ref, *outs):
    for at, o_ref in enumerate(outs):
        o_ref[...] = piece(vb_ref, info, info[8 + at], leaf)


def basis_kernel(leaf, v_ref, high_ref, low_ref, p_ref):
    cols = v_ref.shape[0]
    for row in range(v_ref.shape[1]):
        of, part = divmod(row, 2)
        place = (slice(part * cols, (part + 1) * cols), slice(of * leaf, (of + 1) * leaf))
        high, low = split(v_ref[:, row])
        high_ref[place] = high
        low_ref[place] = low
    high = high_ref[...]
    cross = lax.dot_general(high, low_ref[...], NT, preferred_element_type=F32)
    s = lax.dot_general(high, high, NT, preferred_element_type=F32) + cross + cross.T
    p_ref[...] = packed(s, cols)


def packed(s, cols):
    below = lax.broadcasted_iota(jnp.int32, (cols, cols), 0) >= lax.broadcasted_iota(
        jnp.int32, (cols, cols), 1
    )
    re = s[:cols, :cols] + s[cols:, cols:]
    return jnp.where(below, re, s[cols:, :cols] - s[:cols, cols:])


def own_kernel(at, adjoint, s_ref, f_ref, *rest):
    o_ref = rest[-1]
    rows = o_ref.shape[0] // len(rest)
    product = adj if adjoint else mul
    for part, f in enumerate((f_ref,) + rest[:-1]):
        cut = slice(part * rows, (part + 1) * rows)
        o_ref[cut] = product(s_ref[cut], f[at, 0, 0], f[at, 0, 1])


def up_kernel(at, count, extra, own_ref, r_ref, *rest):
    rows = own_ref.shape[0] // count
    outs = rest[count + extra :]
    for piece_ref in rest[count : count + extra]:
        outs[0][count * rows :] = piece_ref[...]
    for part, f in enumerate(rest[:count]):
        cut = slice(part * rows, (part + 1) * rows)
        state = own_ref[cut] + mul(r_ref[cut], f[at, 1, 0], f[at, 1, 1])
        if len(outs) > 1:
            outs[part][...] = state.astype(BF16)
        else:
            outs[0][cut] = state.astype(BF16)


def join_kernel(a_ref, b_ref, o_ref):
    rows = a_ref.shape[0]
    o_ref[:rows] = a_ref[...]
    o_ref[rows:] = b_ref[...]


def leaves_kernel(leaf, adjoint, x_ref, b_ref, o_ref):
    product = adj if adjoint else mul
    for at in range(b_ref.shape[1]):
        cut = slice(at * leaf, (at + 1) * leaf)
        o_ref[:, cut] = product(x_ref[:, cut], b_ref[0, at], b_ref[1, at])


def sides_kernel(leaf, info, near_ref, ra_ref, rb_ref, rc_ref, rd_ref, b_ref, o_ref):
    rows = near_ref.shape[0]
    o_ref[...] = near_ref[...]
    for at, ref in enumerate((ra_ref, rb_ref, rc_ref, rd_ref)):
        side = info[8 + at]
        term = mul(ref[ref.shape[0] - rows :], b_ref[side, 0], b_ref[side, 1])

        @pl.when(info[13 + at] == 1)
        def _():
            for e in range(2):
                o_ref[:, leaf_at(info[2 * side + e], leaf)] += term[:, e * leaf : (e + 1) * leaf]


def field_kernel(info, mine_ref, sent_ref, near_ref, e_ref, y_ref, yb_ref, g_ref, state_ref):
    chosen(info, mine_ref, sent_ref, state_ref)
    y = near_ref[...] + mul(state_ref[...], e_ref[0], e_ref[1])
    y_ref[...] = y
    yb = y.astype(BF16)
    yb_ref[...] = yb
    g_ref[...] = adj(yb, e_ref[0], e_ref[1]).astype(BF16)


def chosen(info, mine_ref, sent_ref, o_ref):
    @pl.when(info[12] == 1)
    def _():
        o_ref[...] = mine_ref[...]

    @pl.when(info[12] == 0)
    def _():
        o_ref[...] = sent_ref[...]


def shape_kernel(leaf, y_ref, o_ref):
    cols = o_ref.shape[0]
    for row in range(o_ref.shape[1]):
        of, part = divmod(row, 2)
        o_ref[:, row] = y_ref[part * cols : (part + 1) * cols, of * leaf : (of + 1) * leaf]


def terms_kernel(leaf, info, yb_ref, b_ref, *outs):
    for at, o_ref in enumerate(outs):
        side = info[8 + at]
        x = piece(yb_ref, info, side, leaf)
        o_ref[...] = adj(x, b_ref[side, 0], b_ref[side, 1]).astype(BF16)


def turn_kernel(at, a_ref, b_ref, f_ref, fo_ref, g_ref, m_ref):
    rows = a_ref.shape[0]
    for part, (x, f) in enumerate(((a_ref, f_ref), (b_ref, fo_ref))):
        cut = slice(part * rows, (part + 1) * rows)
        g_ref[cut] = x[...]
        m_ref[cut] = adj(x[...], f[at, 1, 0], f[at, 1, 1]).astype(BF16)


def down_kernel(at, own_ref, r_ref, f_ref, fo_ref, *rest):
    rows = own_ref.shape[0] // 2
    g_ref, m_ref = rest[-2:]
    if len(rest) > 2:
        m_ref[2 * rows :] = rest[0][...]
    for part, f in enumerate((f_ref, fo_ref)):
        cut = slice(part * rows, (part + 1) * rows)
        g = (own_ref[cut] + r_ref[cut].astype(F32)).astype(BF16)
        g_ref[cut] = g
        m_ref[cut] = adj(g, f[at, 1, 0], f[at, 1, 1]).astype(BF16)


def last_kernel(own_ref, r_ref, f_ref, fo_ref, mine_ref, other_ref):
    rows = mine_ref.shape[0]
    a, b = [
        (own_ref[cut] + r_ref[cut].astype(F32)).astype(BF16)
        for cut in (slice(0, rows), slice(rows, 2 * rows))
    ]
    for x, f, y, h, o_ref in ((a, f_ref, b, fo_ref, mine_ref), (b, fo_ref, a, f_ref, other_ref)):
        message = adj(y, h[0, 1, 0], h[0, 1, 1]).astype(BF16).astype(F32)
        o_ref[...] = (adj(x, f[0, 0, 0], f[0, 0, 1]) + message).astype(BF16)


def gather_kernel(leaf, info, near_ref, ra_ref, rb_ref, rc_ref, rd_ref, o_ref):
    rows = near_ref.shape[0]
    o_ref[...] = near_ref[...]
    for at, ref in enumerate((ra_ref, rb_ref, rc_ref, rd_ref)):
        side = info[8 + at]
        low = ref.shape[0] - rows

        @pl.when(info[13 + at] == 1)
        def _():
            for e in range(2):
                o_ref[:, leaf_at(info[2 * side + e], leaf)] += ref[
                    low:, e * leaf : (e + 1) * leaf
                ].astype(F32)


def close_kernel(
    info, near_ref, mine_ref, sent_ref, c_ref, vh_ref, vl_ref, vv_ref, zh_ref, zl_ref, p_ref, g_ref
):
    rows = mine_ref.shape[0]
    cols = rows // 2
    chosen(info, mine_ref, sent_ref, g_ref)
    high, low = split(near_ref[...] + adj(g_ref[...], c_ref[0], c_ref[1]))
    zh_ref[...] = high
    zl_ref[...] = low
    many = jnp.concatenate([high, low, vh_ref[...], vl_ref[...]], 0)
    s = lax.dot_general(high, many, NT, preferred_element_type=F32)
    cross = s[:, rows : 2 * rows]
    zz = s[:, :rows] + cross + cross.T
    zv = s[:, 2 * rows : 3 * rows] + s[:, 3 * rows :]
    zv += lax.dot_general(low, vh_ref[...], NT, preferred_element_type=F32)
    p_ref[...] = jnp.concatenate(
        [
            packed(zz, cols),
            vv_ref[...],
            zv[:cols, :cols] + zv[cols:, cols:],
            zv[cols:, :cols] - zv[:cols, cols:],
        ],
        1,
    )


def spread_kernel(*refs):
    o_ref = refs[-1]
    total = sum(parts_of(refs[:-1]))
    for at in range(o_ref.shape[0]):
        o_ref[at] = total


def parts_of(refs):
    return [ref[at] for ref in refs for at in range(ref.shape[0])]


def exact_dot(a, b, dims=(((1,), (0,)), ((), ()))):
    return lax.dot_general(a, b, dims, preferred_element_type=F32, precision=lax.Precision.HIGHEST)


def real_form(re, im):
    return jnp.concatenate(
        [jnp.concatenate([re, im], 1), jnp.concatenate([-im, re], 1)], 0
    )


def inverse_factor(gram):
    size, step = gram.shape[0], 8
    eye = (
        lax.broadcasted_iota(jnp.int32, (size, size), 0)
        == lax.broadcasted_iota(jnp.int32, (size, size), 1)
    ).astype(F32)
    wide = jnp.concatenate([gram, eye], 1)
    width = wide.shape[1]
    blocks = [wide[step * j : step * (j + 1)] for j in range(size // step)]
    sub = lax.broadcasted_iota(jnp.int32, (step, width), 0)
    done = []
    for at in range(size // step):
        left = [
            [jnp.broadcast_to(b[:, at * step + p : at * step + p + 1], (step, width)) for b in blocks[at:]]
            for p in range(step)
        ]
        pivot = [
            [jnp.broadcast_to(left[q][0][p : p + 1], (step, width)) for q in range(p + 1)]
            for p in range(step)
        ]
        lines = [jnp.broadcast_to(blocks[at][p : p + 1], (step, width)) for p in range(step)]
        result = jnp.zeros((step, width), F32)
        updates = [None] * len(left[0])
        for p in range(step):
            inverse = 1.0 / pivot[p][p]
            result = jnp.where(sub == p, lines[p] * lax.rsqrt(pivot[p][p]), result)
            scaled = lines[p] * inverse
            for q in range(p + 1, step):
                ratio = pivot[q][p] * inverse
                lines[q] = lines[q] - ratio * lines[p]
                for r in range(p + 1, q + 1):
                    pivot[q][r] = pivot[q][r] - ratio * pivot[r][p]
                for i in range(1, len(left[q])):
                    left[q][i] = left[q][i] - ratio * left[p][i]
            for i in range(1, len(updates)):
                term = left[p][i] * scaled
                updates[i] = term if p == 0 else updates[i] + term
        done.append(result)
        for i in range(1, len(updates)):
            blocks[at + i] = blocks[at + i] - updates[i]
    return jnp.concatenate(done, 0)[:, size:]


def finish_kernel(leaf, total, p_ref, zh_ref, zl_ref, vh_ref, vl_ref, o_ref, buffer, sems):
    p = sum(parts_of([p_ref])) * (1.0 / total)
    cols = p.shape[0]
    lower = lax.broadcasted_iota(jnp.int32, (cols, cols), 0)
    upper = lax.broadcasted_iota(jnp.int32, (cols, cols), 1)

    def hermitian(t):
        turned = t.T
        re = jnp.where(lower >= upper, t, turned)
        im = jnp.where(lower < upper, t, jnp.where(lower > upper, -turned, 0.0))
        return real_form(re, im)

    zz = hermitian(p[:, :cols])
    vv = hermitian(p[:, cols : 2 * cols])
    h = real_form(p[:, 2 * cols : 3 * cols], p[:, 3 * cols :])
    nt = (((1,), (1,)), ((), ()))
    middle = exact_dot(h, vv) - 2.0 * h
    gram = zz + exact_dot(middle, h, nt)
    inverse = inverse_factor(gram)
    w = exact_dot(inverse, h)
    l1, l2 = inverse[:, :cols], inverse[:, cols:]
    w1, w2 = w[:, :cols], w[:, cols:]
    mix = jnp.concatenate(
        [
            jnp.concatenate([l1, -l2, -w1, w2], 1),
            jnp.concatenate([l2, l1, -w2, -w1], 1),
        ],
        0,
    )
    mix_high, mix_low = split(mix)
    mix = jnp.concatenate([mix_high, mix_high, mix_low], 1)
    rows = 2 * cols
    count, _, lines, _ = buffer.shape
    width = lines // 2 * leaf
    copies = []
    for at in range(count):
        cut = slice(at * width, (at + 1) * width)
        high = [zh_ref[:, cut], vh_ref[:, cut]]
        x = jnp.concatenate(high + [zl_ref[:, cut], vl_ref[:, cut]] + high, 0)
        out = jnp.dot(mix, x, preferred_element_type=F32)
        for line in range(lines):
            of, part = divmod(line, 2)
            buffer[at, :, line] = out[part * rows : (part + 1) * rows, of * leaf : (of + 1) * leaf]
        copy = pltpu.make_async_copy(
            buffer.at[at], o_ref.at[:, at * lines : (at + 1) * lines], sems.at[at]
        )
        copy.start()
        copies.append(copy)
    for copy in copies:
        copy.wait()


def per_device(v_block, edge_leaves, self_blocks, side_blocks, compress, expand, factors):
    cols = v_block.shape[0]
    unknowns = v_block.shape[4]
    leaves = self_blocks.shape[3]
    leaf = self_blocks.shape[4]
    levels = factors.shape[2]
    rank = compress.shape[4]
    rows = 2 * cols
    row_count = lax.axis_size("px")
    col_count = lax.axis_size("py")
    row_bits = row_count.bit_length() - 1
    total = 2 * unknowns * row_count * col_count
    row_at = lax.axis_index("px")
    col_at = lax.axis_index("py")
    selfs = self_blocks.reshape(self_blocks.shape[2:])
    sides = side_blocks.reshape(side_blocks.shape[2:])
    squeeze = compress.reshape(compress.shape[2:])
    spread = expand.reshape(expand.shape[2:])
    sections = factors.reshape(factors.shape[2:])
    own_leaves = lax.dynamic_slice(edge_leaves, (row_at, col_at, 0, 0), (1, 1, 4, 2)).reshape(8)
    odd_row, odd_col = row_at % 2, col_at % 2
    order = jnp.stack([1 - odd_row, odd_row, 3 - odd_col, 2 + odd_col]).astype(jnp.int32)
    inner_row = (row_at > 0) & (row_at < row_count - 1)
    inner_col = (col_at > 0) & (col_at < col_count - 1)
    flags = jnp.stack([odd_row == 1, row_at >= 0, inner_row, row_at >= 0, inner_col])
    info = jnp.concatenate([own_leaves, order, flags.astype(jnp.int32)])
    tall = v_block.reshape(cols, 2, leaves, leaf).transpose(0, 2, 1, 3).reshape(cols, -1, leaf)

    def partner(x, level):
        near_bit, far_bit = (1 << level, 0) if level < row_bits else (0, 1 << level - row_bits)
        flips = [(2, 0), (near_bit, far_bit)]
        if level == row_bits:
            flips[0] = flips[1]
        pairs = [
            (i * col_count + j, (i ^ flips[i % 2][0]) * col_count + (j ^ flips[i % 2][1]))
            for i in range(row_count)
            for j in range(col_count)
        ]
        return lax.ppermute(x, ("px", "py"), pairs)

    def swapped(x, axis, count):
        return lax.ppermute(x, axis, [(i, i ^ 1) for i in range(count)])

    def over(x):
        return swapped(x, "px", row_count)

    def beyond(x, axis, count):
        pairs = [(i, (i + 1) % count) for i in range(1, count, 2)]
        return lax.ppermute(x, axis, pairs + [(j, i) for i, j in pairs])

    small = ((rows, rank), BF16)
    double = ((2 * rows, rank), BF16)
    triple = ((3 * rows, rank), BF16)
    wide = ((rows, rank), F32)
    wide_double = ((2 * rows, rank), F32)
    step_flops = 8 * cols * rank * rank
    patch_flops = 8 * cols * rank * unknowns
    leaf_flops = 8 * cols * leaf * unknowns

    half, sent = head(leaf, tall, squeeze)
    bounds = [0, 1, 3, levels]
    sections_sent = over(sections)
    zero = load(sections, 0, 1, EARLY, [sent])
    arrived = swapped(sent, "px", row_count)
    (own,) = call(functools.partial(own_kernel, 0, False), [wide], [sent, zero], step_flops)
    (sent,) = call(functools.partial(up_kernel, 0, 1, 0), [small], [own, arrived, zero], step_flops)
    first = load(sections, 1, 3, EARLY, [sent])
    other = over(sent)
    (sent,) = call(join_kernel, [double], [sent, other], 0, after=[first])
    held = {0: zero, 1: first}
    held_other = {}

    def weights(level):
        at = sum(level >= low for low in bounds[1:-1])
        for now, array, limit in ((held, sections, LATE), (held_other, sections_sent, OTHER)):
            if at not in now:
                now[at] = load(array, bounds[at], bounds[at + 1], limit, [sent])
        return [held[at], held_other[at]], level - bounds[at]

    got = {}
    for level in range(1, levels):
        arrived = partner(sent, level)
        after, ended = [], []
        if level == 1:
            pieces = call(
                functools.partial(pick_kernel, leaf), [small] * 4, [info, half], 0, smem=1, after=[sent]
            )
            after = list(pieces)
        if level == 2:
            f, _ = weights(level + 1)
            ended = f
        if level == 3:
            (near,) = call(
                functools.partial(leaves_kernel, leaf, False),
                [((rows, unknowns), F32)],
                [half, selfs],
                leaf_flops,
                after=[sent],
            )
            after = [near]
        if level == 3:
            got["a"] = swapped(pieces[0], "px", row_count)
            ended = [got["a"]]
        if level == row_bits + 1:
            got["b"] = beyond(pieces[1], "px", row_count)
            got["d"] = beyond(pieces[3], "py", col_count)
        if level == row_bits:
            got["c"] = arrived
        f, at = weights(level)
        (own,) = call(
            functools.partial(own_kernel, at, False),
            [wide_double],
            [sent] + f,
            2 * step_flops,
            after=after,
        )
        last = level == levels - 1
        extra = [pieces[2]] if level == row_bits - 1 else []
        outs = call(
            functools.partial(up_kernel, at, 2, len(extra)),
            [small, small] if last else [triple if extra else double],
            [own, arrived] + f + extra,
            2 * step_flops,
            after=ended,
        )
        sent = outs[0]
    mine, other = outs
    other = over(other)
    (near,) = call(
        functools.partial(sides_kernel, leaf),
        [((rows, unknowns), F32)],
        [info, near, got["a"], got["b"], got["c"], got["d"], sides],
        4 * step_flops,
        smem=1,
        after=[mine],
    )
    y, yb, g = call(
        field_kernel,
        [((rows, unknowns), F32), ((rows, unknowns), BF16), small],
        [info, mine, other, near, spread],
        2 * patch_flops,
        smem=1,
        scratch=[pltpu.VMEM((rows, rank), BF16)],
    )
    other = over(g)
    terms = call(
        functools.partial(terms_kernel, leaf), [small] * 4, [info, yb, sides], 4 * step_flops, smem=1
    )
    (shaped,) = call(
        functools.partial(shape_kernel, leaf), [((cols, 2 * leaves, leaf), F32)], [y], 0
    )
    f, at = weights(levels - 1)
    g, message = call(
        functools.partial(turn_kernel, at), [double, double], [g, other] + f, 2 * step_flops
    )
    for level in range(levels - 1, 0, -1):
        arrived = partner(message, level)
        after, ended = [], []
        if level == levels - 1:
            after = list(terms)
        if level == levels - 2:
            (z_near,) = call(
                functools.partial(leaves_kernel, leaf, True),
                [((rows, unknowns), F32)],
                [yb, selfs],
                leaf_flops,
                after=[message],
            )
            after = [z_near]
        if level == 4:
            v_high, v_low, vv = call(
                functools.partial(basis_kernel, leaf),
                [((rows, unknowns), BF16), ((rows, unknowns), BF16), ((cols, cols), F32)],
                [tall],
                leaf_flops,
                after=[message],
            )
            after = [v_high, v_low, vv]
        if level == 3:
            got["d"] = beyond(terms[3], "py", col_count)
            ended = [got["d"]]
        if level == 2:
            got["a"] = swapped(terms[0], "px", row_count)
            ended = [got["a"]]
        if level == 1:
            after = [squeeze]
            got["b"] = beyond(terms[1], "px", row_count)
        if level == row_bits:
            got["c"] = arrived
        f, at = weights(level)
        (own,) = call(
            functools.partial(own_kernel, at, True),
            [wide_double],
            [g] + f,
            2 * step_flops,
            after=after,
        )
        if level > 1:
            f, at = weights(level - 1)
            extra = [terms[2]] if level == row_bits + 1 else []
            g, message = call(
                functools.partial(down_kernel, at),
                [double, triple if extra else double],
                [own, arrived] + f + extra,
                2 * step_flops,
                after=ended,
            )
    f, at = weights(0)
    mine, other = call(
        last_kernel, [small, small], [own, arrived] + f, 4 * step_flops
    )
    other = over(other)
    (z_near,) = call(
        functools.partial(gather_kernel, leaf),
        [((rows, unknowns), F32)],
        [info, z_near, got["a"], got["b"], got["c"], got["d"]],
        0,
        smem=1,
    )
    z_high, z_low, part = call(
        close_kernel,
        [((rows, unknowns), BF16), ((rows, unknowns), BF16), ((cols, 4 * cols), F32)],
        [info, z_near, mine, other, squeeze, v_high, v_low, vv],
        patch_flops,
        smem=1,
        scratch=[pltpu.VMEM((rows, rank), BF16)],
    )
    part = part.reshape(1, cols, 4 * cols)
    chips = row_count // 2
    (part,) = call(
        spread_kernel, [((chips, cols, 4 * cols), F32)], [part, swapped(part, "px", row_count)], 0
    )
    groups = [[2 * i + core for i in range(chips)] for core in range(2)]
    part = lax.all_to_all(part, "px", 0, 0, axis_index_groups=groups, tiled=True)
    (part,) = call(spread_kernel, [((col_count, cols, 4 * cols), F32)], [part], 0)
    part = lax.all_to_all(part, "py", 0, 0, tiled=True)
    lines = 8
    (basis,) = call(
        functools.partial(finish_kernel, leaf, total),
        [((rows, 2 * leaves, leaf), F32)],
        [part, z_high, z_low, v_high, v_low],
        8 * rows * rows * unknowns,
        out_spec=pl.BlockSpec(memory_space=pl.ANY),
        scratch=[
            pltpu.VMEM((2 * leaves // lines, rows, lines, leaf), F32),
            pltpu.SemaphoreType.DMA((2 * leaves // lines,)),
        ],
    )

    def patch_form(a):
        count = a.shape[0]
        a = a.reshape(count, leaves, 2, leaf).transpose(0, 2, 1, 3)
        return a.reshape(count, 1, 1, 2, unknowns)

    return patch_form(shaped), patch_form(basis)


def solution(mesh):
    in_specs = (
        P(None, "px", "py", None, None),
        P(),
        P("px", "py", None, None, None, None),
        P("px", "py", None, None, None, None),
        P("px", "py", None, None, None),
        P("px", "py", None, None, None),
        P("px", "py", None, None, None, None, None),
    )
    out_specs = (P(None, "px", "py", None, None), P(None, "px", "py", None, None))
    return jax.shard_map(
        per_device, mesh=mesh, in_specs=in_specs, out_specs=out_specs, check_vma=False
    )
```

```python
import functools
import math

import jax
import jax.numpy as jnp
from jax import lax
from jax.experimental import pallas as pl
from jax.experimental.pallas import tpu as pltpu
from jax.sharding import PartitionSpec as P

F32 = jnp.float32
BF16 = jnp.bfloat16
NT = (((1,), (1,)), ((), ()))
VM = pl.BlockSpec(memory_space=pltpu.VMEM)
SM = pl.BlockSpec(memory_space=pltpu.SMEM)

HEAD, EARLY, LATE = 214, 200, 196


def call(kernel, outs, args, flops, smem=0, limit=24, after=(), out_spec=VM, scratch=()):
    size = sum(a.size * a.dtype.itemsize for a in args)
    args = list(args) + list(after)
    count, extra = len(args), len(after)

    def body(*refs):
        kernel(*refs[: count - extra], *refs[count:])

    return pl.pallas_call(
        body,
        out_shape=[jax.ShapeDtypeStruct(s, d) for s, d in outs],
        in_specs=[SM] * smem + [VM] * (count - smem),
        out_specs=[out_spec] * len(outs),
        scratch_shapes=list(scratch),
        cost_estimate=pl.CostEstimate(flops=flops, bytes_accessed=size, transcendentals=0),
        compiler_params=pltpu.CompilerParams(vmem_limit_bytes=limit * 2**20),
    )(*args)


def mul(x, gr, gi):
    h = x.shape[0] // 2
    re, im = x[:h], x[h:]
    first = jnp.dot(x, gr, preferred_element_type=F32)
    second = jnp.dot(jnp.concatenate([-im, re], 0), gi, preferred_element_type=F32)
    return first + second


def adj(x, gr, gi):
    h = x.shape[0] // 2
    re, im = x[:h], x[h:]
    first = lax.dot_general(x, gr, NT, preferred_element_type=F32)
    second = lax.dot_general(jnp.concatenate([im, -re], 0), gi, NT, preferred_element_type=F32)
    return first + second


def leaf_at(at, leaf):
    return pl.ds(pl.multiple_of(at * leaf, leaf), leaf)


def split(x):
    high = x.astype(BF16)
    return high, (x - high.astype(F32)).astype(BF16)


def piece(ref, info, side, leaf):
    return jnp.concatenate(
        [ref[:, leaf_at(info[2 * side + e], leaf)] for e in range(2)], 1
    )


def head_kernel(leaf, v_in, c_in, vb_ref, m_ref, v_ref, c_ref, v_sems, c_sems):
    cols, lines, _ = v_ref.shape
    count = v_sems.shape[0]
    step = lines // count
    width = step // 2 * leaf
    copies = []
    for at in range(count):
        some = slice(at * step, (at + 1) * step)
        cut = slice(at * width, (at + 1) * width)
        pair = [
            pltpu.make_async_copy(v_in.at[:, some], v_ref.at[:, some], v_sems.at[at]),
            pltpu.make_async_copy(c_in.at[:, cut], c_ref.at[:, cut], c_sems.at[at]),
        ]
        for copy in pair:
            copy.start()
        copies.append(pair)
    total = None
    for at in range(count):
        copies[at][0].wait()
        for row in range(at * step, (at + 1) * step):
            of, part = divmod(row, 2)
            vb_ref[part * cols : (part + 1) * cols, of * leaf : (of + 1) * leaf] = v_ref[
                :, row
            ].astype(BF16)
        copies[at][1].wait()
        cut = slice(at * width, (at + 1) * width)
        product = mul(vb_ref[:, cut], c_ref[0, cut], c_ref[1, cut])
        total = product if total is None else total + product
    m_ref[...] = total.astype(BF16)


def head(leaf, tall, squeeze):
    cols = tall.shape[0]
    unknowns, rank = squeeze.shape[1:]
    count = 4
    return pl.pallas_call(
        functools.partial(head_kernel, leaf),
        in_specs=[pl.BlockSpec(memory_space=pltpu.HBM)] * 2,
        out_specs=[VM] * 2,
        out_shape=[
            jax.ShapeDtypeStruct((2 * cols, unknowns), BF16),
            jax.ShapeDtypeStruct((2 * cols, rank), BF16),
        ],
        scratch_shapes=[
            pltpu.VMEM(tall.shape, F32),
            pltpu.VMEM(squeeze.shape, BF16),
            pltpu.SemaphoreType.DMA((count,)),
            pltpu.SemaphoreType.DMA((count,)),
        ],
        cost_estimate=pl.CostEstimate(
            flops=8 * cols * rank * unknowns,
            bytes_accessed=tall.size * 4 + squeeze.size * 2,
            transcendentals=0,
        ),
        compiler_params=pltpu.CompilerParams(vmem_limit_bytes=HEAD * 2**18),
    )(tall, squeeze)


def load_kernel(begin, f_in, *rest):
    o_ref, sem = rest[-2:]
    copy = pltpu.make_async_copy(f_in.at[begin : begin + o_ref.shape[0]], o_ref, sem)
    copy.start()
    copy.wait()


def load(sections, begin, end, limit, after=()):
    shape = (end - begin,) + sections.shape[1:]
    return pl.pallas_call(
        functools.partial(load_kernel, begin),
        in_specs=[pl.BlockSpec(memory_space=pltpu.HBM)] + [VM] * len(after),
        out_specs=VM,
        out_shape=jax.ShapeDtypeStruct(shape, BF16),
        scratch_shapes=[pltpu.SemaphoreType.DMA],
        cost_estimate=pl.CostEstimate(
            flops=0, bytes_accessed=2 * math.prod(shape), transcendentals=0
        ),
        compiler_params=pltpu.CompilerParams(vmem_limit_bytes=limit * 2**18),
    )(sections, *after)


def pick_kernel(leaf, info, vb_ref, *outs):
    for at, o_ref in enumerate(outs):
        o_ref[...] = piece(vb_ref, info, info[8 + at], leaf)


def basis_kernel(leaf, v_ref, high_ref, low_ref, p_ref):
    cols = v_ref.shape[0]
    for row in range(v_ref.shape[1]):
        of, part = divmod(row, 2)
        place = (slice(part * cols, (part + 1) * cols), slice(of * leaf, (of + 1) * leaf))
        high, low = split(v_ref[:, row])
        high_ref[place] = high
        low_ref[place] = low
    high = high_ref[...]
    cross = lax.dot_general(high, low_ref[...], NT, preferred_element_type=F32)
    s = lax.dot_general(high, high, NT, preferred_element_type=F32) + cross + cross.T
    p_ref[...] = packed(s, cols)


def packed(s, cols):
    below = lax.broadcasted_iota(jnp.int32, (cols, cols), 0) >= lax.broadcasted_iota(
        jnp.int32, (cols, cols), 1
    )
    re = s[:cols, :cols] + s[cols:, cols:]
    return jnp.where(below, re, s[cols:, :cols] - s[:cols, cols:])


def own_kernel(level, adjoint, s_ref, f_ref, o_ref):
    rows = o_ref.shape[0]
    product = adj if adjoint else mul
    o_ref[...] = product(s_ref[:rows], f_ref[level, 0, 0], f_ref[level, 0, 1])


def up_kernel(level, own_ref, r_ref, f_ref, *rest):
    rows = own_ref.shape[0]
    o_ref = rest[-1]
    state = own_ref[...] + mul(r_ref[:rows], f_ref[level, 1, 0], f_ref[level, 1, 1])
    o_ref[:rows] = state.astype(BF16)
    if len(rest) > 1:
        o_ref[rows:] = rest[0][...]


def leaves_kernel(leaf, adjoint, x_ref, b_ref, o_ref):
    product = adj if adjoint else mul
    for at in range(b_ref.shape[1]):
        cut = slice(at * leaf, (at + 1) * leaf)
        o_ref[:, cut] = product(x_ref[:, cut], b_ref[0, at], b_ref[1, at])


def sides_kernel(leaf, info, near_ref, ra_ref, rb_ref, rc_ref, rd_ref, b_ref, o_ref):
    rows = near_ref.shape[0]
    o_ref[...] = near_ref[...]
    for at, ref in enumerate((ra_ref, rb_ref, rc_ref, rd_ref)):
        side = info[8 + at]
        x = ref[ref.shape[0] - rows :]
        term = mul(x, b_ref[side, 0], b_ref[side, 1])

        @pl.when(info[12 + at] == 1)
        def _():
            for e in range(2):
                o_ref[:, leaf_at(info[2 * side + e], leaf)] += term[:, e * leaf : (e + 1) * leaf]


def field_kernel(level, own_ref, r_ref, f_ref, near_ref, e_ref, y_ref, yb_ref, g_ref, m_ref):
    rows = own_ref.shape[0]
    state = own_ref[...] + mul(r_ref[:rows], f_ref[level, 1, 0], f_ref[level, 1, 1])
    y = near_ref[...] + mul(state.astype(BF16), e_ref[0], e_ref[1])
    y_ref[...] = y
    yb = y.astype(BF16)
    yb_ref[...] = yb
    g = adj(yb, e_ref[0], e_ref[1]).astype(BF16)
    g_ref[...] = g
    m_ref[...] = adj(g, f_ref[level, 1, 0], f_ref[level, 1, 1]).astype(BF16)


def shape_kernel(leaf, y_ref, o_ref):
    cols = o_ref.shape[0]
    for row in range(o_ref.shape[1]):
        of, part = divmod(row, 2)
        o_ref[:, row] = y_ref[part * cols : (part + 1) * cols, of * leaf : (of + 1) * leaf]


def terms_kernel(leaf, info, yb_ref, b_ref, *outs):
    for at, o_ref in enumerate(outs):
        side = info[8 + at]
        x = piece(yb_ref, info, side, leaf)
        o_ref[...] = adj(x, b_ref[side, 0], b_ref[side, 1]).astype(BF16)


def down_kernel(level, own_ref, r_ref, f_ref, *rest):
    rows = own_ref.shape[0]
    g_ref, m_ref = rest[-2:]
    g = (own_ref[...] + r_ref[:rows].astype(F32)).astype(BF16)
    g_ref[...] = g
    m_ref[:rows] = adj(g, f_ref[level, 1, 0], f_ref[level, 1, 1]).astype(BF16)
    if len(rest) > 2:
        m_ref[rows:] = rest[0][...]


def gather_kernel(leaf, info, near_ref, ra_ref, rb_ref, rc_ref, rd_ref, o_ref):
    rows = near_ref.shape[0]
    o_ref[...] = near_ref[...]
    for at, ref in enumerate((ra_ref, rb_ref, rc_ref, rd_ref)):
        side = info[8 + at]
        low = ref.shape[0] - rows

        @pl.when(info[12 + at] == 1)
        def _():
            for e in range(2):
                o_ref[:, leaf_at(info[2 * side + e], leaf)] += ref[
                    low:, e * leaf : (e + 1) * leaf
                ].astype(F32)


def close_kernel(near_ref, own_ref, r_ref, c_ref, vh_ref, vl_ref, vv_ref, zh_ref, zl_ref, p_ref):
    rows = own_ref.shape[0]
    cols = rows // 2
    g = (own_ref[...] + r_ref[...].astype(F32)).astype(BF16)
    high, low = split(near_ref[...] + adj(g, c_ref[0], c_ref[1]))
    zh_ref[...] = high
    zl_ref[...] = low
    many = jnp.concatenate([high, low, vh_ref[...], vl_ref[...]], 0)
    s = lax.dot_general(high, many, NT, preferred_element_type=F32)
    cross = s[:, rows : 2 * rows]
    zz = s[:, :rows] + cross + cross.T
    zv = s[:, 2 * rows : 3 * rows] + s[:, 3 * rows :]
    zv += lax.dot_general(low, vh_ref[...], NT, preferred_element_type=F32)
    p_ref[...] = jnp.concatenate(
        [
            packed(zz, cols),
            vv_ref[...],
            zv[:cols, :cols] + zv[cols:, cols:],
            zv[cols:, :cols] - zv[:cols, cols:],
        ],
        1,
    )


def spread_kernel(*refs):
    o_ref = refs[-1]
    total = sum(parts_of(refs[:-1]))
    for at in range(o_ref.shape[0]):
        o_ref[at] = total


def parts_of(refs):
    return [ref[at] for ref in refs for at in range(ref.shape[0])]


def exact_dot(a, b, dims=(((1,), (0,)), ((), ()))):
    return lax.dot_general(a, b, dims, preferred_element_type=F32, precision=lax.Precision.HIGHEST)


def real_form(re, im):
    return jnp.concatenate(
        [jnp.concatenate([re, im], 1), jnp.concatenate([-im, re], 1)], 0
    )


def inverse_factor(gram):
    size, step = gram.shape[0], 8
    eye = (
        lax.broadcasted_iota(jnp.int32, (size, size), 0)
        == lax.broadcasted_iota(jnp.int32, (size, size), 1)
    ).astype(F32)
    wide = jnp.concatenate([gram, eye], 1)
    width = wide.shape[1]
    blocks = [wide[step * j : step * (j + 1)] for j in range(size // step)]
    sub = lax.broadcasted_iota(jnp.int32, (step, width), 0)
    done = []
    for at in range(size // step):
        left = [
            [jnp.broadcast_to(b[:, at * step + p : at * step + p + 1], (step, width)) for b in blocks[at:]]
            for p in range(step)
        ]
        pivot = [
            [jnp.broadcast_to(left[q][0][p : p + 1], (step, width)) for q in range(p + 1)]
            for p in range(step)
        ]
        lines = [jnp.broadcast_to(blocks[at][p : p + 1], (step, width)) for p in range(step)]
        result = jnp.zeros((step, width), F32)
        updates = [None] * len(left[0])
        for p in range(step):
            inverse = 1.0 / pivot[p][p]
            result = jnp.where(sub == p, lines[p] * lax.rsqrt(pivot[p][p]), result)
            scaled = lines[p] * inverse
            for q in range(p + 1, step):
                ratio = pivot[q][p] * inverse
                lines[q] = lines[q] - ratio * lines[p]
                for r in range(p + 1, q + 1):
                    pivot[q][r] = pivot[q][r] - ratio * pivot[r][p]
                for i in range(1, len(left[q])):
                    left[q][i] = left[q][i] - ratio * left[p][i]
            for i in range(1, len(updates)):
                term = left[p][i] * scaled
                updates[i] = term if p == 0 else updates[i] + term
        done.append(result)
        for i in range(1, len(updates)):
            blocks[at + i] = blocks[at + i] - updates[i]
    return jnp.concatenate(done, 0)[:, size:]


def finish_kernel(leaf, total, p_ref, zh_ref, zl_ref, vh_ref, vl_ref, o_ref, buffer, sems):
    p = sum(parts_of([p_ref])) * (1.0 / total)
    cols = p.shape[0]
    lower = lax.broadcasted_iota(jnp.int32, (cols, cols), 0)
    upper = lax.broadcasted_iota(jnp.int32, (cols, cols), 1)

    def hermitian(t):
        turned = t.T
        re = jnp.where(lower >= upper, t, turned)
        im = jnp.where(lower < upper, t, jnp.where(lower > upper, -turned, 0.0))
        return real_form(re, im)

    zz = hermitian(p[:, :cols])
    vv = hermitian(p[:, cols : 2 * cols])
    h = real_form(p[:, 2 * cols : 3 * cols], p[:, 3 * cols :])
    nt = (((1,), (1,)), ((), ()))
    middle = exact_dot(h, vv) - 2.0 * h
    gram = zz + exact_dot(middle, h, nt)
    inverse = inverse_factor(gram)
    w = exact_dot(inverse, h)
    l1, l2 = inverse[:, :cols], inverse[:, cols:]
    w1, w2 = w[:, :cols], w[:, cols:]
    mix = jnp.concatenate(
        [
            jnp.concatenate([l1, -l2, -w1, w2], 1),
            jnp.concatenate([l2, l1, -w2, -w1], 1),
        ],
        0,
    )
    mix_high, mix_low = split(mix)
    mix = jnp.concatenate([mix_high, mix_high, mix_low], 1)
    rows = 2 * cols
    count, _, lines, _ = buffer.shape
    width = lines // 2 * leaf
    copies = []
    for at in range(count):
        cut = slice(at * width, (at + 1) * width)
        high = [zh_ref[:, cut], vh_ref[:, cut]]
        x = jnp.concatenate(high + [zl_ref[:, cut], vl_ref[:, cut]] + high, 0)
        out = jnp.dot(mix, x, preferred_element_type=F32)
        for line in range(lines):
            of, part = divmod(line, 2)
            buffer[at, :, line] = out[part * rows : (part + 1) * rows, of * leaf : (of + 1) * leaf]
        copy = pltpu.make_async_copy(
            buffer.at[at], o_ref.at[:, at * lines : (at + 1) * lines], sems.at[at]
        )
        copy.start()
        copies.append(copy)
    for copy in copies:
        copy.wait()


def per_device(v_block, edge_leaves, self_blocks, side_blocks, compress, expand, factors):
    cols = v_block.shape[0]
    unknowns = v_block.shape[4]
    leaves = self_blocks.shape[3]
    leaf = self_blocks.shape[4]
    levels = factors.shape[2]
    rank = compress.shape[4]
    rows = 2 * cols
    row_count = lax.axis_size("px")
    col_count = lax.axis_size("py")
    row_bits = row_count.bit_length() - 1
    total = 2 * unknowns * row_count * col_count
    row_at = lax.axis_index("px")
    col_at = lax.axis_index("py")
    selfs = self_blocks.reshape(self_blocks.shape[2:])
    sides = side_blocks.reshape(side_blocks.shape[2:])
    squeeze = compress.reshape(compress.shape[2:])
    spread = expand.reshape(expand.shape[2:])
    sections = factors.reshape(factors.shape[2:])
    own_leaves = lax.dynamic_slice(edge_leaves, (row_at, col_at, 0, 0), (1, 1, 4, 2)).reshape(8)
    odd_row, odd_col = row_at % 2, col_at % 2
    order = jnp.stack([1 - odd_row, odd_row, 3 - odd_col, 2 + odd_col]).astype(jnp.int32)
    inner_row = (row_at > 0) & (row_at < row_count - 1)
    inner_col = (col_at > 0) & (col_at < col_count - 1)
    inner = jnp.stack([inner_row, inner_row, inner_col, inner_col]).astype(jnp.int32)
    ones = jnp.array([1, 0, 1, 0], jnp.int32)
    info = jnp.concatenate([own_leaves, order, jnp.maximum(inner, ones)])
    tall = v_block.reshape(cols, 2, leaves, leaf).transpose(0, 2, 1, 3).reshape(cols, -1, leaf)

    def partner(x, level):
        if level < row_bits:
            return lax.ppermute(x, "px", [(i, i ^ 1 << level) for i in range(row_count)])
        bit = level - row_bits
        return lax.ppermute(x, "py", [(i, i ^ 1 << bit) for i in range(col_count)])

    def beyond(x, axis, count):
        pairs = [(i, (i + 1) % count) for i in range(1, count, 2)]
        return lax.ppermute(x, axis, pairs + [(j, i) for i, j in pairs])

    small = ((rows, rank), BF16)
    double = ((2 * rows, rank), BF16)
    wide = ((rows, rank), F32)
    step_flops = 8 * cols * rank * rank
    patch_flops = 8 * cols * rank * unknowns
    leaf_flops = 8 * cols * leaf * unknowns

    half, sent = head(leaf, tall, squeeze)
    bounds = [0, 1, 3, levels]
    held = {}

    def weights(level):
        at = sum(level >= low for low in bounds[1:-1])
        if at not in held:
            limit = LATE if at == 2 else EARLY
            held[at] = load(sections, bounds[at], bounds[at + 1], limit, [sent])
        return held[at], level - bounds[at]

    got = {}
    for level in range(levels):
        arrived = partner(sent, level)
        after = []
        if level == 2:
            after = [weights(3)[0]]
        if level == 3:
            pieces = call(
                functools.partial(pick_kernel, leaf), [small] * 4, [info, half], 0, smem=1, after=[sent]
            )
            (near,) = call(
                functools.partial(leaves_kernel, leaf, False),
                [((rows, unknowns), F32)],
                [half, selfs],
                leaf_flops,
                after=[sent],
            )
            after = list(pieces) + [near]
        if level == 4:
            got["a"] = partner(pieces[0], 0)
        if level == row_bits:
            after = [got["a"]]
        if level == row_bits:
            got["c"] = arrived
            got["b"] = beyond(pieces[1], "px", row_count)
            got["d"] = beyond(pieces[3], "py", col_count)
        if level == levels - 1:
            (near,) = call(
                functools.partial(sides_kernel, leaf),
                [((rows, unknowns), F32)],
                [info, near, got["a"], got["b"], got["c"], got["d"], sides],
                4 * step_flops,
                smem=1,
                after=[sent],
            )
            after = [near, spread]
        f, at = weights(level)
        (own,) = call(
            functools.partial(own_kernel, at, False),
            [wide],
            [sent, f],
            step_flops,
            after=after,
        )
        if level < levels - 1:
            extra = [pieces[2]] if level == row_bits - 1 else []
            (sent,) = call(
                functools.partial(up_kernel, at),
                [double if extra else small],
                [own, arrived, f] + extra,
                step_flops,
            )
    y, yb, g, message = call(
        functools.partial(field_kernel, at),
        [((rows, unknowns), F32), ((rows, unknowns), BF16), small, small],
        [own, arrived, f, near, spread],
        2 * patch_flops,
    )
    terms = call(
        functools.partial(terms_kernel, leaf), [small] * 4, [info, yb, sides], 4 * step_flops, smem=1
    )
    (shaped,) = call(
        functools.partial(shape_kernel, leaf), [((cols, 2 * leaves, leaf), F32)], [y], 0
    )
    for level in range(levels - 1, -1, -1):
        arrived = partner(message, level)
        after = []
        if level == levels - 1:
            after = list(terms)
        if level == levels - 2:
            (z_near,) = call(
                functools.partial(leaves_kernel, leaf, True),
                [((rows, unknowns), F32)],
                [yb, selfs],
                leaf_flops,
                after=[message],
            )
            after = [z_near]
        if level == row_bits:
            got["c"] = arrived
        if level == 4:
            v_high, v_low, vv = call(
                functools.partial(basis_kernel, leaf),
                [((rows, unknowns), BF16), ((rows, unknowns), BF16), ((cols, cols), F32)],
                [tall],
                leaf_flops,
                after=[message],
            )
            after = [v_high, v_low, vv]
        if level == 3:
            got["d"] = beyond(terms[3], "py", col_count)
        if level == 2:
            after = [got["d"]]
            got["a"] = partner(terms[0], 0)
        if level == 1:
            after = [got["a"], squeeze]
            got["b"] = beyond(terms[1], "px", row_count)
        if level == 0:
            (z_near,) = call(
                functools.partial(gather_kernel, leaf),
                [((rows, unknowns), F32)],
                [info, z_near, got["a"], got["b"], got["c"], got["d"]],
                0,
                smem=1,
            )
            after = [z_near]
        f, at = weights(level)
        (own,) = call(
            functools.partial(own_kernel, at, True),
            [wide],
            [g, f],
            step_flops,
            after=after,
        )
        if level > 0:
            extra = [terms[2]] if level == row_bits + 1 else []
            f, at = weights(level - 1)
            g, message = call(
                functools.partial(down_kernel, at),
                [small, double if extra else small],
                [own, arrived, f] + extra,
                step_flops,
            )
    z_high, z_low, part = call(
        close_kernel,
        [((rows, unknowns), BF16), ((rows, unknowns), BF16), ((cols, 4 * cols), F32)],
        [z_near, own, arrived, squeeze, v_high, v_low, vv],
        patch_flops,
    )
    part = part.reshape(1, cols, 4 * cols)
    chips = row_count // 2
    (part,) = call(
        spread_kernel, [((chips, cols, 4 * cols), F32)], [part, partner(part, 0)], 0
    )
    groups = [[2 * i + core for i in range(chips)] for core in range(2)]
    part = lax.all_to_all(part, "px", 0, 0, axis_index_groups=groups, tiled=True)
    (part,) = call(spread_kernel, [((col_count, cols, 4 * cols), F32)], [part], 0)
    part = lax.all_to_all(part, "py", 0, 0, tiled=True)
    lines = 8
    (basis,) = call(
        functools.partial(finish_kernel, leaf, total),
        [((rows, 2 * leaves, leaf), F32)],
        [part, z_high, z_low, v_high, v_low],
        8 * rows * rows * unknowns,
        out_spec=pl.BlockSpec(memory_space=pl.ANY),
        scratch=[
            pltpu.VMEM((2 * leaves // lines, rows, lines, leaf), F32),
            pltpu.SemaphoreType.DMA((2 * leaves // lines,)),
        ],
    )

    def patch_form(a):
        count = a.shape[0]
        a = a.reshape(count, leaves, 2, leaf).transpose(0, 2, 1, 3)
        return a.reshape(count, 1, 1, 2, unknowns)

    return patch_form(shaped), patch_form(basis)


def solution(mesh):
    in_specs = (
        P(None, "px", "py", None, None),
        P(),
        P("px", "py", None, None, None, None),
        P("px", "py", None, None, None, None),
        P("px", "py", None, None, None),
        P("px", "py", None, None, None),
        P("px", "py", None, None, None, None, None),
    )
    out_specs = (P(None, "px", "py", None, None), P(None, "px", "py", None, None))
    return jax.shard_map(
        per_device, mesh=mesh, in_specs=in_specs, out_specs=out_specs, check_vma=False
    )
```

```python
import functools
import math

import jax
import jax.numpy as jnp
from jax import lax
from jax.experimental import pallas as pl
from jax.experimental.pallas import tpu as pltpu
from jax.sharding import PartitionSpec as P

F32 = jnp.float32
BF16 = jnp.bfloat16
NT = (((1,), (1,)), ((), ()))
VM = pl.BlockSpec(memory_space=pltpu.VMEM)
SM = pl.BlockSpec(memory_space=pltpu.SMEM)

HEAD, EARLY, LATE = 214, 200, 196


def call(kernel, outs, args, flops, smem=0, limit=24, after=(), out_spec=VM, scratch=()):
    size = sum(a.size * a.dtype.itemsize for a in args)
    args = list(args) + list(after)
    count, extra = len(args), len(after)

    def body(*refs):
        kernel(*refs[: count - extra], *refs[count:])

    return pl.pallas_call(
        body,
        out_shape=[jax.ShapeDtypeStruct(s, d) for s, d in outs],
        in_specs=[SM] * smem + [VM] * (count - smem),
        out_specs=[out_spec] * len(outs),
        scratch_shapes=list(scratch),
        cost_estimate=pl.CostEstimate(flops=flops, bytes_accessed=size, transcendentals=0),
        compiler_params=pltpu.CompilerParams(vmem_limit_bytes=limit * 2**20),
    )(*args)


def mul(x, gr, gi):
    h = x.shape[0] // 2
    re, im = x[:h], x[h:]
    first = jnp.dot(x, gr, preferred_element_type=F32)
    second = jnp.dot(jnp.concatenate([-im, re], 0), gi, preferred_element_type=F32)
    return first + second


def adj(x, gr, gi):
    h = x.shape[0] // 2
    re, im = x[:h], x[h:]
    first = lax.dot_general(x, gr, NT, preferred_element_type=F32)
    second = lax.dot_general(jnp.concatenate([im, -re], 0), gi, NT, preferred_element_type=F32)
    return first + second


def leaf_at(at, leaf):
    return pl.ds(pl.multiple_of(at * leaf, leaf), leaf)


def split(x):
    high = x.astype(BF16)
    return high, (x - high.astype(F32)).astype(BF16)


def piece(ref, info, side, leaf):
    return jnp.concatenate(
        [ref[:, leaf_at(info[2 * side + e], leaf)] for e in range(2)], 1
    )


def head_kernel(leaf, v_in, c_in, vb_ref, m_ref, v_ref, c_ref, v_sems, c_sems):
    cols, lines, _ = v_ref.shape
    count = v_sems.shape[0]
    step = lines // count
    width = step // 2 * leaf
    copies = []
    for at in range(count):
        some = slice(at * step, (at + 1) * step)
        cut = slice(at * width, (at + 1) * width)
        pair = [
            pltpu.make_async_copy(v_in.at[:, some], v_ref.at[:, some], v_sems.at[at]),
            pltpu.make_async_copy(c_in.at[:, cut], c_ref.at[:, cut], c_sems.at[at]),
        ]
        for copy in pair:
            copy.start()
        copies.append(pair)
    total = None
    for at in range(count):
        copies[at][0].wait()
        for row in range(at * step, (at + 1) * step):
            of, part = divmod(row, 2)
            vb_ref[part * cols : (part + 1) * cols, of * leaf : (of + 1) * leaf] = v_ref[
                :, row
            ].astype(BF16)
        copies[at][1].wait()
        cut = slice(at * width, (at + 1) * width)
        product = mul(vb_ref[:, cut], c_ref[0, cut], c_ref[1, cut])
        total = product if total is None else total + product
    m_ref[...] = total.astype(BF16)


def head(leaf, tall, squeeze):
    cols = tall.shape[0]
    unknowns, rank = squeeze.shape[1:]
    count = 4
    return pl.pallas_call(
        functools.partial(head_kernel, leaf),
        in_specs=[pl.BlockSpec(memory_space=pltpu.HBM)] * 2,
        out_specs=[VM] * 2,
        out_shape=[
            jax.ShapeDtypeStruct((2 * cols, unknowns), BF16),
            jax.ShapeDtypeStruct((2 * cols, rank), BF16),
        ],
        scratch_shapes=[
            pltpu.VMEM(tall.shape, F32),
            pltpu.VMEM(squeeze.shape, BF16),
            pltpu.SemaphoreType.DMA((count,)),
            pltpu.SemaphoreType.DMA((count,)),
        ],
        cost_estimate=pl.CostEstimate(
            flops=8 * cols * rank * unknowns,
            bytes_accessed=tall.size * 4 + squeeze.size * 2,
            transcendentals=0,
        ),
        compiler_params=pltpu.CompilerParams(vmem_limit_bytes=HEAD * 2**18),
    )(tall, squeeze)


def load_kernel(begin, f_in, *rest):
    o_ref, sem = rest[-2:]
    copy = pltpu.make_async_copy(f_in.at[begin : begin + o_ref.shape[0]], o_ref, sem)
    copy.start()
    copy.wait()


def load(sections, begin, end, limit, after=()):
    shape = (end - begin,) + sections.shape[1:]
    return pl.pallas_call(
        functools.partial(load_kernel, begin),
        in_specs=[pl.BlockSpec(memory_space=pltpu.HBM)] + [VM] * len(after),
        out_specs=VM,
        out_shape=jax.ShapeDtypeStruct(shape, BF16),
        scratch_shapes=[pltpu.SemaphoreType.DMA],
        cost_estimate=pl.CostEstimate(
            flops=0, bytes_accessed=2 * math.prod(shape), transcendentals=0
        ),
        compiler_params=pltpu.CompilerParams(vmem_limit_bytes=limit * 2**18),
    )(sections, *after)


def pick_kernel(leaf, info, vb_ref, *outs):
    for at, o_ref in enumerate(outs):
        o_ref[...] = piece(vb_ref, info, info[8 + at], leaf)


def basis_kernel(leaf, v_ref, high_ref, low_ref, p_ref):
    cols = v_ref.shape[0]
    for row in range(v_ref.shape[1]):
        of, part = divmod(row, 2)
        place = (slice(part * cols, (part + 1) * cols), slice(of * leaf, (of + 1) * leaf))
        high, low = split(v_ref[:, row])
        high_ref[place] = high
        low_ref[place] = low
    high = high_ref[...]
    cross = lax.dot_general(high, low_ref[...], NT, preferred_element_type=F32)
    s = lax.dot_general(high, high, NT, preferred_element_type=F32) + cross + cross.T
    p_ref[...] = packed(s, cols)


def packed(s, cols):
    below = lax.broadcasted_iota(jnp.int32, (cols, cols), 0) >= lax.broadcasted_iota(
        jnp.int32, (cols, cols), 1
    )
    re = s[:cols, :cols] + s[cols:, cols:]
    return jnp.where(below, re, s[cols:, :cols] - s[:cols, cols:])


def own_kernel(level, adjoint, s_ref, f_ref, o_ref):
    rows = o_ref.shape[0]
    product = adj if adjoint else mul
    o_ref[...] = product(s_ref[:rows], f_ref[level, 0, 0], f_ref[level, 0, 1])


def up_kernel(level, own_ref, r_ref, f_ref, *rest):
    rows = own_ref.shape[0]
    o_ref = rest[-1]
    state = own_ref[...] + mul(r_ref[:rows], f_ref[level, 1, 0], f_ref[level, 1, 1])
    o_ref[:rows] = state.astype(BF16)
    if len(rest) > 1:
        o_ref[rows:] = rest[0][...]


def leaves_kernel(leaf, adjoint, x_ref, b_ref, o_ref):
    product = adj if adjoint else mul
    for at in range(b_ref.shape[1]):
        cut = slice(at * leaf, (at + 1) * leaf)
        o_ref[:, cut] = product(x_ref[:, cut], b_ref[0, at], b_ref[1, at])


def sides_kernel(leaf, info, near_ref, ra_ref, rb_ref, rc_ref, rd_ref, b_ref, o_ref):
    rows = near_ref.shape[0]
    o_ref[...] = near_ref[...]
    for at, ref in enumerate((ra_ref, rb_ref, rc_ref, rd_ref)):
        side = info[8 + at]
        x = ref[ref.shape[0] - rows :]
        term = mul(x, b_ref[side, 0], b_ref[side, 1])

        @pl.when(info[12 + at] == 1)
        def _():
            for e in range(2):
                o_ref[:, leaf_at(info[2 * side + e], leaf)] += term[:, e * leaf : (e + 1) * leaf]


def field_kernel(
    level, own_ref, r_ref, f_ref, near_ref, e_ref, vv_ref, y_ref, yb_ref, g_ref, m_ref, sum_ref
):
    rows = own_ref.shape[0]
    state = own_ref[...] + mul(r_ref[:rows], f_ref[level, 1, 0], f_ref[level, 1, 1])
    y = near_ref[...] + mul(state.astype(BF16), e_ref[0], e_ref[1])
    y_ref[...] = y
    yb = y.astype(BF16)
    yb_ref[...] = yb
    g = adj(yb, e_ref[0], e_ref[1]).astype(BF16)
    g_ref[...] = g
    m_ref[:rows] = adj(g, f_ref[level, 1, 0], f_ref[level, 1, 1]).astype(BF16)
    yy = packed(lax.dot_general(yb, yb, NT, preferred_element_type=F32), rows // 2)
    total = jnp.concatenate([yy, vv_ref[...]], 1)
    sum_ref[...] = total
    share(total, m_ref, rows)


def share(total, m_ref, low):
    high = total.astype(BF16)
    middle, least = split(total - high.astype(F32))
    parts = [high, middle, least, jnp.zeros_like(high)]
    m_ref[low : low + total.shape[0]] = jnp.concatenate([p.astype(F32) for p in parts], 1).astype(BF16)


def shared(r_ref, low, total):
    width = total.shape[1]
    rows = r_ref[low : low + total.shape[0]].astype(F32)
    other = rows[:, :width] + rows[:, width : 2 * width] + rows[:, 2 * width : 3 * width]
    return total + other


def shape_kernel(leaf, y_ref, o_ref):
    cols = o_ref.shape[0]
    for row in range(o_ref.shape[1]):
        of, part = divmod(row, 2)
        o_ref[:, row] = y_ref[part * cols : (part + 1) * cols, of * leaf : (of + 1) * leaf]


def terms_kernel(leaf, info, yb_ref, b_ref, *outs):
    for at, o_ref in enumerate(outs):
        side = info[8 + at]
        x = piece(yb_ref, info, side, leaf)
        low = o_ref.shape[0] - x.shape[0]
        if low:
            o_ref[:low] = jnp.zeros((low, o_ref.shape[1]), BF16)
        o_ref[low:] = adj(x, b_ref[side, 0], b_ref[side, 1]).astype(BF16)


def down_kernel(level, own_ref, r_ref, sum_ref, f_ref, *rest):
    rows = own_ref.shape[0]
    g_ref, m_ref, total_ref = rest[-3:]
    g = (own_ref[...] + r_ref[:rows].astype(F32)).astype(BF16)
    g_ref[...] = g
    m_ref[:rows] = adj(g, f_ref[level, 1, 0], f_ref[level, 1, 1]).astype(BF16)
    total = shared(r_ref, rows, sum_ref[...])
    total_ref[...] = total
    share(total, m_ref, rows)
    if len(rest) > 3:
        m_ref[rows + rows // 2 :] = rest[0][...]


def gather_kernel(leaf, info, near_ref, ra_ref, rb_ref, rc_ref, rd_ref, o_ref):
    rows = near_ref.shape[0]
    o_ref[...] = near_ref[...]
    for at, ref in enumerate((ra_ref, rb_ref, rc_ref, rd_ref)):
        side = info[8 + at]
        low = ref.shape[0] - rows

        @pl.when(info[12 + at] == 1)
        def _():
            for e in range(2):
                o_ref[:, leaf_at(info[2 * side + e], leaf)] += ref[
                    low:, e * leaf : (e + 1) * leaf
                ].astype(F32)


def close_kernel(near_ref, own_ref, r_ref, sum_ref, c_ref, zh_ref, zl_ref, p_ref, total_ref):
    rows = own_ref.shape[0]
    cols = rows // 2
    g = (own_ref[...] + r_ref[:rows].astype(F32)).astype(BF16)
    high, low = split(near_ref[...] + adj(g, c_ref[0], c_ref[1]))
    zh_ref[...] = high
    zl_ref[...] = low
    s = lax.dot_general(high, jnp.concatenate([high, low], 0), NT, preferred_element_type=F32)
    cross = s[:, rows:]
    zz = packed(s[:, :rows] + cross + cross.T, cols)
    lines = p_ref.shape[1]
    part = jnp.concatenate([zz[at : at + lines] for at in range(0, cols, lines)], 1)
    for at in range(p_ref.shape[0]):
        p_ref[at] = part
    total_ref[...] = shared(r_ref, rows, sum_ref[...])


def spread_kernel(*refs):
    o_ref = refs[-1]
    total = sum(parts_of(refs[:-1]))
    for at in range(o_ref.shape[0]):
        o_ref[at] = total


def parts_of(refs):
    return [ref[at] for ref in refs for at in range(ref.shape[0])]


def exact_dot(a, b, dims=(((1,), (0,)), ((), ()))):
    return lax.dot_general(a, b, dims, preferred_element_type=F32, precision=lax.Precision.HIGHEST)


def real_form(re, im):
    return jnp.concatenate(
        [jnp.concatenate([re, im], 1), jnp.concatenate([-im, re], 1)], 0
    )


def inverse_factor(gram):
    size, step = gram.shape[0], 8
    eye = (
        lax.broadcasted_iota(jnp.int32, (size, size), 0)
        == lax.broadcasted_iota(jnp.int32, (size, size), 1)
    ).astype(F32)
    wide = jnp.concatenate([gram, eye], 1)
    width = wide.shape[1]
    blocks = [wide[step * j : step * (j + 1)] for j in range(size // step)]
    sub = lax.broadcasted_iota(jnp.int32, (step, width), 0)
    done = []
    for at in range(size // step):
        left = [
            [jnp.broadcast_to(b[:, at * step + p : at * step + p + 1], (step, width)) for b in blocks[at:]]
            for p in range(step)
        ]
        pivot = [
            [jnp.broadcast_to(left[q][0][p : p + 1], (step, width)) for q in range(p + 1)]
            for p in range(step)
        ]
        lines = [jnp.broadcast_to(blocks[at][p : p + 1], (step, width)) for p in range(step)]
        result = jnp.zeros((step, width), F32)
        updates = [None] * len(left[0])
        for p in range(step):
            inverse = 1.0 / pivot[p][p]
            result = jnp.where(sub == p, lines[p] * lax.rsqrt(pivot[p][p]), result)
            scaled = lines[p] * inverse
            for q in range(p + 1, step):
                ratio = pivot[q][p] * inverse
                lines[q] = lines[q] - ratio * lines[p]
                for r in range(p + 1, q + 1):
                    pivot[q][r] = pivot[q][r] - ratio * pivot[r][p]
                for i in range(1, len(left[q])):
                    left[q][i] = left[q][i] - ratio * left[p][i]
            for i in range(1, len(updates)):
                term = left[p][i] * scaled
                updates[i] = term if p == 0 else updates[i] + term
        done.append(result)
        for i in range(1, len(updates)):
            blocks[at + i] = blocks[at + i] - updates[i]
    return jnp.concatenate(done, 0)[:, size:]


def finish_kernel(leaf, total, p_ref, sum_ref, zh_ref, zl_ref, vh_ref, vl_ref, o_ref, buffer, sems):
    p = sum(parts_of([p_ref])) * (1.0 / total)
    known = sum_ref[...] * (1.0 / total)
    cols = known.shape[0]
    lower = lax.broadcasted_iota(jnp.int32, (cols, cols), 0)
    upper = lax.broadcasted_iota(jnp.int32, (cols, cols), 1)

    def hermitian(t):
        turned = t.T
        re = jnp.where(lower >= upper, t, turned)
        im = jnp.where(lower < upper, t, jnp.where(lower > upper, -turned, 0.0))
        return real_form(re, im)

    zz = hermitian(jnp.concatenate([p[:, at : at + cols] for at in range(0, p.shape[1], cols)], 0))
    h = hermitian(known[:, :cols])
    vv = hermitian(known[:, cols:])
    nt = (((1,), (1,)), ((), ()))
    middle = exact_dot(h, vv) - 2.0 * h
    gram = zz + exact_dot(middle, h, nt)
    inverse = inverse_factor(gram)
    w = exact_dot(inverse, h)
    l1, l2 = inverse[:, :cols], inverse[:, cols:]
    w1, w2 = w[:, :cols], w[:, cols:]
    mix = jnp.concatenate(
        [
            jnp.concatenate([l1, -l2, -w1, w2], 1),
            jnp.concatenate([l2, l1, -w2, -w1], 1),
        ],
        0,
    )
    mix_high, mix_low = split(mix)
    mix = jnp.concatenate([mix_high, mix_high, mix_low], 1)
    rows = 2 * cols
    count, _, lines, _ = buffer.shape
    width = lines // 2 * leaf
    copies = []
    for at in range(count):
        cut = slice(at * width, (at + 1) * width)
        high = [zh_ref[:, cut], vh_ref[:, cut]]
        x = jnp.concatenate(high + [zl_ref[:, cut], vl_ref[:, cut]] + high, 0)
        out = jnp.dot(mix, x, preferred_element_type=F32)
        for line in range(lines):
            of, part = divmod(line, 2)
            buffer[at, :, line] = out[part * rows : (part + 1) * rows, of * leaf : (of + 1) * leaf]
        copy = pltpu.make_async_copy(
            buffer.at[at], o_ref.at[:, at * lines : (at + 1) * lines], sems.at[at]
        )
        copy.start()
        copies.append(copy)
    for copy in copies:
        copy.wait()


def per_device(v_block, edge_leaves, self_blocks, side_blocks, compress, expand, factors):
    cols = v_block.shape[0]
    unknowns = v_block.shape[4]
    leaves = self_blocks.shape[3]
    leaf = self_blocks.shape[4]
    levels = factors.shape[2]
    rank = compress.shape[4]
    rows = 2 * cols
    row_count = lax.axis_size("px")
    col_count = lax.axis_size("py")
    row_bits = row_count.bit_length() - 1
    total = 2 * unknowns * row_count * col_count
    row_at = lax.axis_index("px")
    col_at = lax.axis_index("py")
    selfs = self_blocks.reshape(self_blocks.shape[2:])
    sides = side_blocks.reshape(side_blocks.shape[2:])
    squeeze = compress.reshape(compress.shape[2:])
    spread = expand.reshape(expand.shape[2:])
    sections = factors.reshape(factors.shape[2:])
    own_leaves = lax.dynamic_slice(edge_leaves, (row_at, col_at, 0, 0), (1, 1, 4, 2)).reshape(8)
    odd_row, odd_col = row_at % 2, col_at % 2
    order = jnp.stack([1 - odd_row, odd_row, 3 - odd_col, 2 + odd_col]).astype(jnp.int32)
    inner_row = (row_at > 0) & (row_at < row_count - 1)
    inner_col = (col_at > 0) & (col_at < col_count - 1)
    inner = jnp.stack([inner_row, inner_row, inner_col, inner_col]).astype(jnp.int32)
    ones = jnp.array([1, 0, 1, 0], jnp.int32)
    info = jnp.concatenate([own_leaves, order, jnp.maximum(inner, ones)])
    tall = v_block.reshape(cols, 2, leaves, leaf).transpose(0, 2, 1, 3).reshape(cols, -1, leaf)

    def partner(x, level):
        if level < row_bits:
            return lax.ppermute(x, "px", [(i, i ^ 1 << level) for i in range(row_count)])
        bit = level - row_bits
        return lax.ppermute(x, "py", [(i, i ^ 1 << bit) for i in range(col_count)])

    def beyond(x, axis, count):
        pairs = [(i, (i + 1) % count) for i in range(1, count, 2)]
        return lax.ppermute(x, axis, pairs + [(j, i) for i, j in pairs])

    small = ((rows, rank), BF16)
    double = ((2 * rows, rank), BF16)
    wide = ((rows, rank), F32)
    step_flops = 8 * cols * rank * rank
    patch_flops = 8 * cols * rank * unknowns
    leaf_flops = 8 * cols * leaf * unknowns

    half, sent = head(leaf, tall, squeeze)
    bounds = [0, 1, 3, levels]
    held = {}

    def weights(level):
        at = sum(level >= low for low in bounds[1:-1])
        if at not in held:
            limit = LATE if at == 2 else EARLY
            held[at] = load(sections, bounds[at], bounds[at + 1], limit, [sent])
        return held[at], level - bounds[at]

    got = {}
    for level in range(levels):
        arrived = partner(sent, level)
        after = []
        if level == 2:
            after = [weights(3)[0]]
        if level == 3:
            pieces = call(
                functools.partial(pick_kernel, leaf), [small] * 4, [info, half], 0, smem=1, after=[sent]
            )
            (near,) = call(
                functools.partial(leaves_kernel, leaf, False),
                [((rows, unknowns), F32)],
                [half, selfs],
                leaf_flops,
                after=[sent],
            )
            after = list(pieces) + [near]
        if level == 4:
            v_high, v_low, vv = call(
                functools.partial(basis_kernel, leaf),
                [((rows, unknowns), BF16), ((rows, unknowns), BF16), ((cols, cols), F32)],
                [tall],
                leaf_flops,
                after=[sent],
            )
            after = [v_high, v_low, vv]
            got["a"] = partner(pieces[0], 0)
        if level == row_bits:
            after = [got["a"]]
        if level == row_bits:
            got["c"] = arrived
            got["b"] = beyond(pieces[1], "px", row_count)
            got["d"] = beyond(pieces[3], "py", col_count)
        if level == levels - 1:
            (near,) = call(
                functools.partial(sides_kernel, leaf),
                [((rows, unknowns), F32)],
                [info, near, got["a"], got["b"], got["c"], got["d"], sides],
                4 * step_flops,
                smem=1,
                after=[sent],
            )
            after = [near, spread]
        f, at = weights(level)
        (own,) = call(
            functools.partial(own_kernel, at, False),
            [wide],
            [sent, f],
            step_flops,
            after=after,
        )
        if level < levels - 1:
            extra = [pieces[2]] if level == row_bits - 1 else []
            (sent,) = call(
                functools.partial(up_kernel, at),
                [double if extra else small],
                [own, arrived, f] + extra,
                step_flops,
            )
    longer = ((rows + cols, rank), BF16)
    longest = ((2 * rows + cols, rank), BF16)
    sums = ((cols, 2 * cols), F32)
    y, yb, g, message, running = call(
        functools.partial(field_kernel, at),
        [((rows, unknowns), F32), ((rows, unknowns), BF16), small, longer, sums],
        [own, arrived, f, near, spread, vv],
        2 * patch_flops,
    )
    terms = call(
        functools.partial(terms_kernel, leaf),
        [longer, longer, small, longer],
        [info, yb, sides],
        4 * step_flops,
        smem=1,
    )
    (shaped,) = call(
        functools.partial(shape_kernel, leaf), [((cols, 2 * leaves, leaf), F32)], [y], 0
    )
    for level in range(levels - 1, -1, -1):
        arrived = partner(message, level)
        after = []
        if level == levels - 1:
            after = list(terms)
        if level == levels - 2:
            (z_near,) = call(
                functools.partial(leaves_kernel, leaf, True),
                [((rows, unknowns), F32)],
                [yb, selfs],
                leaf_flops,
                after=[message],
            )
            after = [z_near]
        if level == row_bits:
            got["c"] = arrived
        if level == 3:
            got["d"] = beyond(terms[3], "py", col_count)
        if level == 2:
            after = [got["d"]]
            got["a"] = partner(terms[0], 0)
        if level == 1:
            after = [got["a"], squeeze]
            got["b"] = beyond(terms[1], "px", row_count)
        if level == 0:
            (z_near,) = call(
                functools.partial(gather_kernel, leaf),
                [((rows, unknowns), F32)],
                [info, z_near, got["a"], got["b"], got["c"], got["d"]],
                0,
                smem=1,
            )
            after = [z_near]
        f, at = weights(level)
        (own,) = call(
            functools.partial(own_kernel, at, True),
            [wide],
            [g, f],
            step_flops,
            after=after,
        )
        if level > 0:
            extra = [terms[2]] if level == row_bits + 1 else []
            f, at = weights(level - 1)
            g, message, running = call(
                functools.partial(down_kernel, at),
                [small, longest if extra else longer, sums],
                [own, arrived, running, f] + extra,
                step_flops,
            )
    payload = (8, cols * cols // 8)
    z_high, z_low, part, running = call(
        close_kernel,
        [
            ((rows, unknowns), BF16),
            ((rows, unknowns), BF16),
            ((row_count,) + payload, F32),
            sums,
        ],
        [z_near, own, arrived, running, squeeze],
        patch_flops,
    )
    part = lax.all_to_all(part, "px", 0, 0, tiled=True)
    (part,) = call(spread_kernel, [((col_count,) + payload, F32)], [part], 0)
    part = lax.all_to_all(part, "py", 0, 0, tiled=True)
    lines = 8
    (basis,) = call(
        functools.partial(finish_kernel, leaf, total),
        [((rows, 2 * leaves, leaf), F32)],
        [part, running, z_high, z_low, v_high, v_low],
        8 * rows * rows * unknowns,
        out_spec=pl.BlockSpec(memory_space=pl.ANY),
        scratch=[
            pltpu.VMEM((2 * leaves // lines, rows, lines, leaf), F32),
            pltpu.SemaphoreType.DMA((2 * leaves // lines,)),
        ],
    )

    def patch_form(a):
        count = a.shape[0]
        a = a.reshape(count, leaves, 2, leaf).transpose(0, 2, 1, 3)
        return a.reshape(count, 1, 1, 2, unknowns)

    return patch_form(shaped), patch_form(basis)


def solution(mesh):
    in_specs = (
        P(None, "px", "py", None, None),
        P(),
        P("px", "py", None, None, None, None),
        P("px", "py", None, None, None, None),
        P("px", "py", None, None, None),
        P("px", "py", None, None, None),
        P("px", "py", None, None, None, None, None),
    )
    out_specs = (P(None, "px", "py", None, None), P(None, "px", "py", None, None))
    return jax.shard_map(
        per_device, mesh=mesh, in_specs=in_specs, out_specs=out_specs, check_vma=False
    )
```
